32 devices in a mesh: fsdp: 4 (over z), ctx: 2 (over x), tp: 4 (over y, core).
Axes of the slice: x: 2, y: 2, z: 4, core: 2. Of those that a mesh axis runs over, the one named last changes fastest.
Arguments:
- layer_input: float32 [12288, 1536], P(('fsdp', 'ctx')), may hold values from -6 to 6
- doc_lengths: int32 [4, 3], P('fsdp'), may hold values from 1 to 2048, 3072 in all within a row
- attention_gain: bfloat16 [1536], P('fsdp'), may hold values from 0.5 to 1.5
- query_weight: bfloat16 [1536, 1536], P('fsdp', 'tp'), may hold values from -0.15625 to 0.15625
- key_matrix: bfloat16 [1536, 768], P('fsdp', 'tp'), may hold values from -0.15625 to 0.15625
- value_matrix: bfloat16 [1536, 768], P('fsdp', 'tp'), may hold values from -0.15625 to 0.15625
- output_weight: bfloat16 [1536, 1536], P('tp', 'fsdp'), may hold values from -0.875 to 0.875
- feedforward_gain: bfloat16 [1536], P('fsdp'), may hold values from 0.5 to 1.5
- gate_weight: bfloat16 [1536, 4096], P('fsdp', 'tp'), may hold values from -0.15625 to 0.15625
- up_weight: bfloat16 [1536, 4096], P('fsdp', 'tp'), may hold values from -0.15625 to 0.15625
- down_weight: bfloat16 [4096, 1536], P('tp', 'fsdp'), may hold values from -0.09375 to 0.09375
- output_cotangent: float32 [12288, 1536], P(('fsdp', 'ctx')), may hold values from -6 to 6
Outputs:
- layer_output: float32 [12288, 1536], P(('fsdp', 'ctx'))
- input_gradient: float32 [12288, 1536], P(('fsdp', 'ctx'))
- attention_gain_gradient: float32 [1536], P('fsdp')
- query_gradient: float32 [1536, 1536], P('fsdp', 'tp')
- key_gradient: float32 [1536, 768], P('fsdp', 'tp')
- value_gradient: float32 [1536, 768], P('fsdp', 'tp')
- output_gradient: float32 [1536, 1536], P('tp', 'fsdp')
- feedforward_gain_gradient: float32 [1536], P('fsdp')
- gate_gradient: float32 [1536, 4096], P('fsdp', 'tp')
- up_gradient: float32 [1536, 4096], P('fsdp', 'tp')
- down_gradient: float32 [4096, 1536], P('tp', 'fsdp')
The draws below stay inside these ranges and needn't reach their ends.
Inputs may be any that keep to these rules, and one draw needn't show every extreme that they name: `doc_lengths`: each row holds the lengths of the 3 documents packed in order into the 3072 tokens of one group; a row sums to 3072 and its longest document has exactly 2048 tokens.
All inputs are finite; a program needn't handle non-finite values.
Results may differ from the reference program's by a relative error of at most 0.014.
Values may be sent and summed in bfloat16 or wider, within the bound.
A program may use at most 256 MiB of HBM per device.

```python
import math
import jax
import jax.numpy as jnp
import numpy as np
from jax import lax

MODEL_WIDTH = 1536
QUERY_HEAD_COUNT = 16
KEY_VALUE_HEADS = 8
HEAD_SIZE = 96
FF = 4096
DOCS = 3
GROUP_TOKENS = 3072
MAXLEN = 2048
TOKEN_GROUPS = 4
TOKEN_TOTAL = 12288


def shard_levels(key, extent, cuts, low, largest):
    def one(position, blocks):
        steps = jax.random.uniform(jax.random.fold_in(jax.random.fold_in(key, 6), position), (blocks,), jnp.float32, low / len(cuts), largest / len(cuts))
        return jnp.repeat(jnp.exp(steps), extent[position] // blocks).reshape((-1,) + (1,) * (len(extent) - position - 1))

    factor_of = one(*cuts[0])
    for cut in cuts[1:]:
        factor_of = factor_of * one(*cut)
    return factor_of


def split_up(number_of, total, limit, slope):
    loads = [(1 << 20) // math.isqrt(grade ** slope) + 1 for grade in range(2, number_of + 1)]
    rest, holding = total - limit - (number_of - 1), [1] * (number_of - 1)
    while rest > 0:
        free = [i for i in range(number_of - 1) if holding[i] < limit]
        whole, budget = sum([loads[i] for i in free]), rest
        for i in free:
            addition = min(limit - holding[i], max(1, budget * loads[i] // whole), rest)
            holding[i] = holding[i] + addition
            rest = rest - addition
    return np.array([limit] + holding)


def ragged_sizes(stream_key, count, total, limit, lean):
    if count == 2:
        one = jax.random.randint(stream_key, (), max(1, total - limit), min(limit, total - 1) + 1)
        return jnp.stack([one, total - one])
    sizes = jnp.asarray(split_up(count, total, limit, lean), jnp.int32)
    pairs = (count - 1) // 2
    donor, sink = sizes[1:1 + 2 * pairs:2], sizes[2:2 + 2 * pairs:2]
    margin = jnp.minimum(donor - 1, limit - sink)
    shifted = jax.random.randint(jax.random.fold_in(stream_key, 1), (pairs,), 0, 1 << 20) % (margin + 1)
    sizes = sizes.at[1:1 + 2 * pairs:2].set(donor - shifted).at[2:2 + 2 * pairs:2].set(sink + shifted)
    return sizes[jax.random.permutation(jax.random.fold_in(stream_key, 2), count)]


def noise(own_key, extent, spread, reach, shards=(), kind=jnp.bfloat16):
    drawn = jax.random.normal(own_key, extent, jnp.float32) * spread
    if len(shards) > 0:
        drawn = shard_levels(own_key, extent, shards, -0.22, 0.18) * drawn
    return jnp.clip(drawn, min=-reach, max=reach).astype(kind)


def setup_inputs(seed: int = 0) -> dict:
    key_list = jax.random.split(jax.random.key(seed), 13)
    return {
        "layer_input": noise(key_list[0], (TOKEN_TOTAL, MODEL_WIDTH), 1.0, 6.0, ((0, 8),), jnp.float32),
        "doc_lengths": jax.vmap(lambda own: ragged_sizes(own, DOCS, GROUP_TOKENS, MAXLEN, 2))(jax.random.split(key_list[1], TOKEN_GROUPS)).reshape((TOKEN_GROUPS, DOCS)).astype(jnp.int32),
        "attention_gain": jnp.clip(1.0 + 0.1 * jax.random.normal(key_list[2], (MODEL_WIDTH,), jnp.float32), 0.5, 1.5).astype(jnp.bfloat16),
        "query_weight": noise(key_list[3], (MODEL_WIDTH, QUERY_HEAD_COUNT * HEAD_SIZE), MODEL_WIDTH ** -0.5, 0.15625, ((0, 4), (1, 4))),
        "key_matrix": noise(key_list[4], (MODEL_WIDTH, KEY_VALUE_HEADS * HEAD_SIZE), MODEL_WIDTH ** -0.5, 0.15625, ((0, 4), (1, 4))),
        "value_matrix": noise(key_list[5], (MODEL_WIDTH, KEY_VALUE_HEADS * HEAD_SIZE), MODEL_WIDTH ** -0.5, 0.15625, ((0, 4), (1, 4))),
        "output_weight": noise(key_list[6], (QUERY_HEAD_COUNT * HEAD_SIZE, MODEL_WIDTH), (QUERY_HEAD_COUNT * HEAD_SIZE // 32) ** -0.5, 0.875, ((0, 4), (1, 4))),
        "feedforward_gain": jnp.clip(1.0 + 0.1 * jax.random.normal(key_list[7], (MODEL_WIDTH,), jnp.float32), 0.5, 1.5).astype(jnp.bfloat16),
        "gate_weight": noise(key_list[8], (MODEL_WIDTH, FF), MODEL_WIDTH ** -0.5, 0.15625, ((0, 4), (1, 4))),
        "up_weight": noise(key_list[9], (MODEL_WIDTH, FF), MODEL_WIDTH ** -0.5, 0.15625, ((0, 4), (1, 4))),
        "down_weight": noise(key_list[10], (FF, MODEL_WIDTH), FF ** -0.5, 0.09375, ((0, 4), (1, 4))),
        "output_cotangent": noise(key_list[11], (TOKEN_TOTAL, MODEL_WIDTH), 1.0, 6.0, ((0, 8),), jnp.float32),
    }


EPSILON = 1e-05
THETA = 100000.0
NEGATIVE = -1e+30

@jax.custom_vjp
def lowered_rows(v):
    return lax.optimization_barrier(v.astype(jnp.bfloat16)).astype(jnp.float32)

@jax.custom_vjp
def low_back(v):
    return v

def low_keep(v):
    return (lowered_rows(v), None)

def low_pass(kept, grad):
    return (grad,)

def back_keep(v):
    return (v, None)

def back_low(kept, grad):
    return (lowered_rows(grad),)
lowered_rows.defvjp(low_keep, low_pass)
low_back.defvjp(back_keep, back_low)

def hdot(left, right):
    return jnp.dot(left, right, precision=lax.Precision.HIGHEST, preferred_element_type=jnp.float32)

def rms(value_rows):
    return value_rows * lax.rsqrt(lax.optimization_barrier(jnp.mean(value_rows * value_rows, axis=-1, keepdims=True)) + EPSILON)

def doc_positions(lengths, first, count):
    ends = jnp.cumsum(lengths).astype(jnp.int32)
    starts = (ends - lengths).astype(jnp.int32)
    index = (first + jnp.arange(count, dtype=jnp.int32)).astype(jnp.int32)
    document_list = lax.optimization_barrier(jnp.sum((index[None, :] >= ends[:, None]).astype(jnp.int32), axis=0)).astype(jnp.int32)
    chosen = document_list[None, :] == jnp.arange(lengths.shape[0], dtype=jnp.int32)[:, None]
    start_of = lax.optimization_barrier(jnp.sum(jnp.where(chosen, starts[:, None], 0), axis=0)).astype(jnp.int32)
    return (document_list, (index - start_of).astype(jnp.int32))

def rotary_tables(positions, head_dim):
    half = head_dim // 2
    freqs = THETA ** (-(jnp.arange(half, dtype=jnp.float32) * 2.0 / head_dim))
    angles = positions.astype(jnp.float32)[:, None] * freqs[None, :]
    return (jnp.cos(angles), jnp.sin(angles))

def apply_rotary(value_rows, cosine_table, sine_table):
    half = value_rows.shape[-1] // 2
    first, second = (value_rows[..., :half], value_rows[..., half:])
    cosine_table, sine_table = (cosine_table[:, None, :], sine_table[:, None, :])
    return jnp.concatenate([first * cosine_table - second * sine_table, second * cosine_table + first * sine_table], axis=-1)

def grouped_attention_fn(inputs):
    rotated_queries, rotated_keys, lowered_values, document_list = inputs
    block = math.gcd(GROUP_TOKENS, 512)
    grouped_rows = rotated_queries.reshape(GROUP_TOKENS, KEY_VALUE_HEADS, QUERY_HEAD_COUNT // KEY_VALUE_HEADS, HEAD_SIZE)
    key_index = jnp.arange(GROUP_TOKENS, dtype=jnp.int32)
    scale = 1.0 / math.sqrt(HEAD_SIZE)

    @jax.checkpoint
    def block_attention(start):
        query_block = lax.dynamic_slice_in_dim(grouped_rows, start, block, 0)
        raw = jnp.einsum('qhgd,khd->hgqk', query_block, rotated_keys, precision=lax.Precision.HIGHEST) * scale
        scores = low_back(raw)
        query_index = start + jnp.arange(block, dtype=jnp.int32)
        doc_block = lax.dynamic_slice_in_dim(document_list, start, block, 0)
        allowed = (key_index[None, :] <= query_index[:, None]) & (document_list[None, :] == doc_block[:, None])
        scores = jnp.where(allowed[None, None], scores, NEGATIVE)
        probs = jax.nn.softmax(scores, axis=-1)
        result = jnp.einsum('hgqk,khd->qhgd', lowered_rows(probs), lowered_values, precision=lax.Precision.HIGHEST)
        return result.reshape(block, QUERY_HEAD_COUNT * HEAD_SIZE)
    starts = (jnp.arange(GROUP_TOKENS // block, dtype=jnp.int32) * block).astype(jnp.int32)
    return lax.map(block_attention, starts).reshape(GROUP_TOKENS, QUERY_HEAD_COUNT * HEAD_SIZE)

def forward(layer_input, positions, document_list, gain_one, query_w, key_w, value_w, output_w, gain_two, gate_w, up_w, down_w):
    normed_one = lowered_rows(rms(layer_input) * gain_one)
    queries = low_back(hdot(normed_one, query_w))
    key_rows = low_back(hdot(normed_one, key_w))
    value_rows = lowered_rows(low_back(hdot(normed_one, value_w)))
    cosine_table, sine_table = rotary_tables(positions, HEAD_SIZE)
    rotated_queries = lowered_rows(apply_rotary(queries.reshape(TOKEN_TOTAL, QUERY_HEAD_COUNT, HEAD_SIZE), cosine_table, sine_table))
    rotated_keys = lowered_rows(apply_rotary(key_rows.reshape(TOKEN_TOTAL, KEY_VALUE_HEADS, HEAD_SIZE), cosine_table, sine_table))
    lowered_values = value_rows.reshape(TOKEN_TOTAL, KEY_VALUE_HEADS, HEAD_SIZE)
    attended_rows = lax.map(grouped_attention_fn, (rotated_queries.reshape(TOKEN_GROUPS, GROUP_TOKENS, QUERY_HEAD_COUNT, HEAD_SIZE), rotated_keys.reshape(TOKEN_GROUPS, GROUP_TOKENS, KEY_VALUE_HEADS, HEAD_SIZE), lowered_values.reshape(TOKEN_GROUPS, GROUP_TOKENS, KEY_VALUE_HEADS, HEAD_SIZE), document_list.reshape(TOKEN_GROUPS, GROUP_TOKENS)))
    attended_rows = lowered_rows(low_back(attended_rows.reshape(TOKEN_TOTAL, QUERY_HEAD_COUNT * HEAD_SIZE)))
    middle = layer_input + low_back(hdot(attended_rows, output_w))
    normed_two = lowered_rows(rms(middle) * gain_two)
    gate = low_back(hdot(normed_two, gate_w))
    up = low_back(hdot(normed_two, up_w))
    hidden = lowered_rows(jax.nn.silu(gate) * up)
    return middle + low_back(hdot(hidden, down_w))

def reference(layer_input, doc_lengths, attention_gain, query_weight, key_matrix, value_matrix, output_weight, feedforward_gain, gate_weight, up_weight, down_weight, output_cotangent):
    document_list, positions = jax.vmap(lambda row: doc_positions(row, 0, GROUP_TOKENS))(doc_lengths)
    document_list = document_list.reshape(TOKEN_TOTAL)
    positions = positions.reshape(TOKEN_TOTAL)
    params = (attention_gain.astype(jnp.float32), query_weight.astype(jnp.float32), key_matrix.astype(jnp.float32), value_matrix.astype(jnp.float32), output_weight.astype(jnp.float32), feedforward_gain.astype(jnp.float32), gate_weight.astype(jnp.float32), up_weight.astype(jnp.float32), down_weight.astype(jnp.float32))

    def apply(value_rows, gain_one, query_w, key_w, value_w, output_w, gain_two, gate_w, up_w, down_w):
        return forward(value_rows, positions, document_list, gain_one, query_w, key_w, value_w, output_w, gain_two, gate_w, up_w, down_w)
    result, pullback = jax.vjp(apply, layer_input, *params)
    grads = pullback(output_cotangent)
    return (result, grads[0], grads[1], grads[2], grads[3], grads[4], grads[5], grads[6], grads[7], grads[8], grads[9])
```

```python
import functools
import math

import jax
import jax.numpy as jnp
from jax import lax
from jax.experimental import pallas as pl
from jax.experimental.pallas import tpu as pltpu
from jax.sharding import PartitionSpec as P

HEAD_SIZE = 96
EPSILON = 1e-05
THETA = 100000.0
NEGATIVE = -1e30
LOG2E = 1.4426950408889634
LANES = 128
F32 = jnp.float32
BF16 = jnp.bfloat16
NN = (((1,), (0,)), ((), ()))
NT = (((1,), (1,)), ((), ()))
TN = (((0,), (0,)), ((), ()))


def dot(left, right, dims=NN):
    return lax.dot_general(left, right, dims, preferred_element_type=F32)


def select_rotary(heads, head_dim):
    shape = (heads * LANES, heads * head_dim)
    row = lax.broadcasted_iota(jnp.int32, shape, 0)
    col = lax.broadcasted_iota(jnp.int32, shape, 1)
    half = head_dim // 2
    within = col % head_dim
    want = (col // head_dim) * LANES + jnp.where(within < half, within, within - half + LANES // 2)
    return (row == want).astype(BF16)


def select_value(heads, head_dim):
    shape = (heads * LANES, heads * head_dim)
    row = lax.broadcasted_iota(jnp.int32, shape, 0)
    col = lax.broadcasted_iota(jnp.int32, shape, 1)
    return (row == (col // head_dim) * LANES + col % head_dim).astype(BF16)


def rotary_lanes(positions, head_dim):
    half = head_dim // 2
    freqs = THETA ** (-(jnp.arange(half, dtype=F32) * 2.0 / head_dim))
    angles = positions.astype(F32)[:, None] * freqs[None, :]
    cos, sin = jnp.cos(angles), jnp.sin(angles)
    pad = jnp.zeros((positions.shape[0], LANES // 2 - half), F32)
    return (
        jnp.concatenate([cos, pad, cos, pad], axis=1),
        jnp.concatenate([-sin, pad, sin, pad], axis=1),
    )


def doc_positions(lengths, first, count):
    ends = jnp.cumsum(lengths)
    starts = ends - lengths
    index = first + jnp.arange(count, dtype=jnp.int32)
    document = jnp.sum((index[None, :] >= ends[:, None]).astype(jnp.int32), axis=0)
    chosen = document[None, :] == jnp.arange(lengths.shape[0], dtype=jnp.int32)[:, None]
    start_of = jnp.sum(jnp.where(chosen, starts[:, None], 0), axis=0)
    return index - start_of


def doc_start(ends_ref, base, rows):
    start = base if jnp.ndim(rows) == 0 else jnp.zeros_like(rows) + base
    for j in range(ends_ref.shape[0]):
        end = ends_ref[j]
        start = jnp.where(rows >= end, jnp.maximum(start, end), start)
    return start


def put_lanes(rows, column, lane):
    at = lax.broadcasted_iota(jnp.int32, rows.shape, 1)
    high = column.astype(BF16).astype(F32)
    rest = column - high
    mid = rest.astype(BF16).astype(F32)
    low = rest - mid
    wide = rows.astype(F32)
    wide = jnp.where(at == lane, high, wide)
    wide = jnp.where(at == lane + 1, mid, wide)
    return jnp.where(at == lane + 2, low, wide).astype(BF16)


def block_ranges(first_row, rows, block, low, last_low, key_base, key_count):
    begin = (jnp.maximum(low, key_base) - key_base) // block
    stop = jnp.minimum((first_row + rows - key_base + block - 1) // block, key_count // block)
    inner = jnp.minimum(jnp.maximum((last_low - key_base + block - 1) // block, begin), stop)
    diagonal = jnp.minimum(jnp.maximum((first_row - key_base) // block, inner), stop)
    return begin, inner, diagonal, stop


def stack_heads(ref, kv, group):
    parts = [ref[:, (kv * group + g) * LANES : (kv * group + g + 1) * LANES] for g in range(group)]
    return jnp.concatenate(parts, axis=0)


def row_marks(ends_ref, base, first_row, bq, group):
    rows = lax.broadcasted_iota(jnp.int32, (1, bq), 1) + first_row
    starts = doc_start(ends_ref, base, rows)
    return jnp.concatenate([rows] * group, axis=1), jnp.concatenate([starts] * group, axis=1)


def attention_forward_kernel(
    first, key_base, tokens, bq, bk, head_dim, group, ends_ref, base_ref, q_ref, kv_ref, *rest
):
    if first:
        max_ref, acc_ref = rest
    else:
        sel_ref, max_in, acc_in, o_ref, qa_ref, max_ref, acc_ref = rest
    first_row = tokens + pl.program_id(0) * bq
    base = base_ref[0]
    low = doc_start(ends_ref, base, first_row)
    last_low = doc_start(ends_ref, base, first_row + bq - 1)
    rows, starts = row_marks(ends_ref, base, first_row, bq, group)
    kv_heads = kv_ref.shape[1] // LANES // 2
    unit = LOG2E / math.sqrt(head_dim)
    queries = [stack_heads(q_ref, h, group) for h in range(kv_heads)]
    if first:
        max_ref[...] = jnp.full(max_ref.shape, NEGATIVE, F32)
        acc_ref[...] = jnp.zeros(acc_ref.shape, F32)
    else:
        max_ref[...] = max_in[...]
        acc_ref[...] = acc_in[...]

    def body(masked, index, carry):
        at = pl.multiple_of(index * bk, bk)
        if masked:
            keys = lax.broadcasted_iota(jnp.int32, (bk, group * bq), 0) + (at + key_base)
            keep = (keys <= rows) & (keys >= starts)
        for h in range(kv_heads):
            key = kv_ref[pl.ds(at, bk), h * LANES : (h + 1) * LANES]
            value = kv_ref[pl.ds(at, bk), (kv_heads + h) * LANES : (kv_heads + h + 1) * LANES]
            scores = dot(key, queries[h], NT)
            if masked:
                scores = jnp.where(keep, scores, NEGATIVE)
            old = max_ref[0, h]
            new = jnp.maximum(old, jnp.max(scores, axis=0, keepdims=True))
            probs = jnp.exp2((scores - new) * unit)
            if masked:
                probs = jnp.where(keep, probs, 0.0)
            acc_ref[0, h] = acc_ref[0, h] * jnp.exp2((old - new) * unit) + dot(
                value, probs.astype(BF16), TN
            )
            max_ref[0, h] = new
        return carry

    begin, inner, diagonal, stop = block_ranges(
        first_row, bq, bk, low, last_low, key_base, kv_ref.shape[0]
    )
    lax.fori_loop(begin, inner, functools.partial(body, True), 0)
    lax.fori_loop(inner, diagonal, functools.partial(body, False), 0)
    lax.fori_loop(diagonal, stop, functools.partial(body, True), 0)
    if first:
        return
    outs = []
    for h in range(kv_heads):
        acc = acc_ref[0, h]
        total = acc[head_dim : head_dim + 1, :]
        out = jnp.transpose(acc * (1.0 / total)).astype(BF16)
        logsum = jnp.broadcast_to(max_ref[0, h] + jnp.log2(total) * (1.0 / unit), (8, group * bq))
        marked = put_lanes(queries[h], jnp.transpose(logsum)[:, :1], head_dim // 2)
        for g in range(group):
            head = h * group + g
            qa_ref[:, head * LANES : (head + 1) * LANES] = marked[g * bq : (g + 1) * bq]
            outs.append(out[g * bq : (g + 1) * bq])
    o_ref[...] = dot(jnp.concatenate(outs, axis=1), sel_ref[...]).astype(BF16)


def attention_forward(ends, base, q, kv, head_dim, key_base, state=None, select=None):
    tokens, width = q.shape
    kv_heads = kv.shape[1] // LANES // 2
    group = width // LANES // kv_heads
    bq = bk = math.gcd(tokens, 512)
    steps = tokens // bq
    whole = lambda a: pl.BlockSpec(a.shape, lambda i, *_: (0, 0))
    row = lambda w: pl.BlockSpec((bq, w), lambda i, *_: (i, 0))
    shapes = [(steps, kv_heads, 1, group * bq), (steps, kv_heads, LANES, group * bq)]
    kept = [pl.BlockSpec((1,) + a[1:], lambda i, *_: (i, 0, 0, 0)) for a in shapes]
    pairs = tokens * tokens * group * kv_heads // 2
    if state is None:
        in_specs, operands = [row(width), whole(kv)], (q, kv)
        out_specs, out_shape = kept, [jax.ShapeDtypeStruct(a, F32) for a in shapes]
        scratch = []
    else:
        in_specs, operands = [row(width), whole(kv), whole(select)] + kept, (q, kv, select) + tuple(state)
        out_specs = [row(select.shape[1]), row(width)]
        out_shape = [
            jax.ShapeDtypeStruct((tokens, select.shape[1]), BF16),
            jax.ShapeDtypeStruct(q.shape, BF16),
        ]
        scratch = [pltpu.VMEM((1,) + a[1:], F32) for a in shapes]
    return pl.pallas_call(
        functools.partial(
            attention_forward_kernel, state is None, key_base, tokens, bq, bk, head_dim, group
        ),
        grid_spec=pltpu.PrefetchScalarGridSpec(
            num_scalar_prefetch=2, grid=(steps,), in_specs=in_specs, out_specs=out_specs,
            scratch_shapes=scratch,
        ),
        out_shape=out_shape,
        compiler_params=pltpu.CompilerParams(vmem_limit_bytes=40 << 20),
        cost_estimate=pl.CostEstimate(
            flops=pairs * 1024, bytes_accessed=8 << 20, transcendentals=pairs
        ),
        name="attention_forward",
    )(ends, base, *operands)


def attention_backward_kernel(
    first, key_base, tokens, bq, bk, head_dim, group,
    ends_ref, base_ref, qa_ref, do_ref, o_ref, kv_ref, spread_ref, *rest
):
    if first:
        dq_ref, dkv_ref, dk_acc, dv_acc, dq_acc = rest
    else:
        part_ref, cos_ref, sin_ref, sel_ref, dq_ref, dkv_ref, dk_acc, dv_acc, dq_acc = rest
    step = pl.program_id(0)
    first_row = tokens + step * bq
    base = base_ref[0]
    low = doc_start(ends_ref, base, first_row)
    last_low = doc_start(ends_ref, base, first_row + bq - 1)
    kv_heads = kv_ref.shape[1] // LANES // 2
    scale = 1.0 / math.sqrt(head_dim)
    unit = LOG2E * scale
    begin, inner, diagonal, stop = block_ranges(
        first_row, bq, bk, low, last_low, key_base, kv_ref.shape[0]
    )

    @pl.when(step == 0)
    def _():
        dk_acc[...] = jnp.zeros(dk_acc.shape, F32)
        dv_acc[...] = jnp.zeros(dv_acc.shape, F32)

    if first:
        dq_acc[...] = jnp.zeros(dq_acc.shape, F32)
    else:
        for h in range(kv_heads):
            dq_acc[h] = stack_heads(part_ref, h, group)

    @pl.when(begin < stop)
    def _():
        rows, starts = row_marks(ends_ref, base, first_row, bq, group)
        grads_wide = dot(do_ref[...], spread_ref[...])
        outs_wide = dot(o_ref[...], spread_ref[...])
        queries, grads = [], []
        for h in range(kv_heads):
            queries.append(stack_heads(qa_ref, h, group))
            grad = stack_heads(grads_wide, h, group)
            inner_sum = jnp.sum(grad * stack_heads(outs_wide, h, group), axis=1, keepdims=True)
            grads.append(put_lanes(grad, -inner_sum, head_dim))

        def body(masked, index, carry):
            at = pl.multiple_of(index * bk, bk)
            if masked:
                keys = lax.broadcasted_iota(jnp.int32, (bk, group * bq), 0) + (at + key_base)
                keep = (keys <= rows) & (keys >= starts)
            for h in range(kv_heads):
                key = kv_ref[pl.ds(at, bk), h * LANES : (h + 1) * LANES]
                value = kv_ref[pl.ds(at, bk), (kv_heads + h) * LANES : (kv_heads + h + 1) * LANES]
                probs = jnp.exp2(dot(key, queries[h], NT) * unit)
                if masked:
                    probs = jnp.where(keep, probs, 0.0)
                slope = (probs * dot(value, grads[h], NT)).astype(BF16)
                dv_acc[h, pl.ds(at, bk), :] += dot(probs.astype(BF16), grads[h])
                dk_acc[h, pl.ds(at, bk), :] += dot(slope, queries[h])
                dq_acc[h] += dot(slope, key, TN)
            return carry

        lax.fori_loop(begin, inner, functools.partial(body, True), 0)
        lax.fori_loop(inner, diagonal, functools.partial(body, False), 0)
        lax.fori_loop(diagonal, stop, functools.partial(body, True), 0)

    outs = []
    for h in range(kv_heads):
        for g in range(group):
            grad = dq_acc[h, g * bq : (g + 1) * bq, :]
            if first:
                dq_ref[:, (h * group + g) * LANES : (h * group + g + 1) * LANES] = grad
            else:
                grad = grad * scale
                outs.append(
                    (grad * cos_ref[...] - pltpu.roll(grad, LANES // 2, 1) * sin_ref[...]).astype(BF16)
                )
    if not first:
        dq_ref[...] = dot(jnp.concatenate(outs, axis=1), sel_ref[...]).astype(BF16)

    @pl.when(step == pl.num_programs(0) - 1)
    def _():
        for h in range(kv_heads):
            dkv_ref[:, h * LANES : (h + 1) * LANES] = (dk_acc[h] * scale).astype(dkv_ref.dtype)
            dkv_ref[:, (kv_heads + h) * LANES : (kv_heads + h + 1) * LANES] = dv_acc[h].astype(dkv_ref.dtype)


def attention_backward(ends, base, qa, grad, out, kv, spread, head_dim, key_base, rest=None):
    tokens, width = qa.shape
    keys = kv.shape[0]
    kv_heads = kv.shape[1] // LANES // 2
    group = width // LANES // kv_heads
    bq = bk = math.gcd(tokens, 512)
    whole = lambda a: pl.BlockSpec(a.shape, lambda i, *_: (0, 0))
    row = lambda w: pl.BlockSpec((bq, w), lambda i, *_: (i, 0))
    pairs = tokens * tokens * group * kv_heads // 2
    in_specs = [row(width), row(grad.shape[1]), row(out.shape[1]), whole(kv), whole(spread)]
    operands = (qa, grad, out, kv, spread)
    if rest is None:
        dq_width, dq_type, dkv_type = width, F32, BF16
    else:
        part, cos, sin, select = rest
        in_specs += [row(width), row(LANES), row(LANES), whole(select)]
        operands += (part, cos, sin, select)
        dq_width, dq_type, dkv_type = select.shape[1], BF16, F32
    return pl.pallas_call(
        functools.partial(
            attention_backward_kernel, rest is None, key_base, tokens, bq, bk, head_dim, group
        ),
        grid_spec=pltpu.PrefetchScalarGridSpec(
            num_scalar_prefetch=2,
            grid=(tokens // bq,),
            in_specs=in_specs,
            out_specs=[row(dq_width), whole(kv)],
            scratch_shapes=[
                pltpu.VMEM((kv_heads, keys, LANES), F32),
                pltpu.VMEM((kv_heads, keys, LANES), F32),
                pltpu.VMEM((kv_heads, group * bq, LANES), F32),
            ],
        ),
        out_shape=[
            jax.ShapeDtypeStruct((tokens, dq_width), dq_type),
            jax.ShapeDtypeStruct(kv.shape, dkv_type),
        ],
        compiler_params=pltpu.CompilerParams(vmem_limit_bytes=48 << 20),
        cost_estimate=pl.CostEstimate(
            flops=pairs * 2560, bytes_accessed=12 << 20, transcendentals=pairs
        ),
        name="attention_backward",
    )(ends, base, qa, grad, out, kv, spread, *operands[5:])


MESH = pl.DeviceIdType.MESH


class Ranks:
    def __init__(self, count):
        self.count, self.chips = count, count // 2
        self.me = lax.axis_index("tp")
        self.chip, self.core = self.me // 2, self.me % 2

    def peer(self, k, j):
        return lax.rem(self.chip + k + self.chips, self.chips) * 2 + lax.rem(self.core + j, 2)

    def others(self):
        return [(k, j) for k in range(self.chips) for j in range(2) if k or j]

    def barrier(self):
        sem = pltpu.get_barrier_semaphore()
        for k, j in self.others():
            pl.semaphore_signal(sem, inc=1, device_id={"tp": self.peer(k, j)}, device_id_type=MESH)
        pl.semaphore_wait(sem, self.count - 1)


def remote(src, dst, send, recv, rank):
    return pltpu.make_async_remote_copy(
        src_ref=src, dst_ref=dst, send_sem=send, recv_sem=recv, device_id={"tp": rank},
        device_id_type=MESH,
    )


def row_mean(x):
    return jnp.sum(x, axis=-1, keepdims=True) * (1.0 / x.shape[-1])


class GatherRows:
    def __init__(self, ranks, rows_ref, out_ref, send, recv, local):
        own = rows_ref.shape[0]
        self.ranks, self.send, self.recv = ranks, send, recv
        self.at = lambda rank: out_ref.at[pl.ds(pl.multiple_of(rank * own, own), own)]
        self.keep = pltpu.make_async_copy(rows_ref, self.at(ranks.me), local)
        self.copies = []
        for k in list(range(1, ranks.chips)) + [0]:
            peer = ranks.peer(k, 0) if k else ranks.peer(0, 1)
            self.copies.append(remote(rows_ref, self.at(ranks.me), send.at[0, k], recv.at[0, k], peer))

    def start(self):
        for copy in self.copies:
            copy.start()
        self.keep.start()

    def finish(self):
        ranks, passed = self.ranks, []
        for k, copy in zip(range(1, ranks.chips), self.copies):
            copy.wait_recv()
            held = self.at(ranks.peer(-k, 0))
            passed.append(
                remote(held, held, self.send.at[1, k], self.recv.at[1, k], ranks.peer(0, 1))
            )
            passed[-1].start()
        self.copies[-1].wait_recv()
        for copy in self.copies:
            copy.wait_send()
        for copy in passed:
            copy.wait()
        self.keep.wait()


def both_cores(ranks, blocks, out_ref, send, recv, local):
    own = blocks[0].shape[0]
    copies = []
    for k, block in enumerate(blocks):
        there = out_ref.at[pl.ds(pl.multiple_of(ranks.peer(-k, 0) * own, own), own)]
        copies.append(remote(block, there, send.at[k], recv.at[k], ranks.peer(0, 1)))
        copies.append(pltpu.make_async_copy(block, there, local.at[k]))
    return copies


def mix_kernel(count, att_ref, x_ref, gain_ref, *rest):
    chips = count // 2
    blocks, rest = rest[:chips], rest[chips:]
    (
        n2_ref, mid_ref, other_ref, heads, rows_in, rows_out, others, a_send, a_recv, b_send, b_recv,
        g_send, g_recv, local,
    ) = rest
    ranks = Ranks(count)
    own = rows_in.shape[0]
    mine_at = pl.ds(pl.multiple_of(ranks.me * own, own), own)
    fetch = pltpu.make_async_copy(x_ref.at[mine_at], rows_in, local.at[0])
    fetch.start()
    mine = pltpu.make_async_copy(att_ref.at[mine_at], heads.at[0], local.at[1])
    mine.start()
    ranks.barrier()
    copies = {}
    for k, j in ranks.others()[::-1]:
        peer, slot = ranks.peer(k, j), 2 * k + j
        copies[slot] = remote(
            att_ref.at[pl.ds(pl.multiple_of(peer * own, own), own)], heads.at[slot],
            a_send.at[slot], a_recv.at[slot], peer,
        )
        copies[slot].start()
    swaps = [
        remote(blocks[k], others.at[k], b_send.at[k], b_recv.at[k], ranks.peer(0, 1))
        for k in range(chips)
    ]
    for copy in swaps:
        copy.start()
    fetch.wait()
    mine.wait()
    mid_ref[...] = rows_in[...] + dot(heads[0], blocks[0][...], NT)
    keeps = []
    for slot in range(1, count):
        k = slot // 2
        if slot % 2:
            swaps[k].wait_recv()
            keeps.append(pltpu.make_async_copy(others.at[k], other_ref.at[k], local.at[2 + k]))
            keeps[-1].start()
        copies[slot].wait_recv()
        mid_ref[...] += dot(heads[slot], others[k] if slot % 2 else blocks[k][...], NT)
    mid = mid_ref[...]
    factor = lax.rsqrt(row_mean(mid * mid) + EPSILON)
    rows_out[...] = (mid * factor * gain_ref[...]).astype(BF16)
    gather = GatherRows(ranks, rows_out, n2_ref, g_send, g_recv, local.at[0])
    gather.start()
    for slot in range(1, count):
        copies[slot].wait_send()
    for copy in swaps:
        copy.wait_send()
    for copy in keeps:
        copy.wait()
    gather.finish()


def mix(count, attended, layer_input, gain, blocks):
    tokens, model = layer_input.shape
    own = tokens // count
    chips = count // 2
    width = attended.shape[1]
    vmem, hbm = pl.BlockSpec(memory_space=pltpu.VMEM), pl.BlockSpec(memory_space=pl.ANY)
    sem = pltpu.SemaphoreType.DMA
    return pl.pallas_call(
        functools.partial(mix_kernel, count),
        in_specs=[hbm, hbm, vmem] + [vmem] * chips,
        out_specs=[hbm, vmem, hbm],
        out_shape=[
            jax.ShapeDtypeStruct((tokens, model), BF16),
            jax.ShapeDtypeStruct((own, model), F32),
            jax.ShapeDtypeStruct((chips, model, width), BF16),
        ],
        scratch_shapes=[
            pltpu.VMEM((count, own, width), BF16),
            pltpu.VMEM((own, model), F32),
            pltpu.VMEM((own, model), BF16),
            pltpu.VMEM((chips, model, width), BF16),
            sem((count,)), sem((count,)), sem((chips,)), sem((chips,)), sem((2, chips)),
            sem((2, chips)), sem((2 + chips,)),
        ],
        compiler_params=pltpu.CompilerParams(
            vmem_limit_bytes=40 << 20, collective_id=1, has_side_effects=True
        ),
        cost_estimate=pl.CostEstimate(
            flops=2 * tokens * model * model, bytes_accessed=150 << 20, transcendentals=0
        ),
        name="mix_heads",
    )(attended, layer_input, gain, *blocks)


def scatter_order(ranks, halves, own, i):
    k = lax.rem(i // halves + 1, ranks.chips)
    half = lax.rem(i, halves)
    rows = own // halves
    at = lambda j: pl.multiple_of(ranks.peer(k, j) * own + half * rows, rows)
    return k, half, at(0), at(1)


def half_rows(shard, which, half):
    return pl.ds(pl.multiple_of((shard * 2 + which) * half, half), half)


def swap_halves(src, dst, send, recv, shards):
    piece = lax.axis_index("ctx")
    half = src.shape[0] // (2 * shards)
    return [
        pltpu.make_async_remote_copy(
            src_ref=src.at[half_rows(s, 1 - piece, half)], dst_ref=dst.at[pl.ds(s * half, half)],
            send_sem=send.at[s], recv_sem=recv.at[s], device_id={"ctx": 1 - piece},
            device_id_type=MESH,
        )
        for s in range(shards)
    ]


def signal_piece(count):
    ranks = Ranks(count)
    sem = pltpu.get_barrier_semaphore()
    for k, j in ranks.others():
        pl.semaphore_signal(sem, inc=1, device_id={"tp": ranks.peer(k, j)}, device_id_type=MESH)
    pl.semaphore_signal(sem, inc=1, device_id={"ctx": 1 - lax.axis_index("ctx")}, device_id_type=MESH)
    pl.semaphore_wait(sem, count)


def feedforward_kernel(count, n2_ref, cot_ref, mid_ref, gain_ref, other_ref, weight_ref, *rest):
    blocks, rest = rest[: count // 2], rest[count // 2 :]
    (
        ffb_ref, mg_ref, bg_ref, gain_grad_ref, da_ref, grad_ref, grads_ref,
        gate_w, up_w, down_w, n2, fg, hid, gu, rows_in, ffb_out,
        c_send, c_recv, y_send, y_recv, f_send, f_recv, heads,
        w_sem, in_sem, out_sem, cs, cr, ys, yr, fs, fr, hs, hr, local,
    ) = rest
    ranks = Ranks(count)
    own = mg_ref.shape[0]
    halves = 2
    rows = own // halves
    steps = ranks.chips * halves
    width = gate_w.shape[1]
    model = n2.shape[1]
    loads = [pltpu.make_async_copy(n2_ref, n2, w_sem.at[3])] + [
        pltpu.make_async_copy(weight_ref.at[:, pl.ds(w * width, width)], full, w_sem.at[w])
        for w, full in enumerate((gate_w, up_w, down_w))
    ]
    for load in loads:
        load.start()

    def read(at, slot):
        return pltpu.make_async_copy(cot_ref.at[pl.ds(at, rows)], rows_in.at[slot], in_sem.at[slot])

    def tile(at, slot, begin):
        here = pl.ds(at, rows)

        def ready(n):
            if begin is not None:
                @pl.when(begin)
                def _():
                    loads[n].wait()

        ready(0)
        ready(1)
        n = n2[here, :]
        grad = rows_in[slot].astype(BF16)
        fg[here, :] = grad
        gate = dot(n, gate_w[...])
        ready(2)
        up = dot(n, up_w[...])
        ready(3)
        back = dot(grad, down_w[...])
        sig = 1.0 / (1.0 + jnp.exp(-gate))
        act = gate * sig
        hidden = (act * up).astype(BF16)
        hid[here, :] = hidden
        gg = (back * up * (sig * (1.0 + gate * (1.0 - sig)))).astype(BF16)
        gu[here, :width] = gg
        ug = (back * act).astype(BF16)
        gu[here, width:] = ug
        return dot(gg, gate_w[...], NT) + dot(ug, up_w[...], NT), dot(hidden, down_w[...], NT)

    read(scatter_order(ranks, halves, own, 0)[3], 0).start()
    ranks.barrier()
    neighbour = ranks.peer(0, 1)

    def to_core(i):
        slot = lax.rem(i, 2)
        return [
            remote(c_send.at[slot], c_recv.at[slot], cs.at[slot], cr.at[slot], neighbour),
            remote(f_send.at[slot], f_recv.at[slot], fs.at[slot], fr.at[slot], neighbour),
        ]

    def to_chip(i, k):
        return remote(y_send.at[i], y_recv.at[i], ys.at[i], yr.at[i], ranks.peer(k, 0))

    def ffb_write(i):
        return pltpu.make_async_copy(ffb_out, ffb_ref.at[i], out_sem.at[0])

    def step(i, carry):
        k, u, at_mine, at_other = scatter_order(ranks, halves, own, i)
        slot = lax.rem(i, 2)
        read(at_mine, 1).start()
        read(at_other, 0).wait()
        grad, forward = tile(at_other, 0, i == 0)

        @pl.when(i + 1 < steps)
        def _():
            read(scatter_order(ranks, halves, own, i + 1)[3], 0).start()

        @pl.when(i > 1)
        def _():
            for copy in to_core(i):
                copy.wait_send()

        c_send[slot] = grad.astype(BF16)
        f_send[slot] = forward.astype(BF16)
        for copy in to_core(i):
            copy.start()
        read(at_mine, 1).wait()
        grad, forward = tile(at_mine, 1, None)

        @pl.when(i > 0)
        def _():
            ffb_write(i).wait()

        for copy in to_core(i):
            copy.wait_recv()
        grad = grad + c_recv[slot].astype(F32)
        ffb_out[...] = (forward + f_recv[slot].astype(F32)).astype(BF16)
        ffb_write(i).start()

        @pl.when(k != 0)
        def _():
            y_send[i] = grad.astype(BF16)
            to_chip(i, k).start()

        @pl.when(k == 0)
        def _():
            mg_ref[pl.ds(pl.multiple_of(u * rows, rows), rows), :] = grad

        return carry

    lax.fori_loop(0, steps, step, 0)
    mine_at = pl.multiple_of(ranks.me * own, own)
    fetch = lambda u: [
        pltpu.make_async_copy(mid_ref.at[pl.ds(u * rows, rows)], rows_in.at[0], in_sem.at[0]),
        read(mine_at + u * rows, 1),
    ]
    for copy in fetch(0):
        copy.start()
    cols = math.gcd(model, 384)
    writes = []

    def product(left, right, full, dst, n):
        for d in range(model // cols):
            full[d * cols : (d + 1) * cols, :] = dot(
                left[:, d * cols : (d + 1) * cols], right, TN
            ).astype(BF16)
        writes.append(pltpu.make_async_copy(full, dst, out_sem.at[1 + n]))
        writes[-1].start()

    product(n2, gu[:, :width], gate_w, grad_ref, 0)
    gain = gain_ref[...]
    gain_total = None
    for u in range(halves):
        here = slice(u * rows, (u + 1) * rows)
        total = mg_ref[here, :]
        for k in range(1, ranks.chips):
            i = (k - 1) * halves + u
            to_chip(i, k).wait_recv()
            total = total + y_recv[i].astype(F32)
        for copy in fetch(u):
            copy.wait()
        mid = rows_in[0]
        factor = lax.rsqrt(row_mean(mid * mid) + EPSILON)
        hat = mid * factor
        term = jnp.sum(total * hat, axis=0, keepdims=True)
        gain_total = term if gain_total is None else gain_total + term
        inner = total * gain
        grad = rows_in[1] + factor * (inner - hat * row_mean(inner * hat))
        mg_ref[here, :] = grad
        bg_ref[here, :] = grad.astype(BF16)
        if u + 1 < halves:
            for copy in fetch(u + 1):
                copy.start()
    gain_grad_ref[...] = gain_total
    back = []
    for k, j in ranks.others()[::-1]:
        slot, peer = 2 * k + j, ranks.peer(-k, j)
        heads[slot] = dot(bg_ref[...], other_ref[k] if j else blocks[k][...]).astype(BF16)
        back.append(
            remote(heads.at[slot], da_ref.at[pl.ds(mine_at, own)], hs.at[slot], hr.at[slot], peer)
        )
        back[-1].start()
    heads[0] = dot(bg_ref[...], blocks[0][...]).astype(BF16)
    keep = pltpu.make_async_copy(heads.at[0], da_ref.at[pl.ds(mine_at, own)], local.at[0])
    keep.start()
    product(n2, gu[:, width:], up_w, grads_ref.at[:, pl.ds(0, width)], 1)
    product(fg, hid[...], down_w, grads_ref.at[:, pl.ds(width, width)], 2)
    for i in (steps - 2, steps - 1):
        for copy in to_core(i):
            copy.wait_send()
    for i in range(steps - halves):
        to_chip(i, i // halves + 1).wait_send()
    ffb_write(steps - 1).wait()
    for copy in back:
        copy.wait()
    keep.wait()
    for copy in writes:
        copy.wait()


def feedforward(count, n2, cotangent, middle, gain, weights, blocks, others):
    tokens, model = n2.shape
    own = tokens // count
    hidden = weights.shape[1] // 3
    width = blocks[0].shape[1]
    rows, steps = own // 2, count
    vmem, hbm = pl.BlockSpec(memory_space=pltpu.VMEM), pl.BlockSpec(memory_space=pl.ANY)
    sem = pltpu.SemaphoreType.DMA
    return pl.pallas_call(
        functools.partial(feedforward_kernel, count),
        in_specs=[hbm, hbm, hbm, vmem, vmem, hbm] + [vmem] * (count // 2),
        out_specs=[hbm, vmem, vmem, vmem, hbm, hbm, hbm],
        out_shape=[
            jax.ShapeDtypeStruct((steps, rows, model), BF16),
            jax.ShapeDtypeStruct((own, model), F32),
            jax.ShapeDtypeStruct((own, model), BF16),
            jax.ShapeDtypeStruct((1, model), F32),
            jax.ShapeDtypeStruct((tokens, width), BF16),
            jax.ShapeDtypeStruct((model, hidden), BF16),
            jax.ShapeDtypeStruct((model, 2 * hidden), BF16),
        ],
        scratch_shapes=[pltpu.VMEM((model, hidden), BF16)] * 3
        + [
            pltpu.VMEM((tokens, model), BF16),
            pltpu.VMEM((tokens, model), BF16),
            pltpu.VMEM((tokens, hidden), BF16),
            pltpu.VMEM((tokens, 2 * hidden), BF16),
            pltpu.VMEM((2, rows, model), F32),
            pltpu.VMEM((rows, model), BF16),
        ]
        + [pltpu.VMEM((2, rows, model), BF16)] * 2
        + [pltpu.VMEM((steps - 2, rows, model), BF16)] * 2
        + [pltpu.VMEM((2, rows, model), BF16)] * 2
        + [
            pltpu.VMEM((count, own, width), BF16),
            sem((4,)), sem((2,)), sem((4,)),
            sem((2,)), sem((2,)), sem((steps - 2,)), sem((steps - 2,)),
            sem((2,)), sem((2,)), sem((count,)), sem((count,)), sem((1,)),
        ],
        compiler_params=pltpu.CompilerParams(
            vmem_limit_bytes=63 << 20, collective_id=2, has_side_effects=True
        ),
        cost_estimate=pl.CostEstimate(
            flops=2 * tokens * model * hidden * 9, bytes_accessed=280 << 20,
            transcendentals=tokens * hidden,
        ),
        name="feed_forward",
    )(n2, cotangent, middle, gain, others, weights, *blocks)


def shard_copy(src, dst, send, recv, axis, index):
    return pltpu.make_async_remote_copy(
        src_ref=src, dst_ref=dst, send_sem=send, recv_sem=recv, device_id={axis: index},
        device_id_type=MESH,
    )


def begin_kernel(
    shards, x_ref, qkv_ref, wo_ref, gains_ref, n_ref, qkv_full_ref, wo_full_ref, gain_out_ref,
    qkv_full, wo_full, normed, rows_in, gain_buf, zs, zr, xs, xr, gs, gr, own_sem, in_sem, out_sem,
):
    me, piece = lax.axis_index("fsdp"), lax.axis_index("ctx")
    fulls, sources = (qkv_full, wo_full), (qkv_ref, wo_ref)
    shard = qkv_ref.shape[0]
    half = shard // 2
    tokens = normed.shape[0]
    rows = rows_in.shape[1]
    steps = tokens // rows

    def read(i):
        return pltpu.make_async_copy(
            x_ref.at[pl.ds(i * rows, rows)], rows_in.at[i % 2], in_sem.at[i % 2]
        )

    read(0).start()
    keeps = [
        pltpu.make_async_copy(src, full.at[pl.ds(pl.multiple_of(me * shard, shard), shard)], own_sem.at[a])
        for a, (src, full) in enumerate(zip(sources, fulls))
    ]
    for copy in keeps:
        copy.start()
    keep_gain = pltpu.make_async_copy(gains_ref, gain_buf.at[me], own_sem.at[2])
    keep_gain.start()
    barrier = pltpu.get_barrier_semaphore()
    for k in range(1, shards):
        pl.semaphore_signal(
            barrier, inc=1, device_id={"fsdp": lax.rem(me + k, shards)}, device_id_type=MESH
        )
    pl.semaphore_signal(barrier, inc=1, device_id={"ctx": 1 - piece}, device_id_type=MESH)
    pl.semaphore_wait(barrier, shards)

    def place(a, s, which):
        return fulls[a].at[half_rows(s, which, half)]

    def own_half(a):
        return sources[a].at[pl.ds(pl.multiple_of(piece * half, half), half)]

    def along(a, s, step, mine):
        way = 0 if step > 0 else 1
        src = own_half(a) if mine else place(a, s, piece)
        return shard_copy(
            src, place(a, s, piece), zs.at[a, way, s], zr.at[a, s], "fsdp",
            lax.rem(me + step + shards, shards),
        )

    def across(a, s):
        return shard_copy(
            place(a, s, piece), place(a, s, piece), xs.at[a, s], xr.at[a, s], "ctx", 1 - piece
        )

    gain_copies = [
        shard_copy(
            gains_ref, gain_buf.at[me], gs.at[k], gr.at[k], "fsdp", lax.rem(me + k, shards)
        )
        for k in range(1, shards)
    ]
    for copy in gain_copies:
        copy.start()
    for a in range(2):
        for step, there in ((1, me < shards - 1), (-1, me > 0)):
            @pl.when(there)
            def _():
                along(a, me, step, True).start()

    for copy in gain_copies:
        copy.wait()
    keep_gain.wait()
    gain_out_ref[...] = jnp.concatenate([gain_buf[s] for s in range(shards)], axis=1)
    for i in range(steps):
        if i + 1 < steps:
            read(i + 1).start()
        read(i).wait()
        x = rows_in[i % 2]
        factor = lax.rsqrt(row_mean(x * x) + EPSILON)
        normed[i * rows : (i + 1) * rows, :] = (x * factor * gain_out_ref[0:1, :]).astype(BF16)
    write_normed = pltpu.make_async_copy(normed, n_ref, out_sem.at[0])
    write_normed.start()

    def arrival(d, step):
        s = me - step * d
        there = (s >= 0) & (s <= shards - 1)
        s = jnp.minimum(jnp.maximum(s, 0), shards - 1)
        onward = (me < shards - 1) if step > 0 else (me > 0)

        @pl.when(there)
        def _():
            for a in range(2):
                along(a, s, step, False).wait_recv()
                across(a, s).start()

        @pl.when(there & onward)
        def _():
            for a in range(2):
                along(a, s, step, False).start()

    for d in range(1, shards):
        arrival(d, 1)
        arrival(d, -1)
    for copy in keeps:
        copy.wait()
    for k in range(1, shards):
        s = lax.rem(me + k, shards)
        for a in range(2):
            across(a, s).wait_recv()
    writes = [
        pltpu.make_async_copy(qkv_full, qkv_full_ref, out_sem.at[1]),
        pltpu.make_async_copy(wo_full, wo_full_ref, out_sem.at[2]),
    ]
    for copy in writes:
        copy.start()
    for a in range(2):
        for s in range(shards):
            @pl.when((me >= s) & (me < shards - 1))
            def _():
                along(a, s, 1, False).wait_send()

            @pl.when((me <= s) & (me > 0))
            def _():
                along(a, s, -1, False).wait_send()

        for k in range(1, shards):
            across(a, lax.rem(me + k, shards)).wait_send()
    write_normed.wait()
    for copy in writes:
        copy.wait()


def begin(shards, x, qkv, wo, gains):
    tokens, model = x.shape
    rows = math.gcd(tokens, 256)
    vmem, hbm = pl.BlockSpec(memory_space=pltpu.VMEM), pl.BlockSpec(memory_space=pl.ANY)
    sem = pltpu.SemaphoreType.DMA
    return pl.pallas_call(
        functools.partial(begin_kernel, shards),
        in_specs=[hbm, vmem, vmem, vmem],
        out_specs=[hbm, hbm, hbm, vmem],
        out_shape=[
            jax.ShapeDtypeStruct((tokens, model), BF16),
            jax.ShapeDtypeStruct((model, qkv.shape[1]), BF16),
            jax.ShapeDtypeStruct((model, wo.shape[1]), BF16),
            jax.ShapeDtypeStruct((gains.shape[0], model), F32),
        ],
        scratch_shapes=[
            pltpu.VMEM((model, qkv.shape[1]), BF16),
            pltpu.VMEM((model, wo.shape[1]), BF16),
            pltpu.VMEM((tokens, model), BF16),
            pltpu.VMEM((2, rows, model), F32),
            pltpu.VMEM((shards,) + gains.shape, F32),
            sem((2, 2, shards)), sem((2, shards)), sem((2, shards)), sem((2, shards)),
            sem((shards,)), sem((shards,)), sem((3,)), sem((2,)), sem((3,)),
        ],
        compiler_params=pltpu.CompilerParams(
            vmem_limit_bytes=48 << 20, collective_id=4, has_side_effects=True
        ),
        cost_estimate=pl.CostEstimate(flops=0, bytes_accessed=120 << 20, transcendentals=0),
        name="norm_and_gather",
    )(x, qkv, wo, gains)


def project_kernel(
    q_heads, n_ref, qkv_ref, spread_ref, cos_ref, sin_ref, krow_ref, vrow_ref, q_ref, kv_ref, wide
):
    @pl.when(pl.program_id(0) == 0)
    def _():
        model = qkv_ref.shape[0]
        block = math.gcd(model, 512)
        for r in range(0, model, block):
            wide[r : r + block, :] = dot(qkv_ref[r : r + block, :], spread_ref[...]).astype(BF16)

    kv_heads = kv_ref.shape[1] // LANES // 2
    cos, sin = cos_ref[...], sin_ref[...]
    out = dot(n_ref[...], wide[...])
    for h in range(q_heads + 2 * kv_heads):
        part = out[:, h * LANES : (h + 1) * LANES]
        if h < q_heads + kv_heads:
            part = part * cos + pltpu.roll(part, LANES // 2, 1) * sin
        if h < q_heads:
            q_ref[:, h * LANES : (h + 1) * LANES] = part.astype(BF16)
        else:
            part = part + (krow_ref[...] if h < q_heads + kv_heads else vrow_ref[...])
            kv_ref[:, (h - q_heads) * LANES : (h - q_heads + 1) * LANES] = part.astype(BF16)


def project(normed, qkv, spread, cos, sin, krow, vrow, q_heads, kv_heads):
    tokens, model = normed.shape
    wide = spread.shape[1]
    bm = math.gcd(tokens, 256)
    whole = lambda a: pl.BlockSpec(a.shape, lambda i: (0, 0))
    row = lambda w: pl.BlockSpec((bm, w), lambda i: (i, 0))
    return pl.pallas_call(
        functools.partial(project_kernel, q_heads),
        grid=(tokens // bm,),
        in_specs=[row(model), whole(qkv), whole(spread), row(LANES), row(LANES), whole(krow), whole(vrow)],
        out_specs=[row(q_heads * LANES), row(2 * kv_heads * LANES)],
        out_shape=[
            jax.ShapeDtypeStruct((tokens, q_heads * LANES), BF16),
            jax.ShapeDtypeStruct((tokens, 2 * kv_heads * LANES), BF16),
        ],
        scratch_shapes=[pltpu.VMEM((model, wide), BF16)],
        compiler_params=pltpu.CompilerParams(vmem_limit_bytes=40 << 20),
        cost_estimate=pl.CostEstimate(
            flops=2 * tokens * model * wide, bytes_accessed=16 << 20, transcendentals=0
        ),
        name="project_qkv",
    )(normed, qkv, spread, cos, sin, krow, vrow)


def dense_kernel(
    chips, dq_ref, dkv_ref, after_ref, cos_ref, sin_ref, rotk_ref, valk_ref, att_ref, n_ref, *rest
):
    blocks, rest = rest[:chips], rest[chips:]
    dense_ref, grad_ref, normed, branch, send, recv, local = rest
    ranks = Ranks(2 * chips)
    fetch = pltpu.make_async_copy(n_ref, normed, local.at[chips])
    fetch.start()
    sem = pltpu.get_barrier_semaphore()
    pl.semaphore_signal(sem, inc=1, device_id={"tp": ranks.peer(0, 1)}, device_id_type=MESH)
    pl.semaphore_wait(sem, 1)
    copies = both_cores(ranks, blocks, branch, send, recv, local)
    for copy in copies:
        copy.start()
    width = dense_ref.shape[1]
    lanes = dkv_ref.shape[1] // 2
    cos, sin = cos_ref[...], sin_ref[...]
    turned = []
    for h in range(lanes // LANES):
        at = slice(h * LANES, (h + 1) * LANES)
        key = dkv_ref[:, at] + after_ref[:, at].astype(F32)
        turned.append((key * cos - pltpu.roll(key, LANES // 2, 1) * sin).astype(BF16))
    dk = dot(jnp.concatenate(turned, axis=1), rotk_ref[...]).astype(BF16)
    dv = (dkv_ref[:, lanes:] + after_ref[:, lanes:].astype(F32)).astype(BF16)
    dv = dot(dv, valk_ref[...]).astype(BF16)
    dense_ref[...] = jnp.concatenate([dq_ref[...], dk, dv], axis=1)
    fetch.wait()
    model = normed.shape[1]
    cols = math.gcd(model, 384)
    for d in range(0, model, cols):
        grad_ref[d : d + cols, :width] = dot(
            normed[:, d : d + cols], dense_ref[...], TN
        ).astype(BF16)
    for copy in copies:
        copy.wait()
    for d in range(0, model, cols):
        grad_ref[d : d + cols, width:] = dot(branch[:, d : d + cols], att_ref[...], TN).astype(BF16)


def dense_gradients(dq, dkv, after, cos, sin, rot_k, val_k, attended, normed, blocks):
    tokens, model = normed.shape
    chips = len(blocks)
    width = dq.shape[1] + 2 * rot_k.shape[1]
    total = width + attended.shape[1]
    vmem, hbm = pl.BlockSpec(memory_space=pltpu.VMEM), pl.BlockSpec(memory_space=pl.ANY)
    sem = pltpu.SemaphoreType.DMA
    return pl.pallas_call(
        functools.partial(dense_kernel, chips),
        in_specs=[vmem] * 8 + [hbm] * (1 + chips),
        out_specs=[vmem, vmem],
        out_shape=[
            jax.ShapeDtypeStruct((tokens, width), BF16),
            jax.ShapeDtypeStruct((model, total), BF16),
        ],
        scratch_shapes=[
            pltpu.VMEM((tokens, model), BF16),
            pltpu.VMEM((tokens, model), BF16),
            sem((chips,)), sem((chips,)), sem((chips + 1,)),
        ],
        compiler_params=pltpu.CompilerParams(
            vmem_limit_bytes=48 << 20, collective_id=5, has_side_effects=True
        ),
        cost_estimate=pl.CostEstimate(
            flops=2 * tokens * model * total, bytes_accessed=24 << 20, transcendentals=0
        ),
        name="dense_gradients",
    )(dq, dkv, after, cos, sin, rot_k, val_k, attended, normed, *blocks)


def close_kernel(
    count, shards, dense_ref, w_ref, x_ref, mg_ref, gain_ref, gain_two_ref, grad_ref, gate_ref, *rest
):
    layers, rest = rest[: count // 2], rest[count // 2 :]
    (
        out_ref, gain_grad_ref, half_ref, lay_ref, gate_out_ref, rows_in, rows_out, sums, c_send, c_recv, y_send,
        y_recv, x_mine, x_recv, gate_mine, gate_recv, t_send, t_recv, cs, cr, ys, yr, g_send, g_recv, xs, xr, x_sem,
        ls, lr, lay_sem, ts, tr, gate_sem, local,
    ) = rest
    ranks = Ranks(count)
    own = rows_in.shape[0]
    halves = 2
    rows = own // halves
    steps = ranks.chips * halves
    fetch = pltpu.make_async_copy(
        x_ref.at[pl.ds(pl.multiple_of(ranks.me * own, own), own)], rows_in, local.at[0]
    )
    fetch.start()
    def tile(at):
        return dot(dense_ref[pl.ds(at, rows), :], w_ref[...], NT)

    piece = lax.axis_index("ctx")
    half = grad_ref.shape[0] // (2 * shards)
    keeps = [
        pltpu.make_async_copy(
            grad_ref.at[half_rows(s, piece, half)], x_mine.at[pl.ds(s * half, half)], x_sem.at[s]
        )
        for s in range(shards)
    ]
    keeps.append(pltpu.make_async_copy(gate_ref, gate_mine, gate_sem.at[0]))
    for copy in keeps:
        copy.start()
    me = lax.axis_index("fsdp")
    barrier = pltpu.get_barrier_semaphore()
    for k, j in ranks.others():
        pl.semaphore_signal(barrier, inc=1, device_id={"tp": ranks.peer(k, j)}, device_id_type=MESH)
    for k in range(1, shards):
        pl.semaphore_signal(
            barrier, inc=1, device_id={"fsdp": lax.rem(me + k, shards)}, device_id_type=MESH
        )
    pl.semaphore_signal(barrier, inc=1, device_id={"ctx": 1 - piece}, device_id_type=MESH)
    pl.semaphore_wait(barrier, count + shards - 1)
    swaps = swap_halves(grad_ref, x_recv, xs, xr, shards)
    swaps.append(
        pltpu.make_async_remote_copy(
            src_ref=gate_ref, dst_ref=gate_recv, send_sem=gate_sem.at[1], recv_sem=gate_sem.at[2],
            device_id={"ctx": 1 - piece}, device_id_type=MESH,
        )
    )
    for copy in swaps:
        copy.start()
    forward = both_cores(ranks, layers, lay_ref, ls, lr, lay_sem)
    for copy in forward:
        copy.start()
    neighbour = ranks.peer(0, 1)

    def to_core(i):
        return remote(c_send.at[i], c_recv.at[i], cs.at[i], cr.at[i], neighbour)

    def to_chip(i, k):
        return remote(y_send.at[i], y_recv.at[i], ys.at[i], yr.at[i], ranks.peer(k, 0))

    def send_step(i, carry):
        k, u, at_mine, at_other = scatter_order(ranks, halves, own, i)
        c_send[i] = tile(at_other).astype(BF16)
        to_core(i).start()
        return carry

    def sum_step(i, carry):
        k, u, at_mine, at_other = scatter_order(ranks, halves, own, i)
        grad = tile(at_mine)
        to_core(i).wait_recv()
        grad = grad + c_recv[i].astype(F32)

        @pl.when(k != 0)
        def _():
            y_send[i] = grad.astype(BF16)
            to_chip(i, k).start()

        @pl.when(k == 0)
        def _():
            sums[u] = grad

        return carry

    lax.fori_loop(0, steps, send_step, 0)
    lax.fori_loop(0, steps, sum_step, 0)
    fetch.wait()
    gain = gain_ref[...]
    gain_total = None
    for u in range(halves):
        total = sums[u]
        for k in range(1, ranks.chips):
            i = (k - 1) * halves + u
            to_chip(i, k).wait_recv()
            total = total + y_recv[i].astype(F32)
        x = rows_in[u * rows : (u + 1) * rows]
        factor = lax.rsqrt(row_mean(x * x) + EPSILON)
        hat = x * factor
        term = jnp.sum(total * hat, axis=0, keepdims=True)
        gain_total = term if gain_total is None else gain_total + term
        inner = total * gain
        grad = mg_ref[u * rows : (u + 1) * rows] + factor * (inner - hat * row_mean(inner * hat))
        rows_out[u * rows : (u + 1) * rows] = grad.astype(BF16)
    gather = GatherRows(ranks, rows_out, out_ref, g_send, g_recv, local.at[0])
    gather.start()
    total = jnp.concatenate([gain_total, gain_two_ref[...], jnp.zeros((6, gain_total.shape[1]), F32)], axis=0)
    hops = [[{"tp": ranks.peer(0, 1)}], [{"tp": ranks.peer(k, 0)} for k in range(1, ranks.chips)]]
    hops += [[{"ctx": 1 - piece}], [{"fsdp": lax.rem(me + k, shards)} for k in range(1, shards)]]
    slot, sent = 0, []
    for n, peers in enumerate(hops):
        t_send[n] = total
        copies = []
        for peer in peers:
            copies.append(
                pltpu.make_async_remote_copy(
                    src_ref=t_send.at[n], dst_ref=t_recv.at[slot], send_sem=ts.at[slot],
                    recv_sem=tr.at[slot], device_id=peer, device_id_type=MESH,
                )
            )
            copies[-1].start()
            slot += 1
        for copy, at in zip(copies, range(slot - len(copies), slot)):
            copy.wait_recv()
            total = total + t_recv[at]
        sent += copies
    gain_grad_ref[...] = total
    for copy in sent:
        copy.wait_send()
    gather.finish()
    for copy in forward:
        copy.wait()
    for s in range(shards):
        keeps[s].wait()
        swaps[s].wait_recv()
        here = slice(s * half, (s + 1) * half)
        half_ref[here, :] = (x_mine[here, :].astype(F32) + x_recv[here, :].astype(F32)).astype(BF16)
    keeps[shards].wait()
    swaps[shards].wait_recv()
    gate_out_ref[...] = gate_mine[...].astype(F32) + gate_recv[...].astype(F32)
    for copy in swaps:
        copy.wait_send()
    for i in range(steps):
        to_core(i).wait_send()
    for i in range(steps - halves):
        to_chip(i, i // halves + 1).wait_send()


def close(count, shards, dense, weight, layer_input, middle_grad, gain, gain_two, grad, gate, layers):
    tokens, model = layer_input.shape
    own = tokens // count
    rows, steps, chips = own // 2, count, count // 2
    vmem, hbm = pl.BlockSpec(memory_space=pltpu.VMEM), pl.BlockSpec(memory_space=pl.ANY)
    sem = pltpu.SemaphoreType.DMA
    return pl.pallas_call(
        functools.partial(close_kernel, count, shards),
        in_specs=[vmem, vmem, hbm, vmem, vmem, vmem, hbm, hbm] + [hbm] * chips,
        out_specs=[hbm, vmem, vmem, hbm, vmem],
        out_shape=[
            jax.ShapeDtypeStruct((tokens, model), BF16),
            jax.ShapeDtypeStruct((8, model), F32),
            jax.ShapeDtypeStruct((model // 2, grad.shape[1]), BF16),
            jax.ShapeDtypeStruct((tokens, model), BF16),
            jax.ShapeDtypeStruct(gate.shape, F32),
        ],
        scratch_shapes=[
            pltpu.VMEM((own, model), F32),
            pltpu.VMEM((own, model), BF16),
            pltpu.VMEM((2, rows, model), F32),
        ]
        + [pltpu.VMEM((steps, rows, model), BF16)] * 2
        + [pltpu.VMEM((steps - 2, rows, model), BF16)] * 2
        + [pltpu.VMEM((model // 2, grad.shape[1]), BF16)] * 2
        + [
            pltpu.VMEM(gate.shape, BF16),
            pltpu.VMEM(gate.shape, BF16),
            pltpu.VMEM((4, 8, model), F32),
            pltpu.VMEM((chips + shards, 8, model), F32),
            sem((steps,)), sem((steps,)), sem((steps - 2,)), sem((steps - 2,)),
            sem((2, chips)), sem((2, chips)), sem((shards,)), sem((shards,)), sem((shards,)),
            sem((chips,)), sem((chips,)), sem((chips,)), sem((chips + shards,)),
            sem((chips + shards,)), sem((3,)), sem((2,)),
        ],
        compiler_params=pltpu.CompilerParams(
            vmem_limit_bytes=48 << 20, collective_id=3, has_side_effects=True
        ),
        cost_estimate=pl.CostEstimate(
            flops=2 * tokens * model * dense.shape[1], bytes_accessed=200 << 20, transcendentals=0
        ),
        name="close_layer",
    )(dense, weight, layer_input, middle_grad, gain, gain_two, grad, gate, *layers)


def per_device(
    sizes,
    layer_input,
    doc_lengths,
    attention_gain,
    query_weight,
    key_matrix,
    value_matrix,
    output_weight,
    feedforward_gain,
    gate_weight,
    up_weight,
    down_weight,
    output_cotangent,
):
    shards, pieces, ranks = sizes
    assert pieces == 2 and ranks % 2 == 0
    chips = ranks // 2
    tokens, model = layer_input.shape
    own = tokens // ranks
    head_dim = HEAD_SIZE
    q_heads = query_weight.shape[1] // head_dim
    kv_heads = key_matrix.shape[1] // head_dim
    q_width, kv_width = q_heads * head_dim, kv_heads * head_dim
    piece = lax.axis_index("ctx")
    rank = lax.axis_index("tp")
    chip, core = rank // 2, rank % 2
    me = lax.axis_index("fsdp")
    scale = 1.0 / math.sqrt(head_dim)

    swap_x = [(0, 1), (1, 0)]
    swap_core = [(i, i ^ 1) for i in range(ranks)]

    def chip_shift(k):
        return [(i, (i + 2 * k) % ranks) for i in range(ranks)]

    def shard_shift(k):
        return [(i, (i + k) % shards) for i in range(shards)]

    def pick(array, index, axis=0):
        return lax.dynamic_index_in_dim(array, index, axis, keepdims=False)

    def half_of(shard):
        rows = shard.shape[0] // 2
        return lax.dynamic_slice_in_dim(shard, piece * rows, rows, 0)

    both_axes = ("fsdp", "ctx")

    def reduce_fsdp(part):
        return lax.psum_scatter(part, "fsdp", scatter_dimension=0, tiled=True)

    def add_pieces(mine):
        return mine.astype(F32) + lax.ppermute(mine, "ctx", swap_x).astype(F32)

    def whole_shard(mine):
        other = lax.ppermute(mine, "ctx", swap_x)
        pair = jnp.where(
            piece == 0, jnp.concatenate([mine, other], 0), jnp.concatenate([other, mine], 0)
        )
        return pair.astype(F32)

    ff_half = half_of(jnp.concatenate([gate_weight, up_weight, down_weight.T], axis=1))
    gain_shard = jnp.stack([attention_gain, feedforward_gain]).astype(F32)
    gain_shard = jnp.pad(gain_shard, ((0, 6), (0, 0)))
    qkv_shard = jnp.concatenate([query_weight, key_matrix, value_matrix], axis=1)
    positions = doc_positions(doc_lengths[0], piece * tokens, tokens)
    cos, sin = rotary_lanes(positions, head_dim)
    lane = lax.broadcasted_iota(jnp.int32, (1, LANES), 1)
    krow = jnp.where((lane >= head_dim // 2) & (lane < head_dim // 2 + 3), -1.0, 0.0)
    vrow = jnp.where((lane >= head_dim) & (lane < head_dim + 3), 1.0, 0.0)
    spread = jnp.zeros((q_width + 2 * kv_width, (q_heads + 2 * kv_heads) * LANES), BF16)
    rot_q, rot_k = select_rotary(q_heads, head_dim), select_rotary(kv_heads, head_dim)
    val_q, val_k = select_value(q_heads, head_dim), select_value(kv_heads, head_dim)
    spread = spread.at[:q_width, : q_heads * LANES].set(rot_q.T)
    spread = spread.at[q_width : q_width + kv_width, q_heads * LANES : (q_heads + kv_heads) * LANES].set(rot_k.T)
    spread = spread.at[q_width + kv_width :, (q_heads + kv_heads) * LANES :].set(val_k.T)

    normed_one, qkv_full, out_own, gains_full = begin(
        shards, layer_input, qkv_shard, output_weight.T, gain_shard
    )
    queries, keys_values = project(
        normed_one, qkv_full, spread, cos, sin, krow, vrow, q_heads, kv_heads
    )
    ff_half, gains_full = lax.optimization_barrier((ff_half, gains_full))
    ff_full = lax.all_gather(ff_half, both_axes, axis=0, tiled=True)
    gain_one, gain_two = gains_full[0:1], gains_full[1:2]
    before = lax.ppermute(keys_values, "ctx", [(0, 1)])
    base = -(piece - 1) * tokens
    ends = jnp.cumsum(doc_lengths[0]).astype(jnp.int32) + base
    base = base.astype(jnp.int32).reshape(1)
    state = attention_forward(ends, base, queries, keys_values, head_dim, tokens)
    attended, marked = attention_forward(
        ends, base, queries, before, head_dim, 0, state, val_q
    )
    wo = [out_own] + [lax.ppermute(out_own, "tp", chip_shift(k)) for k in range(1, chips)]
    normed_two, middle, wo_others = mix(ranks, attended, layer_input, gain_two, wo)
    (
        feed_sums, middle_grad, branch_grad, gain_two_grad, attended_grad, gate_part, feed_part,
    ) = feedforward(
        ranks, normed_two, output_cotangent, middle, gain_two, ff_full, wo, wo_others
    )
    gate_own, feed_own = reduce_fsdp(gate_part), reduce_fsdp(feed_part)
    cut = feed_sums.reshape(chips, own, model)
    feed_sums = [lax.ppermute(cut[k - 1], "tp", chip_shift(k)) for k in range(1, chips)]
    dq_part, dkv_before = attention_backward(
        ends, base, marked, attended_grad, attended, before, val_q.T, head_dim, 0
    )
    after = lax.ppermute(dkv_before, "ctx", [(1, 0)])
    dq, dkv = attention_backward(
        ends, base, marked, attended_grad, attended, keys_values, val_q.T, head_dim, tokens,
        (dq_part, cos, sin, rot_q),
    )

    feed_sums, dq = lax.optimization_barrier((feed_sums, dq))
    layer_rows = middle + cut[chips - 1].astype(F32)
    for block in feed_sums:
        layer_rows = layer_rows + block.astype(F32)
    layer_rows = layer_rows.astype(BF16)

    def from_chips(rows):
        return [rows] + [lax.ppermute(rows, "tp", chip_shift(k)) for k in range(1, chips)]

    dqkv, attention_part = dense_gradients(
        dq, dkv, after, cos, sin, rot_k, val_k, attended, normed_one, from_chips(branch_grad)
    )
    input_gradient, gains, attention_half, layer_output, gate = close(
        ranks, shards, dqkv, qkv_full, layer_input, middle_grad, gain_one, gain_two_grad,
        attention_part, gate_own, from_chips(layer_rows),
    )
    attention_half, feed_own = lax.optimization_barrier((attention_half, feed_own))
    attention = whole_shard(reduce_fsdp(attention_half))
    feed = add_pieces(feed_own)
    layer_output, input_gradient = layer_output.astype(F32), input_gradient.astype(F32)
    ff_width = gate_weight.shape[1]
    gains = lax.dynamic_slice_in_dim(gains, me * gain_shard.shape[1], gain_shard.shape[1], 1)

    return (
        layer_output,
        input_gradient,
        gains[0],
        attention[:, :q_width],
        attention[:, q_width : q_width + kv_width],
        attention[:, q_width + kv_width : q_width + 2 * kv_width],
        attention[:, q_width + 2 * kv_width :].T,
        gains[1],
        gate,
        feed[:, :ff_width],
        feed[:, ff_width:].T,
    )


def solution(mesh):
    rows = P(("fsdp", "ctx"), None)
    into, out_of = P("fsdp", "tp"), P("tp", "fsdp")
    sizes = (mesh.shape["fsdp"], mesh.shape["ctx"], mesh.shape["tp"])
    return jax.shard_map(
        functools.partial(per_device, sizes),
        mesh=mesh,
        in_specs=(
            rows, P("fsdp", None), P("fsdp"), into, into, into, out_of, P("fsdp"), into, into,
            out_of, rows,
        ),
        out_specs=(
            rows, rows, P("fsdp"), into, into, into, out_of, P("fsdp"), into, into, out_of,
        ),
        check_vma=False,
    )
```

```python
import functools
import math

import jax
import jax.numpy as jnp
from jax import lax
from jax.experimental import pallas as pl
from jax.experimental.pallas import tpu as pltpu
from jax.sharding import PartitionSpec as P

HEAD_SIZE = 96
EPSILON = 1e-05
THETA = 100000.0
NEGATIVE = -1e30
LOG2E = 1.4426950408889634
LANES = 128
F32 = jnp.float32
BF16 = jnp.bfloat16
NN = (((1,), (0,)), ((), ()))
NT = (((1,), (1,)), ((), ()))
TN = (((0,), (0,)), ((), ()))


def dot(left, right, dims=NN):
    return lax.dot_general(left, right, dims, preferred_element_type=F32)


def select_rotary(heads, head_dim):
    shape = (heads * LANES, heads * head_dim)
    row = lax.broadcasted_iota(jnp.int32, shape, 0)
    col = lax.broadcasted_iota(jnp.int32, shape, 1)
    half = head_dim // 2
    within = col % head_dim
    want = (col // head_dim) * LANES + jnp.where(within < half, within, within - half + LANES // 2)
    return (row == want).astype(BF16)


def select_value(heads, head_dim):
    shape = (heads * LANES, heads * head_dim)
    row = lax.broadcasted_iota(jnp.int32, shape, 0)
    col = lax.broadcasted_iota(jnp.int32, shape, 1)
    return (row == (col // head_dim) * LANES + col % head_dim).astype(BF16)


def rotary_lanes(positions, head_dim):
    half = head_dim // 2
    freqs = THETA ** (-(jnp.arange(half, dtype=F32) * 2.0 / head_dim))
    angles = positions.astype(F32)[:, None] * freqs[None, :]
    cos, sin = jnp.cos(angles), jnp.sin(angles)
    pad = jnp.zeros((positions.shape[0], LANES // 2 - half), F32)
    return (
        jnp.concatenate([cos, pad, cos, pad], axis=1),
        jnp.concatenate([-sin, pad, sin, pad], axis=1),
    )


def doc_positions(lengths, first, count):
    ends = jnp.cumsum(lengths)
    starts = ends - lengths
    index = first + jnp.arange(count, dtype=jnp.int32)
    document = jnp.sum((index[None, :] >= ends[:, None]).astype(jnp.int32), axis=0)
    chosen = document[None, :] == jnp.arange(lengths.shape[0], dtype=jnp.int32)[:, None]
    start_of = jnp.sum(jnp.where(chosen, starts[:, None], 0), axis=0)
    return index - start_of


def doc_start(ends_ref, base, rows):
    start = base if jnp.ndim(rows) == 0 else jnp.zeros_like(rows) + base
    for j in range(ends_ref.shape[0]):
        end = ends_ref[j]
        start = jnp.where(rows >= end, jnp.maximum(start, end), start)
    return start


def put_lanes(rows, column, lane):
    at = lax.broadcasted_iota(jnp.int32, rows.shape, 1)
    high = column.astype(BF16).astype(F32)
    rest = column - high
    mid = rest.astype(BF16).astype(F32)
    low = rest - mid
    wide = rows.astype(F32)
    wide = jnp.where(at == lane, high, wide)
    wide = jnp.where(at == lane + 1, mid, wide)
    return jnp.where(at == lane + 2, low, wide).astype(BF16)


def block_ranges(first_row, rows, block, low, last_low, key_base, key_count):
    begin = (jnp.maximum(low, key_base) - key_base) // block
    stop = jnp.minimum((first_row + rows - key_base + block - 1) // block, key_count // block)
    inner = jnp.minimum(jnp.maximum((last_low - key_base + block - 1) // block, begin), stop)
    diagonal = jnp.minimum(jnp.maximum((first_row - key_base) // block, inner), stop)
    return begin, inner, diagonal, stop


def stack_heads(ref, kv, group):
    parts = [ref[:, (kv * group + g) * LANES : (kv * group + g + 1) * LANES] for g in range(group)]
    return jnp.concatenate(parts, axis=0)


def row_marks(ends_ref, base, first_row, bq, group):
    rows = lax.broadcasted_iota(jnp.int32, (1, bq), 1) + first_row
    starts = doc_start(ends_ref, base, rows)
    return jnp.concatenate([rows] * group, axis=1), jnp.concatenate([starts] * group, axis=1)


def attention_forward_kernel(
    first, key_base, tokens, bq, bk, head_dim, group, ends_ref, base_ref, q_ref, kv_ref, *rest
):
    if first:
        max_ref, acc_ref = rest
    else:
        sel_ref, max_in, acc_in, o_ref, qa_ref, max_ref, acc_ref = rest
    first_row = tokens + pl.program_id(0) * bq
    base = base_ref[0]
    low = doc_start(ends_ref, base, first_row)
    last_low = doc_start(ends_ref, base, first_row + bq - 1)
    rows, starts = row_marks(ends_ref, base, first_row, bq, group)
    kv_heads = kv_ref.shape[1] // LANES // 2
    unit = LOG2E / math.sqrt(head_dim)
    queries = [stack_heads(q_ref, h, group) for h in range(kv_heads)]
    if first:
        max_ref[...] = jnp.full(max_ref.shape, NEGATIVE, F32)
        acc_ref[...] = jnp.zeros(acc_ref.shape, F32)
    else:
        max_ref[...] = max_in[...]
        acc_ref[...] = acc_in[...]

    def body(masked, index, carry):
        at = pl.multiple_of(index * bk, bk)
        if masked:
            keys = lax.broadcasted_iota(jnp.int32, (bk, group * bq), 0) + (at + key_base)
            keep = (keys <= rows) & (keys >= starts)
        for h in range(kv_heads):
            key = kv_ref[pl.ds(at, bk), h * LANES : (h + 1) * LANES]
            value = kv_ref[pl.ds(at, bk), (kv_heads + h) * LANES : (kv_heads + h + 1) * LANES]
            scores = dot(key, queries[h], NT)
            if masked:
                scores = jnp.where(keep, scores, NEGATIVE)
            old = max_ref[0, h]
            new = jnp.maximum(old, jnp.max(scores, axis=0, keepdims=True))
            probs = jnp.exp2((scores - new) * unit)
            if masked:
                probs = jnp.where(keep, probs, 0.0)
            acc_ref[0, h] = acc_ref[0, h] * jnp.exp2((old - new) * unit) + dot(
                value, probs.astype(BF16), TN
            )
            max_ref[0, h] = new
        return carry

    begin, inner, diagonal, stop = block_ranges(
        first_row, bq, bk, low, last_low, key_base, kv_ref.shape[0]
    )
    lax.fori_loop(begin, inner, functools.partial(body, True), 0)
    lax.fori_loop(inner, diagonal, functools.partial(body, False), 0)
    lax.fori_loop(diagonal, stop, functools.partial(body, True), 0)
    if first:
        return
    outs = []
    for h in range(kv_heads):
        acc = acc_ref[0, h]
        total = acc[head_dim : head_dim + 1, :]
        out = jnp.transpose(acc * (1.0 / total)).astype(BF16)
        logsum = jnp.broadcast_to(max_ref[0, h] + jnp.log2(total) * (1.0 / unit), (8, group * bq))
        marked = put_lanes(queries[h], jnp.transpose(logsum)[:, :1], head_dim // 2)
        for g in range(group):
            head = h * group + g
            qa_ref[:, head * LANES : (head + 1) * LANES] = marked[g * bq : (g + 1) * bq]
            outs.append(out[g * bq : (g + 1) * bq])
    o_ref[...] = dot(jnp.concatenate(outs, axis=1), sel_ref[...]).astype(BF16)


def attention_forward(ends, base, q, kv, head_dim, key_base, state=None, select=None):
    tokens, width = q.shape
    kv_heads = kv.shape[1] // LANES // 2
    group = width // LANES // kv_heads
    bq = bk = math.gcd(tokens, 512)
    steps = tokens // bq
    whole = lambda a: pl.BlockSpec(a.shape, lambda i, *_: (0, 0))
    row = lambda w: pl.BlockSpec((bq, w), lambda i, *_: (i, 0))
    shapes = [(steps, kv_heads, 1, group * bq), (steps, kv_heads, LANES, group * bq)]
    kept = [pl.BlockSpec((1,) + a[1:], lambda i, *_: (i, 0, 0, 0)) for a in shapes]
    pairs = tokens * tokens * group * kv_heads // 2
    if state is None:
        in_specs, operands = [row(width), whole(kv)], (q, kv)
        out_specs, out_shape = kept, [jax.ShapeDtypeStruct(a, F32) for a in shapes]
        scratch = []
    else:
        in_specs, operands = [row(width), whole(kv), whole(select)] + kept, (q, kv, select) + tuple(state)
        out_specs = [row(select.shape[1]), row(width)]
        out_shape = [
            jax.ShapeDtypeStruct((tokens, select.shape[1]), BF16),
            jax.ShapeDtypeStruct(q.shape, BF16),
        ]
        scratch = [pltpu.VMEM((1,) + a[1:], F32) for a in shapes]
    return pl.pallas_call(
        functools.partial(
            attention_forward_kernel, state is None, key_base, tokens, bq, bk, head_dim, group
        ),
        grid_spec=pltpu.PrefetchScalarGridSpec(
            num_scalar_prefetch=2, grid=(steps,), in_specs=in_specs, out_specs=out_specs,
            scratch_shapes=scratch,
        ),
        out_shape=out_shape,
        compiler_params=pltpu.CompilerParams(vmem_limit_bytes=40 << 20),
        cost_estimate=pl.CostEstimate(
            flops=pairs * 1024, bytes_accessed=8 << 20, transcendentals=pairs
        ),
        name="attention_forward",
    )(ends, base, *operands)


def attention_backward_kernel(
    first, key_base, tokens, bq, bk, head_dim, group,
    ends_ref, base_ref, qa_ref, do_ref, o_ref, kv_ref, spread_ref, *rest
):
    if first:
        dq_ref, dkv_ref, dk_acc, dv_acc, dq_acc = rest
    else:
        part_ref, cos_ref, sin_ref, sel_ref, dq_ref, dkv_ref, dk_acc, dv_acc, dq_acc = rest
    step = pl.program_id(0)
    first_row = tokens + step * bq
    base = base_ref[0]
    low = doc_start(ends_ref, base, first_row)
    last_low = doc_start(ends_ref, base, first_row + bq - 1)
    kv_heads = kv_ref.shape[1] // LANES // 2
    scale = 1.0 / math.sqrt(head_dim)
    unit = LOG2E * scale
    begin, inner, diagonal, stop = block_ranges(
        first_row, bq, bk, low, last_low, key_base, kv_ref.shape[0]
    )

    @pl.when(step == 0)
    def _():
        dk_acc[...] = jnp.zeros(dk_acc.shape, F32)
        dv_acc[...] = jnp.zeros(dv_acc.shape, F32)

    if first:
        dq_acc[...] = jnp.zeros(dq_acc.shape, F32)
    else:
        for h in range(kv_heads):
            dq_acc[h] = stack_heads(part_ref, h, group)

    @pl.when(begin < stop)
    def _():
        rows, starts = row_marks(ends_ref, base, first_row, bq, group)
        grads_wide = dot(do_ref[...], spread_ref[...])
        outs_wide = dot(o_ref[...], spread_ref[...])
        queries, grads = [], []
        for h in range(kv_heads):
            queries.append(stack_heads(qa_ref, h, group))
            grad = stack_heads(grads_wide, h, group)
            inner_sum = jnp.sum(grad * stack_heads(outs_wide, h, group), axis=1, keepdims=True)
            grads.append(put_lanes(grad, -inner_sum, head_dim))

        def body(masked, index, carry):
            at = pl.multiple_of(index * bk, bk)
            if masked:
                keys = lax.broadcasted_iota(jnp.int32, (bk, group * bq), 0) + (at + key_base)
                keep = (keys <= rows) & (keys >= starts)
            for h in range(kv_heads):
                key = kv_ref[pl.ds(at, bk), h * LANES : (h + 1) * LANES]
                value = kv_ref[pl.ds(at, bk), (kv_heads + h) * LANES : (kv_heads + h + 1) * LANES]
                probs = jnp.exp2(dot(key, queries[h], NT) * unit)
                if masked:
                    probs = jnp.where(keep, probs, 0.0)
                slope = (probs * dot(value, grads[h], NT)).astype(BF16)
                dv_acc[h, pl.ds(at, bk), :] += dot(probs.astype(BF16), grads[h])
                dk_acc[h, pl.ds(at, bk), :] += dot(slope, queries[h])
                dq_acc[h] += dot(slope, key, TN)
            return carry

        lax.fori_loop(begin, inner, functools.partial(body, True), 0)
        lax.fori_loop(inner, diagonal, functools.partial(body, False), 0)
        lax.fori_loop(diagonal, stop, functools.partial(body, True), 0)

    outs = []
    for h in range(kv_heads):
        for g in range(group):
            grad = dq_acc[h, g * bq : (g + 1) * bq, :]
            if first:
                dq_ref[:, (h * group + g) * LANES : (h * group + g + 1) * LANES] = grad
            else:
                grad = grad * scale
                outs.append(
                    (grad * cos_ref[...] - pltpu.roll(grad, LANES // 2, 1) * sin_ref[...]).astype(BF16)
                )
    if not first:
        dq_ref[...] = dot(jnp.concatenate(outs, axis=1), sel_ref[...]).astype(BF16)

    @pl.when(step == pl.num_programs(0) - 1)
    def _():
        for h in range(kv_heads):
            dkv_ref[:, h * LANES : (h + 1) * LANES] = (dk_acc[h] * scale).astype(dkv_ref.dtype)
            dkv_ref[:, (kv_heads + h) * LANES : (kv_heads + h + 1) * LANES] = dv_acc[h].astype(dkv_ref.dtype)


def attention_backward(ends, base, qa, grad, out, kv, spread, head_dim, key_base, rest=None):
    tokens, width = qa.shape
    keys = kv.shape[0]
    kv_heads = kv.shape[1] // LANES // 2
    group = width // LANES // kv_heads
    bq = bk = math.gcd(tokens, 512)
    whole = lambda a: pl.BlockSpec(a.shape, lambda i, *_: (0, 0))
    row = lambda w: pl.BlockSpec((bq, w), lambda i, *_: (i, 0))
    pairs = tokens * tokens * group * kv_heads // 2
    in_specs = [row(width), row(grad.shape[1]), row(out.shape[1]), whole(kv), whole(spread)]
    operands = (qa, grad, out, kv, spread)
    if rest is None:
        dq_width, dq_type, dkv_type = width, F32, BF16
    else:
        part, cos, sin, select = rest
        in_specs += [row(width), row(LANES), row(LANES), whole(select)]
        operands += (part, cos, sin, select)
        dq_width, dq_type, dkv_type = select.shape[1], BF16, F32
    return pl.pallas_call(
        functools.partial(
            attention_backward_kernel, rest is None, key_base, tokens, bq, bk, head_dim, group
        ),
        grid_spec=pltpu.PrefetchScalarGridSpec(
            num_scalar_prefetch=2,
            grid=(tokens // bq,),
            in_specs=in_specs,
            out_specs=[row(dq_width), whole(kv)],
            scratch_shapes=[
                pltpu.VMEM((kv_heads, keys, LANES), F32),
                pltpu.VMEM((kv_heads, keys, LANES), F32),
                pltpu.VMEM((kv_heads, group * bq, LANES), F32),
            ],
        ),
        out_shape=[
            jax.ShapeDtypeStruct((tokens, dq_width), dq_type),
            jax.ShapeDtypeStruct(kv.shape, dkv_type),
        ],
        compiler_params=pltpu.CompilerParams(vmem_limit_bytes=48 << 20),
        cost_estimate=pl.CostEstimate(
            flops=pairs * 2560, bytes_accessed=12 << 20, transcendentals=pairs
        ),
        name="attention_backward",
    )(ends, base, qa, grad, out, kv, spread, *operands[5:])


MESH = pl.DeviceIdType.MESH


class Ranks:
    def __init__(self, count):
        self.count, self.chips = count, count // 2
        self.me = lax.axis_index("tp")
        self.chip, self.core = self.me // 2, self.me % 2

    def peer(self, k, j):
        return lax.rem(self.chip + k + self.chips, self.chips) * 2 + lax.rem(self.core + j, 2)

    def others(self):
        return [(k, j) for k in range(self.chips) for j in range(2) if k or j]

    def barrier(self):
        sem = pltpu.get_barrier_semaphore()
        for k, j in self.others():
            pl.semaphore_signal(sem, inc=1, device_id={"tp": self.peer(k, j)}, device_id_type=MESH)
        pl.semaphore_wait(sem, self.count - 1)


def remote(src, dst, send, recv, rank):
    return pltpu.make_async_remote_copy(
        src_ref=src, dst_ref=dst, send_sem=send, recv_sem=recv, device_id={"tp": rank},
        device_id_type=MESH,
    )


def row_mean(x):
    return jnp.sum(x, axis=-1, keepdims=True) * (1.0 / x.shape[-1])


class GatherRows:
    def __init__(self, ranks, rows_ref, out_ref, send, recv, local):
        own = rows_ref.shape[0]
        self.ranks, self.send, self.recv = ranks, send, recv
        self.at = lambda rank: out_ref.at[pl.ds(pl.multiple_of(rank * own, own), own)]
        self.keep = pltpu.make_async_copy(rows_ref, self.at(ranks.me), local)
        self.copies = []
        for k in list(range(1, ranks.chips)) + [0]:
            peer = ranks.peer(k, 0) if k else ranks.peer(0, 1)
            self.copies.append(remote(rows_ref, self.at(ranks.me), send.at[0, k], recv.at[0, k], peer))

    def start(self):
        for copy in self.copies:
            copy.start()
        self.keep.start()

    def finish(self):
        ranks, passed = self.ranks, []
        for k, copy in zip(range(1, ranks.chips), self.copies):
            copy.wait_recv()
            held = self.at(ranks.peer(-k, 0))
            passed.append(
                remote(held, held, self.send.at[1, k], self.recv.at[1, k], ranks.peer(0, 1))
            )
            passed[-1].start()
        self.copies[-1].wait_recv()
        for copy in self.copies:
            copy.wait_send()
        for copy in passed:
            copy.wait()
        self.keep.wait()


def both_cores(ranks, blocks, out_ref, send, recv, local):
    own = blocks[0].shape[0]
    copies = []
    for k, block in enumerate(blocks):
        there = out_ref.at[pl.ds(pl.multiple_of(ranks.peer(-k, 0) * own, own), own)]
        copies.append(remote(block, there, send.at[k], recv.at[k], ranks.peer(0, 1)))
        copies.append(pltpu.make_async_copy(block, there, local.at[k]))
    return copies


def mix_kernel(count, att_ref, x_ref, gain_ref, *rest):
    chips = count // 2
    blocks, rest = rest[:chips], rest[chips:]
    (
        n2_ref, mid_ref, other_ref, heads, rows_in, rows_out, others, a_send, a_recv, b_send, b_recv,
        g_send, g_recv, local,
    ) = rest
    ranks = Ranks(count)
    own = rows_in.shape[0]
    mine_at = pl.ds(pl.multiple_of(ranks.me * own, own), own)
    fetch = pltpu.make_async_copy(x_ref.at[mine_at], rows_in, local.at[0])
    fetch.start()
    mine = pltpu.make_async_copy(att_ref.at[mine_at], heads.at[0], local.at[1])
    mine.start()
    ranks.barrier()
    copies = {}
    for k, j in ranks.others()[::-1]:
        peer, slot = ranks.peer(k, j), 2 * k + j
        copies[slot] = remote(
            att_ref.at[pl.ds(pl.multiple_of(peer * own, own), own)], heads.at[slot],
            a_send.at[slot], a_recv.at[slot], peer,
        )
        copies[slot].start()
    swaps = [
        remote(blocks[k], others.at[k], b_send.at[k], b_recv.at[k], ranks.peer(0, 1))
        for k in range(chips)
    ]
    for copy in swaps:
        copy.start()
    fetch.wait()
    mine.wait()
    mid_ref[...] = rows_in[...] + dot(heads[0], blocks[0][...], NT)
    keeps = []
    for slot in range(1, count):
        k = slot // 2
        if slot % 2:
            swaps[k].wait_recv()
            keeps.append(pltpu.make_async_copy(others.at[k], other_ref.at[k], local.at[2 + k]))
            keeps[-1].start()
        copies[slot].wait_recv()
        mid_ref[...] += dot(heads[slot], others[k] if slot % 2 else blocks[k][...], NT)
    mid = mid_ref[...]
    factor = lax.rsqrt(row_mean(mid * mid) + EPSILON)
    rows_out[...] = (mid * factor * gain_ref[...]).astype(BF16)
    gather = GatherRows(ranks, rows_out, n2_ref, g_send, g_recv, local.at[0])
    gather.start()
    for slot in range(1, count):
        copies[slot].wait_send()
    for copy in swaps:
        copy.wait_send()
    for copy in keeps:
        copy.wait()
    gather.finish()


def mix(count, attended, layer_input, gain, blocks):
    tokens, model = layer_input.shape
    own = tokens // count
    chips = count // 2
    width = attended.shape[1]
    vmem, hbm = pl.BlockSpec(memory_space=pltpu.VMEM), pl.BlockSpec(memory_space=pl.ANY)
    sem = pltpu.SemaphoreType.DMA
    return pl.pallas_call(
        functools.partial(mix_kernel, count),
        in_specs=[hbm, hbm, vmem] + [vmem] * chips,
        out_specs=[hbm, vmem, hbm],
        out_shape=[
            jax.ShapeDtypeStruct((tokens, model), BF16),
            jax.ShapeDtypeStruct((own, model), F32),
            jax.ShapeDtypeStruct((chips, model, width), BF16),
        ],
        scratch_shapes=[
            pltpu.VMEM((count, own, width), BF16),
            pltpu.VMEM((own, model), F32),
            pltpu.VMEM((own, model), BF16),
            pltpu.VMEM((chips, model, width), BF16),
            sem((count,)), sem((count,)), sem((chips,)), sem((chips,)), sem((2, chips)),
            sem((2, chips)), sem((2 + chips,)),
        ],
        compiler_params=pltpu.CompilerParams(
            vmem_limit_bytes=40 << 20, collective_id=1, has_side_effects=True
        ),
        cost_estimate=pl.CostEstimate(
            flops=2 * tokens * model * model, bytes_accessed=150 << 20, transcendentals=0
        ),
        name="mix_heads",
    )(attended, layer_input, gain, *blocks)


def scatter_order(ranks, halves, own, i):
    k = lax.rem(i // halves + 1, ranks.chips)
    half = lax.rem(i, halves)
    rows = own // halves
    at = lambda j: pl.multiple_of(ranks.peer(k, j) * own + half * rows, rows)
    return k, half, at(0), at(1)


def half_rows(shard, which, half):
    return pl.ds(pl.multiple_of((shard * 2 + which) * half, half), half)


def swap_halves(src, dst, send, recv, shards):
    piece = lax.axis_index("ctx")
    half = src.shape[0] // (2 * shards)
    return [
        pltpu.make_async_remote_copy(
            src_ref=src.at[half_rows(s, 1 - piece, half)], dst_ref=dst.at[pl.ds(s * half, half)],
            send_sem=send.at[s], recv_sem=recv.at[s], device_id={"ctx": 1 - piece},
            device_id_type=MESH,
        )
        for s in range(shards)
    ]


def signal_piece(count):
    ranks = Ranks(count)
    sem = pltpu.get_barrier_semaphore()
    for k, j in ranks.others():
        pl.semaphore_signal(sem, inc=1, device_id={"tp": ranks.peer(k, j)}, device_id_type=MESH)
    pl.semaphore_signal(sem, inc=1, device_id={"ctx": 1 - lax.axis_index("ctx")}, device_id_type=MESH)
    pl.semaphore_wait(sem, count)


def feedforward_kernel(count, shards, n2_ref, cot_ref, mid_ref, gain_ref, other_ref, weight_ref, *rest):
    blocks, rest = rest[: count // 2], rest[count // 2 :]
    (
        ffb_ref, mg_ref, bg_ref, gain_grad_ref, da_ref, gate_ref, up_ref, down_ref,
        gate_w, up_w, down_w, n2, fg, hid, gu, rows_in, ffb_out,
        c_send, c_recv, y_send, y_recv, f_send, f_recv, heads, x_recv,
        w_sem, in_sem, out_sem, cs, cr, ys, yr, fs, fr, hs, hr, xs, xr, local,
    ) = rest
    ranks = Ranks(count)
    own = mg_ref.shape[0]
    halves = 2
    rows = own // halves
    steps = ranks.chips * halves
    width = gate_w.shape[1]
    model = n2.shape[1]
    loads = [pltpu.make_async_copy(n2_ref, n2, w_sem.at[3])] + [
        pltpu.make_async_copy(weight_ref.at[:, pl.ds(w * width, width)], full, w_sem.at[w])
        for w, full in enumerate((gate_w, up_w, down_w))
    ]
    for load in loads:
        load.start()

    def read(at, slot):
        return pltpu.make_async_copy(cot_ref.at[pl.ds(at, rows)], rows_in.at[slot], in_sem.at[slot])

    def tile(at, slot, begin):
        here = pl.ds(at, rows)

        def ready(n):
            if begin is not None:
                @pl.when(begin)
                def _():
                    loads[n].wait()

        ready(0)
        ready(1)
        n = n2[here, :]
        grad = rows_in[slot].astype(BF16)
        fg[here, :] = grad
        gate = dot(n, gate_w[...])
        ready(2)
        up = dot(n, up_w[...])
        ready(3)
        back = dot(grad, down_w[...])
        sig = 1.0 / (1.0 + jnp.exp(-gate))
        act = gate * sig
        hidden = (act * up).astype(BF16)
        hid[here, :] = hidden
        gg = (back * up * (sig * (1.0 + gate * (1.0 - sig)))).astype(BF16)
        gu[here, :width] = gg
        ug = (back * act).astype(BF16)
        gu[here, width:] = ug
        return dot(gg, gate_w[...], NT) + dot(ug, up_w[...], NT), dot(hidden, down_w[...], NT)

    read(scatter_order(ranks, halves, own, 0)[3], 0).start()
    signal_piece(count)
    neighbour = ranks.peer(0, 1)

    def to_core(i):
        slot = lax.rem(i, 2)
        return [
            remote(c_send.at[slot], c_recv.at[slot], cs.at[slot], cr.at[slot], neighbour),
            remote(f_send.at[slot], f_recv.at[slot], fs.at[slot], fr.at[slot], neighbour),
        ]

    def to_chip(i, k):
        return remote(y_send.at[i], y_recv.at[i], ys.at[i], yr.at[i], ranks.peer(k, 0))

    def ffb_write(i):
        return pltpu.make_async_copy(ffb_out, ffb_ref.at[i], out_sem.at[0])

    def step(i, carry):
        k, u, at_mine, at_other = scatter_order(ranks, halves, own, i)
        slot = lax.rem(i, 2)
        read(at_mine, 1).start()
        read(at_other, 0).wait()
        grad, forward = tile(at_other, 0, i == 0)

        @pl.when(i + 1 < steps)
        def _():
            read(scatter_order(ranks, halves, own, i + 1)[3], 0).start()

        @pl.when(i > 1)
        def _():
            for copy in to_core(i):
                copy.wait_send()

        c_send[slot] = grad.astype(BF16)
        f_send[slot] = forward.astype(BF16)
        for copy in to_core(i):
            copy.start()
        read(at_mine, 1).wait()
        grad, forward = tile(at_mine, 1, None)

        @pl.when(i > 0)
        def _():
            ffb_write(i).wait()

        for copy in to_core(i):
            copy.wait_recv()
        grad = grad + c_recv[slot].astype(F32)
        ffb_out[...] = (forward + f_recv[slot].astype(F32)).astype(BF16)
        ffb_write(i).start()

        @pl.when(k != 0)
        def _():
            y_send[i] = grad.astype(BF16)
            to_chip(i, k).start()

        @pl.when(k == 0)
        def _():
            mg_ref[pl.ds(pl.multiple_of(u * rows, rows), rows), :] = grad

        return carry

    lax.fori_loop(0, steps, step, 0)
    mine_at = pl.multiple_of(ranks.me * own, own)
    fetch = lambda u: [
        pltpu.make_async_copy(mid_ref.at[pl.ds(u * rows, rows)], rows_in.at[0], in_sem.at[0]),
        read(mine_at + u * rows, 1),
    ]
    for copy in fetch(0):
        copy.start()
    cols = math.gcd(model, 384)
    writes = []

    def product(left, right, full, pairs):
        for d in range(model // cols):
            full[d * cols : (d + 1) * cols, :] = dot(
                left[:, d * cols : (d + 1) * cols], right, TN
            ).astype(BF16)
        for src, dst in pairs:
            writes.append(pltpu.make_async_copy(src, dst, out_sem.at[1 + len(writes)]))
            writes[-1].start()

    swaps = swap_halves(gate_w, x_recv, xs, xr, shards)
    per_shard = model // shards
    for d in range(model // cols):
        gate_w[d * cols : (d + 1) * cols, :] = dot(
            n2[:, d * cols : (d + 1) * cols], gu[:, :width], TN
        ).astype(BF16)
        for s in range(shards):
            if d * cols < (s + 1) * per_shard <= (d + 1) * cols:
                swaps[s].start()
    gain = gain_ref[...]
    gain_total = None
    for u in range(halves):
        here = slice(u * rows, (u + 1) * rows)
        total = mg_ref[here, :]
        for k in range(1, ranks.chips):
            i = (k - 1) * halves + u
            to_chip(i, k).wait_recv()
            total = total + y_recv[i].astype(F32)
        for copy in fetch(u):
            copy.wait()
        mid = rows_in[0]
        factor = lax.rsqrt(row_mean(mid * mid) + EPSILON)
        hat = mid * factor
        term = jnp.sum(total * hat, axis=0, keepdims=True)
        gain_total = term if gain_total is None else gain_total + term
        inner = total * gain
        grad = rows_in[1] + factor * (inner - hat * row_mean(inner * hat))
        mg_ref[here, :] = grad
        bg_ref[here, :] = grad.astype(BF16)
        if u + 1 < halves:
            for copy in fetch(u + 1):
                copy.start()
    gain_grad_ref[...] = gain_total
    back = []
    for k, j in ranks.others()[::-1]:
        slot, peer = 2 * k + j, ranks.peer(-k, j)
        heads[slot] = dot(bg_ref[...], other_ref[k] if j else blocks[k][...]).astype(BF16)
        back.append(
            remote(heads.at[slot], da_ref.at[pl.ds(mine_at, own)], hs.at[slot], hr.at[slot], peer)
        )
        back[-1].start()
    heads[0] = dot(bg_ref[...], blocks[0][...]).astype(BF16)
    keep = pltpu.make_async_copy(heads.at[0], da_ref.at[pl.ds(mine_at, own)], local.at[0])
    keep.start()
    product(n2, gu[:, width:], up_w, [(up_w, up_ref)])
    product(fg, hid[...], down_w, [(down_w, down_ref)])
    for i in (steps - 2, steps - 1):
        for copy in to_core(i):
            copy.wait_send()
    for i in range(steps - halves):
        to_chip(i, i // halves + 1).wait_send()
    ffb_write(steps - 1).wait()
    for copy in back:
        copy.wait()
    keep.wait()
    half = per_shard // 2
    piece = lax.axis_index("ctx")
    for s in range(shards):
        swaps[s].wait_recv()
        here = slice(s * half, (s + 1) * half)
        gate_ref[here, :] = (
            gate_w[half_rows(s, piece, half), :].astype(F32) + x_recv[here, :].astype(F32)
        ).astype(BF16)
    for copy in swaps:
        copy.wait_send()
    for copy in writes:
        copy.wait()


def feedforward(count, shards, n2, cotangent, middle, gain, weights, blocks, others):
    tokens, model = n2.shape
    own = tokens // count
    hidden = weights.shape[1] // 3
    width = blocks[0].shape[1]
    rows, steps = own // 2, count
    vmem, hbm = pl.BlockSpec(memory_space=pltpu.VMEM), pl.BlockSpec(memory_space=pl.ANY)
    sem = pltpu.SemaphoreType.DMA
    return pl.pallas_call(
        functools.partial(feedforward_kernel, count, shards),
        in_specs=[hbm, hbm, hbm, vmem, vmem, hbm] + [vmem] * (count // 2),
        out_specs=[hbm, vmem, vmem, vmem, hbm, vmem, hbm, hbm],
        out_shape=[
            jax.ShapeDtypeStruct((steps, rows, model), BF16),
            jax.ShapeDtypeStruct((own, model), F32),
            jax.ShapeDtypeStruct((own, model), BF16),
            jax.ShapeDtypeStruct((1, model), F32),
            jax.ShapeDtypeStruct((tokens, width), BF16),
            jax.ShapeDtypeStruct((model // 2, hidden), BF16),
            jax.ShapeDtypeStruct((model, hidden), BF16),
            jax.ShapeDtypeStruct((model, hidden), BF16),
        ],
        scratch_shapes=[pltpu.VMEM((model, hidden), BF16)] * 3
        + [
            pltpu.VMEM((tokens, model), BF16),
            pltpu.VMEM((tokens, model), BF16),
            pltpu.VMEM((tokens, hidden), BF16),
            pltpu.VMEM((tokens, 2 * hidden), BF16),
            pltpu.VMEM((2, rows, model), F32),
            pltpu.VMEM((rows, model), BF16),
        ]
        + [pltpu.VMEM((2, rows, model), BF16)] * 2
        + [pltpu.VMEM((steps - 2, rows, model), BF16)] * 2
        + [pltpu.VMEM((2, rows, model), BF16)] * 2
        + [
            pltpu.VMEM((count, own, width), BF16),
            pltpu.VMEM((model // 2, hidden), BF16),
            sem((4,)), sem((2,)), sem((3,)),
            sem((2,)), sem((2,)), sem((steps - 2,)), sem((steps - 2,)),
            sem((2,)), sem((2,)), sem((count,)), sem((count,)), sem((shards,)), sem((shards,)),
            sem((1,)),
        ],
        compiler_params=pltpu.CompilerParams(
            vmem_limit_bytes=63 << 20, collective_id=2, has_side_effects=True
        ),
        cost_estimate=pl.CostEstimate(
            flops=2 * tokens * model * hidden * 9, bytes_accessed=280 << 20,
            transcendentals=tokens * hidden,
        ),
        name="feed_forward",
    )(n2, cotangent, middle, gain, others, weights, *blocks)


def shard_copy(src, dst, send, recv, axis, index):
    return pltpu.make_async_remote_copy(
        src_ref=src, dst_ref=dst, send_sem=send, recv_sem=recv, device_id={axis: index},
        device_id_type=MESH,
    )


def begin_kernel(
    shards, x_ref, qkv_ref, wo_ref, gains_ref, n_ref, qkv_full_ref, wo_full_ref, gain_out_ref,
    qkv_full, wo_full, normed, rows_in, gain_buf, zs, zr, xs, xr, gs, gr, own_sem, in_sem, out_sem,
):
    me, piece = lax.axis_index("fsdp"), lax.axis_index("ctx")
    fulls, sources = (qkv_full, wo_full), (qkv_ref, wo_ref)
    shard = qkv_ref.shape[0]
    half = shard // 2
    tokens = normed.shape[0]
    rows = rows_in.shape[1]
    steps = tokens // rows

    def read(i):
        return pltpu.make_async_copy(
            x_ref.at[pl.ds(i * rows, rows)], rows_in.at[i % 2], in_sem.at[i % 2]
        )

    read(0).start()
    keeps = [
        pltpu.make_async_copy(src, full.at[pl.ds(pl.multiple_of(me * shard, shard), shard)], own_sem.at[a])
        for a, (src, full) in enumerate(zip(sources, fulls))
    ]
    for copy in keeps:
        copy.start()
    keep_gain = pltpu.make_async_copy(gains_ref, gain_buf.at[me], own_sem.at[2])
    keep_gain.start()
    barrier = pltpu.get_barrier_semaphore()
    for k in range(1, shards):
        pl.semaphore_signal(
            barrier, inc=1, device_id={"fsdp": lax.rem(me + k, shards)}, device_id_type=MESH
        )
    pl.semaphore_signal(barrier, inc=1, device_id={"ctx": 1 - piece}, device_id_type=MESH)
    pl.semaphore_wait(barrier, shards)

    def place(a, s, which):
        return fulls[a].at[half_rows(s, which, half)]

    def own_half(a):
        return sources[a].at[pl.ds(pl.multiple_of(piece * half, half), half)]

    def along(a, s, step, mine):
        way = 0 if step > 0 else 1
        src = own_half(a) if mine else place(a, s, piece)
        return shard_copy(
            src, place(a, s, piece), zs.at[a, way, s], zr.at[a, s], "fsdp",
            lax.rem(me + step + shards, shards),
        )

    def across(a, s):
        return shard_copy(
            place(a, s, piece), place(a, s, piece), xs.at[a, s], xr.at[a, s], "ctx", 1 - piece
        )

    gain_copies = [
        shard_copy(
            gains_ref, gain_buf.at[me], gs.at[k], gr.at[k], "fsdp", lax.rem(me + k, shards)
        )
        for k in range(1, shards)
    ]
    for copy in gain_copies:
        copy.start()
    for a in range(2):
        for step, there in ((1, me < shards - 1), (-1, me > 0)):
            @pl.when(there)
            def _():
                along(a, me, step, True).start()

    for copy in gain_copies:
        copy.wait()
    keep_gain.wait()
    gain_out_ref[...] = jnp.concatenate([gain_buf[s] for s in range(shards)], axis=1)
    for i in range(steps):
        if i + 1 < steps:
            read(i + 1).start()
        read(i).wait()
        x = rows_in[i % 2]
        factor = lax.rsqrt(row_mean(x * x) + EPSILON)
        normed[i * rows : (i + 1) * rows, :] = (x * factor * gain_out_ref[0:1, :]).astype(BF16)
    write_normed = pltpu.make_async_copy(normed, n_ref, out_sem.at[0])
    write_normed.start()

    def arrival(d, step):
        s = me - step * d
        there = (s >= 0) & (s <= shards - 1)
        s = jnp.minimum(jnp.maximum(s, 0), shards - 1)
        onward = (me < shards - 1) if step > 0 else (me > 0)

        @pl.when(there)
        def _():
            for a in range(2):
                along(a, s, step, False).wait_recv()
                across(a, s).start()

        @pl.when(there & onward)
        def _():
            for a in range(2):
                along(a, s, step, False).start()

    for d in range(1, shards):
        arrival(d, 1)
        arrival(d, -1)
    for copy in keeps:
        copy.wait()
    for k in range(1, shards):
        s = lax.rem(me + k, shards)
        for a in range(2):
            across(a, s).wait_recv()
    writes = [
        pltpu.make_async_copy(qkv_full, qkv_full_ref, out_sem.at[1]),
        pltpu.make_async_copy(wo_full, wo_full_ref, out_sem.at[2]),
    ]
    for copy in writes:
        copy.start()
    for a in range(2):
        for s in range(shards):
            @pl.when((me >= s) & (me < shards - 1))
            def _():
                along(a, s, 1, False).wait_send()

            @pl.when((me <= s) & (me > 0))
            def _():
                along(a, s, -1, False).wait_send()

        for k in range(1, shards):
            across(a, lax.rem(me + k, shards)).wait_send()
    write_normed.wait()
    for copy in writes:
        copy.wait()


def begin(shards, x, qkv, wo, gains):
    tokens, model = x.shape
    rows = math.gcd(tokens, 256)
    vmem, hbm = pl.BlockSpec(memory_space=pltpu.VMEM), pl.BlockSpec(memory_space=pl.ANY)
    sem = pltpu.SemaphoreType.DMA
    return pl.pallas_call(
        functools.partial(begin_kernel, shards),
        in_specs=[hbm, vmem, vmem, vmem],
        out_specs=[hbm, hbm, hbm, vmem],
        out_shape=[
            jax.ShapeDtypeStruct((tokens, model), BF16),
            jax.ShapeDtypeStruct((model, qkv.shape[1]), BF16),
            jax.ShapeDtypeStruct((model, wo.shape[1]), BF16),
            jax.ShapeDtypeStruct((gains.shape[0], model), F32),
        ],
        scratch_shapes=[
            pltpu.VMEM((model, qkv.shape[1]), BF16),
            pltpu.VMEM((model, wo.shape[1]), BF16),
            pltpu.VMEM((tokens, model), BF16),
            pltpu.VMEM((2, rows, model), F32),
            pltpu.VMEM((shards,) + gains.shape, F32),
            sem((2, 2, shards)), sem((2, shards)), sem((2, shards)), sem((2, shards)),
            sem((shards,)), sem((shards,)), sem((3,)), sem((2,)), sem((3,)),
        ],
        compiler_params=pltpu.CompilerParams(
            vmem_limit_bytes=48 << 20, collective_id=4, has_side_effects=True
        ),
        cost_estimate=pl.CostEstimate(flops=0, bytes_accessed=120 << 20, transcendentals=0),
        name="norm_and_gather",
    )(x, qkv, wo, gains)


def project_kernel(
    q_heads, n_ref, qkv_ref, spread_ref, cos_ref, sin_ref, krow_ref, vrow_ref, q_ref, kv_ref, wide
):
    @pl.when(pl.program_id(0) == 0)
    def _():
        model = qkv_ref.shape[0]
        block = math.gcd(model, 512)
        for r in range(0, model, block):
            wide[r : r + block, :] = dot(qkv_ref[r : r + block, :], spread_ref[...]).astype(BF16)

    kv_heads = kv_ref.shape[1] // LANES // 2
    cos, sin = cos_ref[...], sin_ref[...]
    out = dot(n_ref[...], wide[...])
    for h in range(q_heads + 2 * kv_heads):
        part = out[:, h * LANES : (h + 1) * LANES]
        if h < q_heads + kv_heads:
            part = part * cos + pltpu.roll(part, LANES // 2, 1) * sin
        if h < q_heads:
            q_ref[:, h * LANES : (h + 1) * LANES] = part.astype(BF16)
        else:
            part = part + (krow_ref[...] if h < q_heads + kv_heads else vrow_ref[...])
            kv_ref[:, (h - q_heads) * LANES : (h - q_heads + 1) * LANES] = part.astype(BF16)


def project(normed, qkv, spread, cos, sin, krow, vrow, q_heads, kv_heads):
    tokens, model = normed.shape
    wide = spread.shape[1]
    bm = math.gcd(tokens, 256)
    whole = lambda a: pl.BlockSpec(a.shape, lambda i: (0, 0))
    row = lambda w: pl.BlockSpec((bm, w), lambda i: (i, 0))
    return pl.pallas_call(
        functools.partial(project_kernel, q_heads),
        grid=(tokens // bm,),
        in_specs=[row(model), whole(qkv), whole(spread), row(LANES), row(LANES), whole(krow), whole(vrow)],
        out_specs=[row(q_heads * LANES), row(2 * kv_heads * LANES)],
        out_shape=[
            jax.ShapeDtypeStruct((tokens, q_heads * LANES), BF16),
            jax.ShapeDtypeStruct((tokens, 2 * kv_heads * LANES), BF16),
        ],
        scratch_shapes=[pltpu.VMEM((model, wide), BF16)],
        compiler_params=pltpu.CompilerParams(vmem_limit_bytes=40 << 20),
        cost_estimate=pl.CostEstimate(
            flops=2 * tokens * model * wide, bytes_accessed=16 << 20, transcendentals=0
        ),
        name="project_qkv",
    )(normed, qkv, spread, cos, sin, krow, vrow)


def dense_kernel(
    chips, dq_ref, dkv_ref, after_ref, cos_ref, sin_ref, rotk_ref, valk_ref, att_ref, n_ref, *rest
):
    blocks, rest = rest[:chips], rest[chips:]
    dense_ref, grad_ref, normed, branch, send, recv, local = rest
    ranks = Ranks(2 * chips)
    fetch = pltpu.make_async_copy(n_ref, normed, local.at[chips])
    fetch.start()
    sem = pltpu.get_barrier_semaphore()
    pl.semaphore_signal(sem, inc=1, device_id={"tp": ranks.peer(0, 1)}, device_id_type=MESH)
    pl.semaphore_wait(sem, 1)
    copies = both_cores(ranks, blocks, branch, send, recv, local)
    for copy in copies:
        copy.start()
    width = dense_ref.shape[1]
    lanes = dkv_ref.shape[1] // 2
    cos, sin = cos_ref[...], sin_ref[...]
    turned = []
    for h in range(lanes // LANES):
        at = slice(h * LANES, (h + 1) * LANES)
        key = dkv_ref[:, at] + after_ref[:, at].astype(F32)
        turned.append((key * cos - pltpu.roll(key, LANES // 2, 1) * sin).astype(BF16))
    dk = dot(jnp.concatenate(turned, axis=1), rotk_ref[...]).astype(BF16)
    dv = (dkv_ref[:, lanes:] + after_ref[:, lanes:].astype(F32)).astype(BF16)
    dv = dot(dv, valk_ref[...]).astype(BF16)
    dense_ref[...] = jnp.concatenate([dq_ref[...], dk, dv], axis=1)
    fetch.wait()
    model = normed.shape[1]
    cols = math.gcd(model, 384)
    for d in range(0, model, cols):
        grad_ref[d : d + cols, :width] = dot(
            normed[:, d : d + cols], dense_ref[...], TN
        ).astype(BF16)
    for copy in copies:
        copy.wait()
    for d in range(0, model, cols):
        grad_ref[d : d + cols, width:] = dot(branch[:, d : d + cols], att_ref[...], TN).astype(BF16)


def dense_gradients(dq, dkv, after, cos, sin, rot_k, val_k, attended, normed, blocks):
    tokens, model = normed.shape
    chips = len(blocks)
    width = dq.shape[1] + 2 * rot_k.shape[1]
    total = width + attended.shape[1]
    vmem, hbm = pl.BlockSpec(memory_space=pltpu.VMEM), pl.BlockSpec(memory_space=pl.ANY)
    sem = pltpu.SemaphoreType.DMA
    return pl.pallas_call(
        functools.partial(dense_kernel, chips),
        in_specs=[vmem] * 8 + [hbm] * (1 + chips),
        out_specs=[vmem, vmem],
        out_shape=[
            jax.ShapeDtypeStruct((tokens, width), BF16),
            jax.ShapeDtypeStruct((model, total), BF16),
        ],
        scratch_shapes=[
            pltpu.VMEM((tokens, model), BF16),
            pltpu.VMEM((tokens, model), BF16),
            sem((chips,)), sem((chips,)), sem((chips + 1,)),
        ],
        compiler_params=pltpu.CompilerParams(
            vmem_limit_bytes=48 << 20, collective_id=5, has_side_effects=True
        ),
        cost_estimate=pl.CostEstimate(
            flops=2 * tokens * model * total, bytes_accessed=24 << 20, transcendentals=0
        ),
        name="dense_gradients",
    )(dq, dkv, after, cos, sin, rot_k, val_k, attended, normed, *blocks)


def close_kernel(
    count, shards, dense_ref, w_ref, x_ref, mg_ref, gain_ref, gain_two_ref, grad_ref, up_ref, gate_ref, *rest
):
    layers, rest = rest[: count // 2], rest[count // 2 :]
    (
        out_ref, gain_grad_ref, att_ref, lay_ref, up_out_ref, gate_out_ref, rows_in, rows_out, sums, c_send, c_recv, y_send,
        y_recv, x_mine, x_recv, up_mine, up_recv, gate_mine, gate_recv, l_own, l_send, l_recv, last_send,
        last_recv, t_send, t_recv, cs, cr, ys, yr, g_send, g_recv, xs, xr, x_sem,
        ls, lr, lay_sem, ts, tr, up_sem, gate_sem, lines, liner, last_sem, local,
    ) = rest
    ranks = Ranks(count)
    own = rows_in.shape[0]
    halves = 2
    rows = own // halves
    steps = ranks.chips * halves
    fetch = pltpu.make_async_copy(
        x_ref.at[pl.ds(pl.multiple_of(ranks.me * own, own), own)], rows_in, local.at[0]
    )
    fetch.start()
    def tile(at):
        return dot(dense_ref[pl.ds(at, rows), :], w_ref[...], NT)

    piece = lax.axis_index("ctx")
    half = grad_ref.shape[0] // (2 * shards)
    keeps = [
        pltpu.make_async_copy(
            grad_ref.at[half_rows(s, piece, half)], x_mine.at[pl.ds(s * half, half)], x_sem.at[s]
        )
        for s in range(shards)
    ]
    keeps.append(pltpu.make_async_copy(up_ref, up_mine, up_sem.at[0]))
    keeps.append(pltpu.make_async_copy(gate_ref, gate_mine, gate_sem.at[0]))
    for copy in keeps:
        copy.start()
    me = lax.axis_index("fsdp")
    barrier = pltpu.get_barrier_semaphore()
    for k, j in ranks.others():
        pl.semaphore_signal(barrier, inc=1, device_id={"tp": ranks.peer(k, j)}, device_id_type=MESH)
    for k in range(1, shards):
        pl.semaphore_signal(
            barrier, inc=1, device_id={"fsdp": lax.rem(me + k, shards)}, device_id_type=MESH
        )
    pl.semaphore_signal(barrier, inc=1, device_id={"ctx": 1 - piece}, device_id_type=MESH)
    pl.semaphore_wait(barrier, count + shards - 1)
    swaps = swap_halves(grad_ref, x_recv, xs, xr, shards)
    swaps.append(shard_copy(up_ref, up_recv, up_sem.at[1], up_sem.at[2], "ctx", 1 - piece))
    swaps.append(shard_copy(gate_ref, gate_recv, gate_sem.at[1], gate_sem.at[2], "ctx", 1 - piece))
    for copy in swaps:
        copy.start()
    forward = both_cores(ranks, layers, lay_ref, ls, lr, lay_sem)
    for copy in forward:
        copy.start()
    neighbour = ranks.peer(0, 1)

    def to_core(i):
        return remote(c_send.at[i], c_recv.at[i], cs.at[i], cr.at[i], neighbour)

    def to_chip(i, k):
        return remote(y_send.at[i], y_recv.at[i], ys.at[i], yr.at[i], ranks.peer(k, 0))

    def send_step(i, carry):
        k, u, at_mine, at_other = scatter_order(ranks, halves, own, i)
        c_send[i] = tile(at_other).astype(BF16)
        to_core(i).start()
        return carry

    def sum_step(i, carry):
        k, u, at_mine, at_other = scatter_order(ranks, halves, own, i)
        grad = tile(at_mine)
        to_core(i).wait_recv()
        grad = grad + c_recv[i].astype(F32)

        @pl.when(k != 0)
        def _():
            y_send[i] = grad.astype(BF16)
            to_chip(i, k).start()

        @pl.when(k == 0)
        def _():
            sums[u] = grad

        return carry

    lax.fori_loop(0, steps, send_step, 0)
    lax.fori_loop(0, steps, sum_step, 0)
    fetch.wait()
    gain = gain_ref[...]
    gain_total = None
    for u in range(halves):
        total = sums[u]
        for k in range(1, ranks.chips):
            i = (k - 1) * halves + u
            to_chip(i, k).wait_recv()
            total = total + y_recv[i].astype(F32)
        x = rows_in[u * rows : (u + 1) * rows]
        factor = lax.rsqrt(row_mean(x * x) + EPSILON)
        hat = x * factor
        term = jnp.sum(total * hat, axis=0, keepdims=True)
        gain_total = term if gain_total is None else gain_total + term
        inner = total * gain
        grad = mg_ref[u * rows : (u + 1) * rows] + factor * (inner - hat * row_mean(inner * hat))
        rows_out[u * rows : (u + 1) * rows] = grad.astype(BF16)
    gather = GatherRows(ranks, rows_out, out_ref, g_send, g_recv, local.at[0])
    gather.start()
    total = jnp.concatenate([gain_total, gain_two_ref[...], jnp.zeros((6, gain_total.shape[1]), F32)], axis=0)
    hops = [[{"tp": ranks.peer(0, 1)}], [{"tp": ranks.peer(k, 0)} for k in range(1, ranks.chips)]]
    hops += [[{"ctx": 1 - piece}], [{"fsdp": lax.rem(me + k, shards)} for k in range(1, shards)]]
    slot, sent = 0, []
    for n, peers in enumerate(hops):
        t_send[n] = total
        copies = []
        for peer in peers:
            copies.append(
                pltpu.make_async_remote_copy(
                    src_ref=t_send.at[n], dst_ref=t_recv.at[slot], send_sem=ts.at[slot],
                    recv_sem=tr.at[slot], device_id=peer, device_id_type=MESH,
                )
            )
            copies[-1].start()
            slot += 1
        for copy, at in zip(copies, range(slot - len(copies), slot)):
            copy.wait_recv()
            total = total + t_recv[at]
        sent += copies
    gain_grad_ref[...] = total
    for copy in sent:
        copy.wait_send()
    for s in range(shards):
        keeps[s].wait()
        swaps[s].wait_recv()
        here = slice(s * half, (s + 1) * half)
        l_own[s] = x_mine[here, :].astype(F32) + x_recv[here, :].astype(F32)

    def line(way, s, step):
        return shard_copy(
            l_send.at[way, s], l_recv.at[way, s], lines.at[way, s], liner.at[way, s], "fsdp",
            lax.rem(me + step + shards, shards),
        )

    def toward(way, s, step, there, follows):
        @pl.when(there & follows)
        def _():
            line(way, s, step).wait_recv()
            l_send[way, s] = (l_own[s] + l_recv[way, s].astype(F32)).astype(BF16)
            line(way, s, step).start()

        @pl.when(there & jnp.logical_not(follows))
        def _():
            l_send[way, s] = l_own[s].astype(BF16)
            line(way, s, step).start()

    for d in range(shards - 1):
        toward(0, shards - 1 - d, 1, me < shards - 1 - d, me > 0)
        toward(1, d, -1, me > d, me < shards - 1)
    gather.finish()
    for copy in forward:
        copy.wait()
    for s in range(shards):
        @pl.when(me == s)
        def _():
            if s > 0:
                line(0, s, 1).wait_recv()
                l_own[s] += l_recv[0, s].astype(F32)
            if s < shards - 1:
                line(1, s, -1).wait_recv()
                l_own[s] += l_recv[1, s].astype(F32)
            last_send[...] = l_own[s].astype(BF16)

    last = shard_copy(last_send, last_recv, last_sem.at[0], last_sem.at[1], "ctx", 1 - piece)
    last.start()
    keeps[shards].wait()
    swaps[shards].wait_recv()
    up_out_ref[...] = up_mine[...].astype(F32) + up_recv[...].astype(F32)
    keeps[shards + 1].wait()
    swaps[shards + 1].wait_recv()
    last.wait_recv()
    for n, (dst, pair) in enumerate(((gate_out_ref, (gate_mine, gate_recv)), (att_ref, (last_send, last_recv)))):
        rows_half = pair[0].shape[0]

        @pl.when(piece == 0)
        def _():
            dst[:rows_half, :] = pair[0][...].astype(F32)
            dst[rows_half:, :] = pair[1][...].astype(F32)

        @pl.when(piece == 1)
        def _():
            dst[:rows_half, :] = pair[1][...].astype(F32)
            dst[rows_half:, :] = pair[0][...].astype(F32)

    for d in range(shards - 1):
        @pl.when(me < shards - 1 - d)
        def _():
            line(0, shards - 1 - d, 1).wait_send()

        @pl.when(me > d)
        def _():
            line(1, d, -1).wait_send()

    last.wait_send()
    for copy in swaps:
        copy.wait_send()
    for i in range(steps):
        to_core(i).wait_send()
    for i in range(steps - halves):
        to_chip(i, i // halves + 1).wait_send()


def close(count, shards, dense, weight, layer_input, middle_grad, gain, gain_two, grad, up, gate, layers):
    tokens, model = layer_input.shape
    own = tokens // count
    rows, steps, chips = own // 2, count, count // 2
    vmem, hbm = pl.BlockSpec(memory_space=pltpu.VMEM), pl.BlockSpec(memory_space=pl.ANY)
    sem = pltpu.SemaphoreType.DMA
    return pl.pallas_call(
        functools.partial(close_kernel, count, shards),
        in_specs=[vmem, vmem, hbm, vmem, vmem, vmem, hbm, hbm, hbm] + [hbm] * chips,
        out_specs=[hbm, vmem, vmem, hbm, vmem, vmem],
        out_shape=[
            jax.ShapeDtypeStruct((tokens, model), BF16),
            jax.ShapeDtypeStruct((8, model), F32),
            jax.ShapeDtypeStruct((model // shards, grad.shape[1]), F32),
            jax.ShapeDtypeStruct((tokens, model), BF16),
            jax.ShapeDtypeStruct(up.shape, F32),
            jax.ShapeDtypeStruct(up.shape, F32),
        ],
        scratch_shapes=[
            pltpu.VMEM((own, model), F32),
            pltpu.VMEM((own, model), BF16),
            pltpu.VMEM((2, rows, model), F32),
        ]
        + [pltpu.VMEM((steps, rows, model), BF16)] * 2
        + [pltpu.VMEM((steps - 2, rows, model), BF16)] * 2
        + [pltpu.VMEM((model // 2, grad.shape[1]), BF16)] * 2
        + [
            pltpu.VMEM(up.shape, BF16),
            pltpu.VMEM(up.shape, BF16),
            pltpu.VMEM(gate.shape, BF16),
            pltpu.VMEM(gate.shape, BF16),
            pltpu.VMEM((shards, gate.shape[0], grad.shape[1]), F32),
            pltpu.VMEM((2, shards, gate.shape[0], grad.shape[1]), BF16),
            pltpu.VMEM((2, shards, gate.shape[0], grad.shape[1]), BF16),
            pltpu.VMEM((gate.shape[0], grad.shape[1]), BF16),
            pltpu.VMEM((gate.shape[0], grad.shape[1]), BF16),
            pltpu.VMEM((4, 8, model), F32),
            pltpu.VMEM((chips + shards, 8, model), F32),
            sem((steps,)), sem((steps,)), sem((steps - 2,)), sem((steps - 2,)),
            sem((2, chips)), sem((2, chips)), sem((shards,)), sem((shards,)), sem((shards,)),
            sem((chips,)), sem((chips,)), sem((chips,)), sem((chips + shards,)),
            sem((chips + shards,)), sem((3,)), sem((3,)), sem((2, shards)), sem((2, shards)), sem((2,)),
            sem((2,)),
        ],
        compiler_params=pltpu.CompilerParams(
            vmem_limit_bytes=48 << 20, collective_id=3, has_side_effects=True
        ),
        cost_estimate=pl.CostEstimate(
            flops=2 * tokens * model * dense.shape[1], bytes_accessed=200 << 20, transcendentals=0
        ),
        name="close_layer",
    )(dense, weight, layer_input, middle_grad, gain, gain_two, grad, up, gate, *layers)


def per_device(
    sizes,
    layer_input,
    doc_lengths,
    attention_gain,
    query_weight,
    key_matrix,
    value_matrix,
    output_weight,
    feedforward_gain,
    gate_weight,
    up_weight,
    down_weight,
    output_cotangent,
):
    shards, pieces, ranks = sizes
    assert pieces == 2 and ranks % 2 == 0
    chips = ranks // 2
    tokens, model = layer_input.shape
    own = tokens // ranks
    head_dim = HEAD_SIZE
    q_heads = query_weight.shape[1] // head_dim
    kv_heads = key_matrix.shape[1] // head_dim
    q_width, kv_width = q_heads * head_dim, kv_heads * head_dim
    piece = lax.axis_index("ctx")
    rank = lax.axis_index("tp")
    chip, core = rank // 2, rank % 2
    me = lax.axis_index("fsdp")
    scale = 1.0 / math.sqrt(head_dim)

    swap_x = [(0, 1), (1, 0)]
    swap_core = [(i, i ^ 1) for i in range(ranks)]

    def chip_shift(k):
        return [(i, (i + 2 * k) % ranks) for i in range(ranks)]

    def shard_shift(k):
        return [(i, (i + k) % shards) for i in range(shards)]

    def pick(array, index, axis=0):
        return lax.dynamic_index_in_dim(array, index, axis, keepdims=False)

    def half_of(shard):
        rows = shard.shape[0] // 2
        return lax.dynamic_slice_in_dim(shard, piece * rows, rows, 0)

    both_axes = ("fsdp", "ctx")

    def reduce_fsdp(part):
        return lax.psum_scatter(part, "fsdp", scatter_dimension=0, tiled=True)

    def add_pieces(mine):
        return mine.astype(F32) + lax.ppermute(mine, "ctx", swap_x).astype(F32)

    ff_half = half_of(jnp.concatenate([gate_weight, up_weight, down_weight.T], axis=1))
    gain_shard = jnp.stack([attention_gain, feedforward_gain]).astype(F32)
    gain_shard = jnp.pad(gain_shard, ((0, 6), (0, 0)))
    qkv_shard = jnp.concatenate([query_weight, key_matrix, value_matrix], axis=1)
    positions = doc_positions(doc_lengths[0], piece * tokens, tokens)
    cos, sin = rotary_lanes(positions, head_dim)
    lane = lax.broadcasted_iota(jnp.int32, (1, LANES), 1)
    krow = jnp.where((lane >= head_dim // 2) & (lane < head_dim // 2 + 3), -1.0, 0.0)
    vrow = jnp.where((lane >= head_dim) & (lane < head_dim + 3), 1.0, 0.0)
    spread = jnp.zeros((q_width + 2 * kv_width, (q_heads + 2 * kv_heads) * LANES), BF16)
    rot_q, rot_k = select_rotary(q_heads, head_dim), select_rotary(kv_heads, head_dim)
    val_q, val_k = select_value(q_heads, head_dim), select_value(kv_heads, head_dim)
    spread = spread.at[:q_width, : q_heads * LANES].set(rot_q.T)
    spread = spread.at[q_width : q_width + kv_width, q_heads * LANES : (q_heads + kv_heads) * LANES].set(rot_k.T)
    spread = spread.at[q_width + kv_width :, (q_heads + kv_heads) * LANES :].set(val_k.T)

    normed_one, qkv_full, out_own, gains_full = begin(
        shards, layer_input, qkv_shard, output_weight.T, gain_shard
    )
    queries, keys_values = project(
        normed_one, qkv_full, spread, cos, sin, krow, vrow, q_heads, kv_heads
    )
    ff_half, gains_full = lax.optimization_barrier((ff_half, gains_full))
    ff_full = lax.all_gather(ff_half, both_axes, axis=0, tiled=True)
    gain_one, gain_two = gains_full[0:1], gains_full[1:2]
    before = lax.ppermute(keys_values, "ctx", [(0, 1)])
    base = -(piece - 1) * tokens
    ends = jnp.cumsum(doc_lengths[0]).astype(jnp.int32) + base
    base = base.astype(jnp.int32).reshape(1)
    state = attention_forward(ends, base, queries, keys_values, head_dim, tokens)
    attended, marked = attention_forward(
        ends, base, queries, before, head_dim, 0, state, val_q
    )
    wo = [out_own] + [lax.ppermute(out_own, "tp", chip_shift(k)) for k in range(1, chips)]
    normed_two, middle, wo_others = mix(ranks, attended, layer_input, gain_two, wo)
    (
        feed_sums, middle_grad, branch_grad, gain_two_grad, attended_grad, gate_half, up_part, down_part,
    ) = feedforward(
        ranks, shards, normed_two, output_cotangent, middle, gain_two, ff_full, wo, wo_others
    )
    gate_own = reduce_fsdp(gate_half)
    up_own = reduce_fsdp(up_part)
    down_own = reduce_fsdp(down_part)
    cut = feed_sums.reshape(chips, own, model)
    feed_sums = [lax.ppermute(cut[k - 1], "tp", chip_shift(k)) for k in range(1, chips)]
    dq_part, dkv_before = attention_backward(
        ends, base, marked, attended_grad, attended, before, val_q.T, head_dim, 0
    )
    after = lax.ppermute(dkv_before, "ctx", [(1, 0)])
    dq, dkv = attention_backward(
        ends, base, marked, attended_grad, attended, keys_values, val_q.T, head_dim, tokens,
        (dq_part, cos, sin, rot_q),
    )

    feed_sums, dq = lax.optimization_barrier((feed_sums, dq))
    layer_rows = middle + cut[chips - 1].astype(F32)
    for block in feed_sums:
        layer_rows = layer_rows + block.astype(F32)
    layer_rows = layer_rows.astype(BF16)

    def from_chips(rows):
        return [rows] + [lax.ppermute(rows, "tp", chip_shift(k)) for k in range(1, chips)]

    dqkv, attention_part = dense_gradients(
        dq, dkv, after, cos, sin, rot_k, val_k, attended, normed_one, from_chips(branch_grad)
    )
    input_gradient, gains, attention, layer_output, up, gate = close(
        ranks, shards, dqkv, qkv_full, layer_input, middle_grad, gain_one, gain_two_grad,
        attention_part, up_own, gate_own, from_chips(layer_rows),
    )
    down_own, gains = lax.optimization_barrier((down_own, gains))
    down = add_pieces(down_own)
    layer_output, input_gradient = layer_output.astype(F32), input_gradient.astype(F32)
    gains = lax.dynamic_slice_in_dim(gains, me * gain_shard.shape[1], gain_shard.shape[1], 1)

    return (
        layer_output,
        input_gradient,
        gains[0],
        attention[:, :q_width],
        attention[:, q_width : q_width + kv_width],
        attention[:, q_width + kv_width : q_width + 2 * kv_width],
        attention[:, q_width + 2 * kv_width :].T,
        gains[1],
        gate,
        up,
        down.T,
    )


def solution(mesh):
    rows = P(("fsdp", "ctx"), None)
    into, out_of = P("fsdp", "tp"), P("tp", "fsdp")
    sizes = (mesh.shape["fsdp"], mesh.shape["ctx"], mesh.shape["tp"])
    return jax.shard_map(
        functools.partial(per_device, sizes),
        mesh=mesh,
        in_specs=(
            rows, P("fsdp", None), P("fsdp"), into, into, into, out_of, P("fsdp"), into, into,
            out_of, rows,
        ),
        out_specs=(
            rows, rows, P("fsdp"), into, into, into, out_of, P("fsdp"), into, into, out_of,
        ),
        check_vma=False,
    )
```

```python
import functools
import math

import jax
import jax.numpy as jnp
import ml_dtypes
import numpy as np
from jax import lax
from jax.experimental import pallas as pl
from jax.experimental.pallas import tpu as pltpu
from jax.sharding import PartitionSpec as P

HEAD_SIZE = 96
EPSILON = 1e-05
THETA = 100000.0
NEGATIVE = -1e30
LOG2E = 1.4426950408889634
LANES = 128
F32 = jnp.float32
BF16 = jnp.bfloat16
NN = (((1,), (0,)), ((), ()))
NT = (((1,), (1,)), ((), ()))
TN = (((0,), (0,)), ((), ()))


def dot(left, right, dims=NN):
    return lax.dot_general(left, right, dims, preferred_element_type=F32)


def select_rotary(heads, head_dim):
    col = np.arange(heads * head_dim)
    half = head_dim // 2
    within = col % head_dim
    lane = np.where(within < half, within, within - half + LANES // 2)
    return select_lanes(heads, (col // head_dim) * LANES + lane)


def select_value(heads, head_dim):
    col = np.arange(heads * head_dim)
    return select_lanes(heads, (col // head_dim) * LANES + col % head_dim)


def select_lanes(heads, want):
    return (np.arange(heads * LANES)[:, None] == want[None, :]).astype(ml_dtypes.bfloat16)


def rotary_lanes(positions, head_dim):
    half = head_dim // 2
    freqs = THETA ** (-(jnp.arange(half, dtype=F32) * 2.0 / head_dim))
    angles = positions.astype(F32)[:, None] * freqs[None, :]
    cos, sin = jnp.cos(angles), jnp.sin(angles)
    pad = jnp.zeros((positions.shape[0], LANES // 2 - half), F32)
    return (
        jnp.concatenate([cos, pad, cos, pad], axis=1),
        jnp.concatenate([-sin, pad, sin, pad], axis=1),
    )


def doc_positions(lengths, first, count):
    ends = jnp.cumsum(lengths)
    starts = ends - lengths
    index = first + jnp.arange(count, dtype=jnp.int32)
    document = jnp.sum((index[None, :] >= ends[:, None]).astype(jnp.int32), axis=0)
    chosen = document[None, :] == jnp.arange(lengths.shape[0], dtype=jnp.int32)[:, None]
    start_of = jnp.sum(jnp.where(chosen, starts[:, None], 0), axis=0)
    return index - start_of


def doc_start(ends_ref, base, rows):
    start = base if jnp.ndim(rows) == 0 else jnp.zeros_like(rows) + base
    for j in range(ends_ref.shape[0]):
        end = ends_ref[j]
        start = jnp.where(rows >= end, jnp.maximum(start, end), start)
    return start


def put_lanes(rows, column, lane):
    at = lax.broadcasted_iota(jnp.int32, rows.shape, 1)
    high = column.astype(BF16).astype(F32)
    rest = column - high
    mid = rest.astype(BF16).astype(F32)
    low = rest - mid
    wide = rows.astype(F32)
    wide = jnp.where(at == lane, high, wide)
    wide = jnp.where(at == lane + 1, mid, wide)
    return jnp.where(at == lane + 2, low, wide).astype(BF16)


def block_ranges(first_row, rows, block, low, last_low, key_base, key_count):
    begin = (jnp.maximum(low, key_base) - key_base) // block
    stop = jnp.minimum((first_row + rows - key_base + block - 1) // block, key_count // block)
    inner = jnp.minimum(jnp.maximum((last_low - key_base + block - 1) // block, begin), stop)
    diagonal = jnp.minimum(jnp.maximum((first_row - key_base) // block, inner), stop)
    return begin, inner, diagonal, stop


def stack_heads(ref, kv, group):
    parts = [ref[:, (kv * group + g) * LANES : (kv * group + g + 1) * LANES] for g in range(group)]
    return jnp.concatenate(parts, axis=0)


def row_marks(ends_ref, base, first_row, bq, group):
    rows = lax.broadcasted_iota(jnp.int32, (1, bq), 1) + first_row
    starts = doc_start(ends_ref, base, rows)
    return jnp.concatenate([rows] * group, axis=1), jnp.concatenate([starts] * group, axis=1)


def widen(dense_ref, spread_ref, mark_ref, wide_ref):
    @pl.when(pl.program_id(0) == 0)
    def _():
        wide = dot(dense_ref[...], spread_ref[...]) + mark_ref[...]
        wide_ref[...] = wide.astype(BF16)

    return wide_ref


def attention_forward_kernel(
    first, key_base, tokens, bq, bk, head_dim, group, ends_ref, base_ref, q_ref, kv_ref, *rest
):
    if first:
        max_ref, acc_ref = rest
    else:
        spread_ref, mark_ref, sel_ref, max_in, acc_in, o_ref, qa_ref, max_ref, acc_ref, wide = rest
        kv_ref = widen(kv_ref, spread_ref, mark_ref, wide)
    first_row = tokens + pl.program_id(0) * bq
    base = base_ref[0]
    low = doc_start(ends_ref, base, first_row)
    last_low = doc_start(ends_ref, base, first_row + bq - 1)
    rows, starts = row_marks(ends_ref, base, first_row, bq, group)
    kv_heads = kv_ref.shape[1] // LANES // 2
    unit = LOG2E / math.sqrt(head_dim)
    queries = [stack_heads(q_ref, h, group) for h in range(kv_heads)]
    if first:
        max_ref[...] = jnp.full(max_ref.shape, NEGATIVE, F32)
        acc_ref[...] = jnp.zeros(acc_ref.shape, F32)
    else:
        max_ref[...] = max_in[...]
        acc_ref[...] = acc_in[...]

    def body(masked, index, carry):
        at = pl.multiple_of(index * bk, bk)
        if masked:
            keys = lax.broadcasted_iota(jnp.int32, (bk, group * bq), 0) + (at + key_base)
            keep = (keys <= rows) & (keys >= starts)
        for h in range(kv_heads):
            key = kv_ref[pl.ds(at, bk), h * LANES : (h + 1) * LANES]
            value = kv_ref[pl.ds(at, bk), (kv_heads + h) * LANES : (kv_heads + h + 1) * LANES]
            scores = dot(key, queries[h], NT)
            if masked:
                scores = jnp.where(keep, scores, NEGATIVE)
            old = max_ref[0, h]
            new = jnp.maximum(old, jnp.max(scores, axis=0, keepdims=True))
            probs = jnp.exp2((scores - new) * unit)
            if masked:
                probs = jnp.where(keep, probs, 0.0)
            acc_ref[0, h] = acc_ref[0, h] * jnp.exp2((old - new) * unit) + dot(
                value, probs.astype(BF16), TN
            )
            max_ref[0, h] = new
        return carry

    begin, inner, diagonal, stop = block_ranges(
        first_row, bq, bk, low, last_low, key_base, kv_ref.shape[0]
    )
    lax.fori_loop(begin, inner, functools.partial(body, True), 0)
    lax.fori_loop(inner, diagonal, functools.partial(body, False), 0)
    lax.fori_loop(diagonal, stop, functools.partial(body, True), 0)
    if first:
        return
    outs = []
    for h in range(kv_heads):
        acc = acc_ref[0, h]
        total = acc[head_dim : head_dim + 1, :]
        out = jnp.transpose(acc * (1.0 / total)).astype(BF16)
        logsum = jnp.broadcast_to(max_ref[0, h] + jnp.log2(total) * (1.0 / unit), (8, group * bq))
        marked = put_lanes(queries[h], jnp.transpose(logsum)[:, :1], head_dim // 2)
        for g in range(group):
            head = h * group + g
            qa_ref[:, head * LANES : (head + 1) * LANES] = marked[g * bq : (g + 1) * bq]
            outs.append(out[g * bq : (g + 1) * bq])
    o_ref[...] = dot(jnp.concatenate(outs, axis=1), sel_ref[...]).astype(BF16)


def attention_forward(ends, base, q, kv, head_dim, key_base, state=None, extra=None):
    tokens, width = q.shape
    kv_heads = (kv if state is None else extra[0]).shape[1] // LANES // 2
    group = width // LANES // kv_heads
    bq = bk = math.gcd(tokens, 512)
    steps = tokens // bq
    whole = lambda a: pl.BlockSpec(a.shape, lambda i, *_: (0, 0))
    row = lambda w: pl.BlockSpec((bq, w), lambda i, *_: (i, 0))
    shapes = [(steps, kv_heads, 1, group * bq), (steps, kv_heads, LANES, group * bq)]
    kept = [pl.BlockSpec((1,) + a[1:], lambda i, *_: (i, 0, 0, 0)) for a in shapes]
    pairs = tokens * tokens * group * kv_heads // 2
    if state is None:
        in_specs, operands = [row(width), whole(kv)], (q, kv)
        out_specs, out_shape = kept, [jax.ShapeDtypeStruct(a, F32) for a in shapes]
        scratch = []
    else:
        select = extra[2]
        in_specs = [row(width), whole(kv)] + [whole(a) for a in extra] + kept
        operands = (q, kv) + tuple(extra) + tuple(state)
        out_specs = [row(select.shape[1]), row(width)]
        out_shape = [
            jax.ShapeDtypeStruct((tokens, select.shape[1]), BF16),
            jax.ShapeDtypeStruct(q.shape, BF16),
        ]
        scratch = [pltpu.VMEM((1,) + a[1:], F32) for a in shapes]
        scratch.append(pltpu.VMEM((tokens, extra[0].shape[1]), BF16))
    return pl.pallas_call(
        functools.partial(
            attention_forward_kernel, state is None, key_base, tokens, bq, bk, head_dim, group
        ),
        grid_spec=pltpu.PrefetchScalarGridSpec(
            num_scalar_prefetch=2, grid=(steps,), in_specs=in_specs, out_specs=out_specs,
            scratch_shapes=scratch,
        ),
        out_shape=out_shape,
        compiler_params=pltpu.CompilerParams(vmem_limit_bytes=40 << 20),
        cost_estimate=pl.CostEstimate(
            flops=pairs * 1024, bytes_accessed=8 << 20, transcendentals=pairs
        ),
        name="attention_forward",
    )(ends, base, *operands)


def attention_backward_kernel(
    first, key_base, tokens, bq, bk, head_dim, group,
    ends_ref, base_ref, qa_ref, do_ref, o_ref, kv_ref, spread_ref, *rest
):
    if first:
        widen_ref, mark_ref, dq_ref, dkv_ref, dk_acc, dv_acc, dq_acc, wide = rest
        kv_ref = widen(kv_ref, widen_ref, mark_ref, wide)
    else:
        part_ref, cos_ref, sin_ref, sel_ref, dq_ref, dkv_ref, dk_acc, dv_acc, dq_acc = rest
    step = pl.program_id(0)
    first_row = tokens + step * bq
    base = base_ref[0]
    low = doc_start(ends_ref, base, first_row)
    last_low = doc_start(ends_ref, base, first_row + bq - 1)
    kv_heads = kv_ref.shape[1] // LANES // 2
    scale = 1.0 / math.sqrt(head_dim)
    unit = LOG2E * scale
    begin, inner, diagonal, stop = block_ranges(
        first_row, bq, bk, low, last_low, key_base, kv_ref.shape[0]
    )

    @pl.when(step == 0)
    def _():
        dk_acc[...] = jnp.zeros(dk_acc.shape, F32)
        dv_acc[...] = jnp.zeros(dv_acc.shape, F32)

    if first:
        dq_acc[...] = jnp.zeros(dq_acc.shape, F32)
    else:
        for h in range(kv_heads):
            dq_acc[h] = stack_heads(part_ref, h, group)

    @pl.when(begin < stop)
    def _():
        rows, starts = row_marks(ends_ref, base, first_row, bq, group)
        grads_wide = dot(do_ref[...], spread_ref[...])
        outs_wide = dot(o_ref[...], spread_ref[...])
        queries, grads = [], []
        for h in range(kv_heads):
            queries.append(stack_heads(qa_ref, h, group))
            grad = stack_heads(grads_wide, h, group)
            inner_sum = jnp.sum(grad * stack_heads(outs_wide, h, group), axis=1, keepdims=True)
            grads.append(put_lanes(grad, -inner_sum, head_dim))

        def body(masked, index, carry):
            at = pl.multiple_of(index * bk, bk)
            if masked:
                keys = lax.broadcasted_iota(jnp.int32, (bk, group * bq), 0) + (at + key_base)
                keep = (keys <= rows) & (keys >= starts)
            for h in range(kv_heads):
                key = kv_ref[pl.ds(at, bk), h * LANES : (h + 1) * LANES]
                value = kv_ref[pl.ds(at, bk), (kv_heads + h) * LANES : (kv_heads + h + 1) * LANES]
                probs = jnp.exp2(dot(key, queries[h], NT) * unit)
                if masked:
                    probs = jnp.where(keep, probs, 0.0)
                slope = (probs * dot(value, grads[h], NT)).astype(BF16)
                dv_acc[h, pl.ds(at, bk), :] += dot(probs.astype(BF16), grads[h])
                dk_acc[h, pl.ds(at, bk), :] += dot(slope, queries[h])
                dq_acc[h] += dot(slope, key, TN)
            return carry

        lax.fori_loop(begin, inner, functools.partial(body, True), 0)
        lax.fori_loop(inner, diagonal, functools.partial(body, False), 0)
        lax.fori_loop(diagonal, stop, functools.partial(body, True), 0)

    outs = []
    for h in range(kv_heads):
        for g in range(group):
            grad = dq_acc[h, g * bq : (g + 1) * bq, :]
            if first:
                dq_ref[:, (h * group + g) * LANES : (h * group + g + 1) * LANES] = grad
            else:
                grad = grad * scale
                outs.append(
                    (grad * cos_ref[...] - pltpu.roll(grad, LANES // 2, 1) * sin_ref[...]).astype(BF16)
                )
    if not first:
        dq_ref[...] = dot(jnp.concatenate(outs, axis=1), sel_ref[...]).astype(BF16)

    @pl.when(step == pl.num_programs(0) - 1)
    def _():
        for h in range(kv_heads):
            dkv_ref[:, h * LANES : (h + 1) * LANES] = (dk_acc[h] * scale).astype(dkv_ref.dtype)
            dkv_ref[:, (kv_heads + h) * LANES : (kv_heads + h + 1) * LANES] = dv_acc[h].astype(dkv_ref.dtype)


def attention_backward(ends, base, qa, grad, out, kv, spread, head_dim, key_base, rest=None, extra=None):
    tokens, width = qa.shape
    keys = kv.shape[0]
    kv_lanes = (kv if rest is not None else extra[0]).shape[1]
    kv_heads = kv_lanes // LANES // 2
    group = width // LANES // kv_heads
    bq = bk = math.gcd(tokens, 512)
    whole = lambda a: pl.BlockSpec(a.shape, lambda i, *_: (0, 0))
    row = lambda w: pl.BlockSpec((bq, w), lambda i, *_: (i, 0))
    pairs = tokens * tokens * group * kv_heads // 2
    in_specs = [row(width), row(grad.shape[1]), row(out.shape[1]), whole(kv), whole(spread)]
    operands = (qa, grad, out, kv, spread)
    scratch = []
    if rest is None:
        in_specs += [whole(a) for a in extra]
        operands += tuple(extra)
        scratch = [pltpu.VMEM((keys, kv_lanes), BF16)]
        dq_width, dq_type, dkv_type = width, F32, BF16
    else:
        part, cos, sin, select = rest
        in_specs += [row(width), row(LANES), row(LANES), whole(select)]
        operands += (part, cos, sin, select)
        dq_width, dq_type, dkv_type = select.shape[1], BF16, F32
    return pl.pallas_call(
        functools.partial(
            attention_backward_kernel, rest is None, key_base, tokens, bq, bk, head_dim, group
        ),
        grid_spec=pltpu.PrefetchScalarGridSpec(
            num_scalar_prefetch=2,
            grid=(tokens // bq,),
            in_specs=in_specs,
            out_specs=[row(dq_width), pl.BlockSpec((keys, kv_lanes), lambda i, *_: (0, 0))],
            scratch_shapes=[
                pltpu.VMEM((kv_heads, keys, LANES), F32),
                pltpu.VMEM((kv_heads, keys, LANES), F32),
                pltpu.VMEM((kv_heads, group * bq, LANES), F32),
            ]
            + scratch,
        ),
        out_shape=[
            jax.ShapeDtypeStruct((tokens, dq_width), dq_type),
            jax.ShapeDtypeStruct((keys, kv_lanes), dkv_type),
        ],
        compiler_params=pltpu.CompilerParams(vmem_limit_bytes=48 << 20),
        cost_estimate=pl.CostEstimate(
            flops=pairs * 2560, bytes_accessed=12 << 20, transcendentals=pairs
        ),
        name="attention_backward",
    )(ends, base, qa, grad, out, kv, spread, *operands[5:])


MESH = pl.DeviceIdType.MESH


class Ranks:
    def __init__(self, count):
        self.count, self.chips = count, count // 2
        self.me = lax.axis_index("tp")
        self.chip, self.core = self.me // 2, self.me % 2

    def peer(self, k, j):
        return lax.rem(self.chip + k + self.chips, self.chips) * 2 + lax.rem(self.core + j, 2)

    def others(self):
        return [(k, j) for k in range(self.chips) for j in range(2) if k or j]

    def barrier(self):
        sem = pltpu.get_barrier_semaphore()
        for k, j in self.others():
            pl.semaphore_signal(sem, inc=1, device_id={"tp": self.peer(k, j)}, device_id_type=MESH)
        pl.semaphore_wait(sem, self.count - 1)


def remote(src, dst, send, recv, rank):
    return pltpu.make_async_remote_copy(
        src_ref=src, dst_ref=dst, send_sem=send, recv_sem=recv, device_id={"tp": rank},
        device_id_type=MESH,
    )


def row_mean(x):
    return jnp.sum(x, axis=-1, keepdims=True) * (1.0 / x.shape[-1])


class GatherRows:
    def __init__(self, ranks, rows_ref, out_ref, send, recv, local):
        own = rows_ref.shape[0]
        self.ranks, self.send, self.recv = ranks, send, recv
        self.at = lambda rank: out_ref.at[pl.ds(pl.multiple_of(rank * own, own), own)]
        self.keep = pltpu.make_async_copy(rows_ref, self.at(ranks.me), local)
        self.copies = []
        for k in list(range(1, ranks.chips)) + [0]:
            peer = ranks.peer(k, 0) if k else ranks.peer(0, 1)
            self.copies.append(remote(rows_ref, self.at(ranks.me), send.at[0, k], recv.at[0, k], peer))

    def start(self):
        for copy in self.copies:
            copy.start()
        self.keep.start()

    def finish(self):
        ranks, passed = self.ranks, []
        for k, copy in zip(range(1, ranks.chips), self.copies):
            copy.wait_recv()
            held = self.at(ranks.peer(-k, 0))
            passed.append(
                remote(held, held, self.send.at[1, k], self.recv.at[1, k], ranks.peer(0, 1))
            )
            passed[-1].start()
        self.copies[-1].wait_recv()
        for copy in self.copies:
            copy.wait_send()
        for copy in passed:
            copy.wait()
        self.keep.wait()


def both_cores(ranks, blocks, out_ref, send, recv, local):
    own = blocks[0].shape[0]
    copies = []
    for k, block in enumerate(blocks):
        there = out_ref.at[pl.ds(pl.multiple_of(ranks.peer(-k, 0) * own, own), own)]
        copies.append(remote(block, there, send.at[k], recv.at[k], ranks.peer(0, 1)))
        copies.append(pltpu.make_async_copy(block, there, local.at[k]))
    return copies


def mix_kernel(count, shards, att_ref, x_ref, gain_ref, z_ref, *rest):
    chips = count // 2
    blocks, rest = rest[:chips], rest[chips:]
    (
        n2_ref, mid_ref, other_ref, z_full_ref, heads, rows_in, rows_out, others, a_send, a_recv,
        b_send, b_recv, g_send, g_recv, z_send, z_recv, x_send, x_recv, local,
    ) = rest
    ranks = Ranks(count)
    own = rows_in.shape[0]
    mine_at = pl.ds(pl.multiple_of(ranks.me * own, own), own)
    fetch = pltpu.make_async_copy(x_ref.at[mine_at], rows_in, local.at[0])
    fetch.start()
    mine = pltpu.make_async_copy(att_ref.at[mine_at], heads.at[0], local.at[1])
    mine.start()
    me = lax.axis_index("fsdp")
    barrier = pltpu.get_barrier_semaphore()
    for k, j in ranks.others():
        pl.semaphore_signal(barrier, inc=1, device_id={"tp": ranks.peer(k, j)}, device_id_type=MESH)
    for k in range(1, shards):
        pl.semaphore_signal(
            barrier, inc=1, device_id={"fsdp": lax.rem(me + k, shards)}, device_id_type=MESH
        )
    piece = lax.axis_index("ctx")
    pl.semaphore_signal(barrier, inc=1, device_id={"ctx": 1 - piece}, device_id_type=MESH)
    pl.semaphore_wait(barrier, count + shards - 1)
    shard = z_ref.shape[0]
    half = shard // 2
    place = lambda s: z_full_ref.at[half_rows(s, piece, half)]

    def along(s, step, own_block):
        way = 0 if step > 0 else 1
        src = z_ref.at[pl.ds(pl.multiple_of(piece * half, half), half)] if own_block else place(s)
        return shard_copy(
            src, place(s), z_send.at[way, s], z_recv.at[s], "fsdp",
            lax.rem(me + step + shards, shards),
        )

    def across(s):
        return shard_copy(place(s), place(s), x_send.at[s], x_recv.at[s], "ctx", 1 - piece)

    def arrival(d):
        for step in (1, -1):
            s = me - step * d
            there = (s >= 0) & (s <= shards - 1)
            s = jnp.minimum(jnp.maximum(s, 0), shards - 1)

            @pl.when(there)
            def _():
                along(s, step, False).wait_recv()
                across(s).start()

            @pl.when(there & ((me < shards - 1) if step > 0 else (me > 0)))
            def _():
                along(s, step, False).start()

    keep_z = pltpu.make_async_copy(
        z_ref, z_full_ref.at[pl.ds(pl.multiple_of(me * shard, shard), shard)], local.at[2 + chips]
    )
    keep_z.start()
    for step, there in ((1, me < shards - 1), (-1, me > 0)):
        @pl.when(there)
        def _():
            along(me, step, True).start()

    copies = {}
    for k, j in ranks.others()[::-1]:
        peer, slot = ranks.peer(k, j), 2 * k + j
        copies[slot] = remote(
            att_ref.at[pl.ds(pl.multiple_of(peer * own, own), own)], heads.at[slot],
            a_send.at[slot], a_recv.at[slot], peer,
        )
        copies[slot].start()
    swaps = [
        remote(blocks[k], others.at[k], b_send.at[k], b_recv.at[k], ranks.peer(0, 1))
        for k in range(chips)
    ]
    for copy in swaps:
        copy.start()
    fetch.wait()
    mine.wait()
    mid_ref[...] = rows_in[...] + dot(heads[0], blocks[0][...], NT)
    keeps = []
    for slot in range(1, count):
        k = slot // 2
        if slot % 2:
            swaps[k].wait_recv()
            keeps.append(pltpu.make_async_copy(others.at[k], other_ref.at[k], local.at[2 + k]))
            keeps[-1].start()
        copies[slot].wait_recv()
        mid_ref[...] += dot(heads[slot], others[k] if slot % 2 else blocks[k][...], NT)
    arrival(1)
    mid = mid_ref[...]
    factor = lax.rsqrt(row_mean(mid * mid) + EPSILON)
    rows_out[...] = (mid * factor * gain_ref[...]).astype(BF16)
    gather = GatherRows(ranks, rows_out, n2_ref, g_send, g_recv, local.at[0])
    gather.start()
    for d in range(2, shards):
        arrival(d)
    for slot in range(1, count):
        copies[slot].wait_send()
    for copy in swaps:
        copy.wait_send()
    for copy in keeps:
        copy.wait()
    gather.finish()
    keep_z.wait()
    for k in range(1, shards):
        across(lax.rem(me + k, shards)).wait()
    for s in range(shards):
        @pl.when((me >= s) & (me < shards - 1))
        def _():
            along(s, 1, False).wait_send()

        @pl.when((me <= s) & (me > 0))
        def _():
            along(s, -1, False).wait_send()


def mix(count, shards, attended, layer_input, gain, along_z, blocks):
    tokens, model = layer_input.shape
    own = tokens // count
    chips = count // 2
    width = attended.shape[1]
    vmem, hbm = pl.BlockSpec(memory_space=pltpu.VMEM), pl.BlockSpec(memory_space=pl.ANY)
    sem = pltpu.SemaphoreType.DMA
    return pl.pallas_call(
        functools.partial(mix_kernel, count, shards),
        in_specs=[hbm, hbm, vmem, hbm] + [vmem] * chips,
        out_specs=[hbm, vmem, hbm, hbm],
        out_shape=[
            jax.ShapeDtypeStruct((tokens, model), BF16),
            jax.ShapeDtypeStruct((own, model), F32),
            jax.ShapeDtypeStruct((chips, model, width), BF16),
            jax.ShapeDtypeStruct((model, along_z.shape[1]), BF16),
        ],
        scratch_shapes=[
            pltpu.VMEM((count, own, width), BF16),
            pltpu.VMEM((own, model), F32),
            pltpu.VMEM((own, model), BF16),
            pltpu.VMEM((chips, model, width), BF16),
            sem((count,)), sem((count,)), sem((chips,)), sem((chips,)), sem((2, chips)),
            sem((2, chips)), sem((2, shards)), sem((shards,)), sem((shards,)), sem((shards,)), sem((3 + chips,)),
        ],
        compiler_params=pltpu.CompilerParams(
            vmem_limit_bytes=40 << 20, collective_id=1, has_side_effects=True
        ),
        cost_estimate=pl.CostEstimate(
            flops=2 * tokens * model * model, bytes_accessed=150 << 20, transcendentals=0
        ),
        name="mix_heads",
    )(attended, layer_input, gain, along_z, *blocks)


def scatter_order(ranks, halves, own, i):
    k = lax.rem(i // halves + 1, ranks.chips)
    half = lax.rem(i, halves)
    rows = own // halves
    at = lambda j: pl.multiple_of(ranks.peer(k, j) * own + half * rows, rows)
    return k, half, at(0), at(1)


def half_rows(shard, which, half):
    return pl.ds(pl.multiple_of((shard * 2 + which) * half, half), half)


def swap_halves(src, dst, send, recv, shards):
    piece = lax.axis_index("ctx")
    half = src.shape[0] // (2 * shards)
    return [
        pltpu.make_async_remote_copy(
            src_ref=src.at[half_rows(s, 1 - piece, half)], dst_ref=dst.at[pl.ds(s * half, half)],
            send_sem=send.at[s], recv_sem=recv.at[s], device_id={"ctx": 1 - piece},
            device_id_type=MESH,
        )
        for s in range(shards)
    ]


def signal_piece(count):
    ranks = Ranks(count)
    sem = pltpu.get_barrier_semaphore()
    for k, j in ranks.others():
        pl.semaphore_signal(sem, inc=1, device_id={"tp": ranks.peer(k, j)}, device_id_type=MESH)
    pl.semaphore_signal(sem, inc=1, device_id={"ctx": 1 - lax.axis_index("ctx")}, device_id_type=MESH)
    pl.semaphore_wait(sem, count)


def feedforward_kernel(count, n2_ref, cot_ref, mid_ref, gain_ref, other_in, weight_ref, z_ref, *rest):
    blocks_in, rest = rest[: count // 2], rest[count // 2 :]
    (
        ffb_ref, mg_ref, bg_ref, gain_grad_ref, da_ref, grad_ref, grads_ref,
        gate_w, up_w, down_w, n2, fg, hid, gu, rows_in, ffb_out,
        c_send, c_recv, y_send, y_recv, f_send, f_recv, heads, other_ref, blocks,
        w_sem, in_sem, out_sem, cs, cr, ys, yr, fs, fr, hs, hr, local,
    ) = rest
    ranks = Ranks(count)
    own = mg_ref.shape[0]
    halves = 2
    rows = own // halves
    steps = ranks.chips * halves
    width = gate_w.shape[1]
    model = n2.shape[1]
    cut = weight_ref.shape[1] - width
    loads = [
        pltpu.make_async_copy(n2_ref, n2, w_sem.at[3]),
        pltpu.make_async_copy(weight_ref.at[:, pl.ds(0, width)], gate_w, w_sem.at[0]),
        pltpu.make_async_copy(weight_ref.at[:, pl.ds(width, cut)], up_w.at[:, pl.ds(0, cut)], w_sem.at[1]),
        pltpu.make_async_copy(
            z_ref.at[:, pl.ds(0, width - cut)], up_w.at[:, pl.ds(cut, width - cut)], w_sem.at[4]
        ),
        pltpu.make_async_copy(z_ref.at[:, pl.ds(width - cut, width)], down_w, w_sem.at[2]),
    ]
    late = [pltpu.make_async_copy(other_in, other_ref, w_sem.at[5])] + [
        pltpu.make_async_copy(block, blocks.at[k], w_sem.at[6 + k])
        for k, block in enumerate(blocks_in)
    ]
    for load in loads + late:
        load.start()

    def read(at, slot):
        return pltpu.make_async_copy(cot_ref.at[pl.ds(at, rows)], rows_in.at[slot], in_sem.at[slot])

    def tile(at, slot, begin):
        here = pl.ds(at, rows)

        def ready(n):
            if begin is not None:
                @pl.when(begin)
                def _():
                    loads[n].wait()

        ready(0)
        ready(1)
        n = n2[here, :]
        grad = rows_in[slot].astype(BF16)
        fg[here, :] = grad
        gate = dot(n, gate_w[...])
        ready(2)
        ready(3)
        up = dot(n, up_w[...])
        ready(4)
        back = dot(grad, down_w[...])
        sig = 1.0 / (1.0 + jnp.exp(-gate))
        act = gate * sig
        hidden = (act * up).astype(BF16)
        hid[here, :] = hidden
        gg = (back * up * (sig * (1.0 + gate * (1.0 - sig)))).astype(BF16)
        gu[here, :width] = gg
        ug = (back * act).astype(BF16)
        gu[here, width:] = ug
        return dot(gg, gate_w[...], NT) + dot(ug, up_w[...], NT), dot(hidden, down_w[...], NT)

    read(scatter_order(ranks, halves, own, 0)[3], 0).start()
    ranks.barrier()
    neighbour = ranks.peer(0, 1)

    def to_core(i):
        slot = lax.rem(i, 2)
        return [
            remote(c_send.at[slot], c_recv.at[slot], cs.at[slot], cr.at[slot], neighbour),
            remote(f_send.at[slot], f_recv.at[slot], fs.at[slot], fr.at[slot], neighbour),
        ]

    def to_chip(i, k):
        return remote(y_send.at[i], y_recv.at[i], ys.at[i], yr.at[i], ranks.peer(k, 0))

    def ffb_write(i):
        return pltpu.make_async_copy(ffb_out, ffb_ref.at[i], out_sem.at[0])

    def step(i, carry):
        k, u, at_mine, at_other = scatter_order(ranks, halves, own, i)
        slot = lax.rem(i, 2)
        read(at_mine, 1).start()
        read(at_other, 0).wait()
        grad, forward = tile(at_other, 0, i == 0)

        @pl.when(i + 1 < steps)
        def _():
            read(scatter_order(ranks, halves, own, i + 1)[3], 0).start()

        @pl.when(i > 1)
        def _():
            for copy in to_core(i):
                copy.wait_send()

        c_send[slot] = grad.astype(BF16)
        f_send[slot] = forward.astype(BF16)
        for copy in to_core(i):
            copy.start()
        read(at_mine, 1).wait()
        grad, forward = tile(at_mine, 1, None)

        @pl.when(i > 0)
        def _():
            ffb_write(i).wait()

        for copy in to_core(i):
            copy.wait_recv()
        grad = grad + c_recv[slot].astype(F32)
        ffb_out[...] = (forward + f_recv[slot].astype(F32)).astype(BF16)
        ffb_write(i).start()

        @pl.when(k != 0)
        def _():
            y_send[i] = grad.astype(BF16)
            to_chip(i, k).start()

        @pl.when(k == 0)
        def _():
            mg_ref[pl.ds(pl.multiple_of(u * rows, rows), rows), :] = grad

        return carry

    lax.fori_loop(0, steps, step, 0)
    mine_at = pl.multiple_of(ranks.me * own, own)
    fetch = lambda u: [
        pltpu.make_async_copy(mid_ref.at[pl.ds(u * rows, rows)], rows_in.at[0], in_sem.at[0]),
        read(mine_at + u * rows, 1),
    ]
    for copy in fetch(0):
        copy.start()
    cols = math.gcd(model, 384)
    writes = []

    def product(left, right, full, dst, n):
        for d in range(model // cols):
            full[d * cols : (d + 1) * cols, :] = dot(
                left[:, d * cols : (d + 1) * cols], right, TN
            ).astype(BF16)
        writes.append(pltpu.make_async_copy(full, dst, out_sem.at[1 + n]))
        writes[-1].start()

    product(n2, gu[:, :width], gate_w, grad_ref, 0)
    gain = gain_ref[...]
    gain_total = None
    for u in range(halves):
        here = slice(u * rows, (u + 1) * rows)
        total = mg_ref[here, :]
        for k in range(1, ranks.chips):
            i = (k - 1) * halves + u
            to_chip(i, k).wait_recv()
            total = total + y_recv[i].astype(F32)
        for copy in fetch(u):
            copy.wait()
        mid = rows_in[0]
        factor = lax.rsqrt(row_mean(mid * mid) + EPSILON)
        hat = mid * factor
        term = jnp.sum(total * hat, axis=0, keepdims=True)
        gain_total = term if gain_total is None else gain_total + term
        inner = total * gain
        grad = rows_in[1] + factor * (inner - hat * row_mean(inner * hat))
        mg_ref[here, :] = grad
        bg_ref[here, :] = grad.astype(BF16)
        if u + 1 < halves:
            for copy in fetch(u + 1):
                copy.start()
    gain_grad_ref[...] = gain_total
    for load in late:
        load.wait()
    back = []
    for k, j in ranks.others()[::-1]:
        slot, peer = 2 * k + j, ranks.peer(-k, j)
        heads[slot] = dot(bg_ref[...], other_ref[k] if j else blocks[k]).astype(BF16)
        back.append(
            remote(heads.at[slot], da_ref.at[pl.ds(mine_at, own)], hs.at[slot], hr.at[slot], peer)
        )
        back[-1].start()
    heads[0] = dot(bg_ref[...], blocks[0]).astype(BF16)
    keep = pltpu.make_async_copy(heads.at[0], da_ref.at[pl.ds(mine_at, own)], local.at[0])
    keep.start()
    product(n2, gu[:, width:], up_w, grads_ref.at[:, pl.ds(0, width)], 1)
    product(fg, hid[...], down_w, grads_ref.at[:, pl.ds(width, width)], 2)
    for i in (steps - 2, steps - 1):
        for copy in to_core(i):
            copy.wait_send()
    for i in range(steps - halves):
        to_chip(i, i // halves + 1).wait_send()
    ffb_write(steps - 1).wait()
    for copy in back:
        copy.wait()
    keep.wait()
    for copy in writes:
        copy.wait()


def feedforward(count, n2, cotangent, middle, gain, weights, along_z, blocks, others):
    tokens, model = n2.shape
    own = tokens // count
    hidden = (weights.shape[1] + along_z.shape[1]) // 3
    width = blocks[0].shape[1]
    rows, steps = own // 2, count
    vmem, hbm = pl.BlockSpec(memory_space=pltpu.VMEM), pl.BlockSpec(memory_space=pl.ANY)
    sem = pltpu.SemaphoreType.DMA
    return pl.pallas_call(
        functools.partial(feedforward_kernel, count),
        in_specs=[hbm, hbm, hbm, vmem, hbm, hbm, hbm] + [hbm] * (count // 2),
        out_specs=[hbm, vmem, vmem, vmem, hbm, hbm, hbm],
        out_shape=[
            jax.ShapeDtypeStruct((steps, rows, model), BF16),
            jax.ShapeDtypeStruct((own, model), F32),
            jax.ShapeDtypeStruct((own, model), BF16),
            jax.ShapeDtypeStruct((1, model), F32),
            jax.ShapeDtypeStruct((tokens, width), BF16),
            jax.ShapeDtypeStruct((model, hidden), BF16),
            jax.ShapeDtypeStruct((model, 2 * hidden), BF16),
        ],
        scratch_shapes=[pltpu.VMEM((model, hidden), BF16)] * 3
        + [
            pltpu.VMEM((tokens, model), BF16),
            pltpu.VMEM((tokens, model), BF16),
            pltpu.VMEM((tokens, hidden), BF16),
            pltpu.VMEM((tokens, 2 * hidden), BF16),
            pltpu.VMEM((2, rows, model), F32),
            pltpu.VMEM((rows, model), BF16),
        ]
        + [pltpu.VMEM((2, rows, model), BF16)] * 2
        + [pltpu.VMEM((steps - 2, rows, model), BF16)] * 2
        + [pltpu.VMEM((2, rows, model), BF16)] * 2
        + [
            pltpu.VMEM((count, own, width), BF16),
            pltpu.VMEM(others.shape, BF16),
            pltpu.VMEM(others.shape, BF16),
            sem((6 + count // 2,)), sem((2,)), sem((4,)),
            sem((2,)), sem((2,)), sem((steps - 2,)), sem((steps - 2,)),
            sem((2,)), sem((2,)), sem((count,)), sem((count,)), sem((1,)),
        ],
        compiler_params=pltpu.CompilerParams(
            vmem_limit_bytes=63 << 20, collective_id=2, has_side_effects=True
        ),
        cost_estimate=pl.CostEstimate(
            flops=2 * tokens * model * hidden * 9, bytes_accessed=280 << 20,
            transcendentals=tokens * hidden,
        ),
        name="feed_forward",
    )(n2, cotangent, middle, gain, others, weights, along_z, *blocks)


def shard_copy(src, dst, send, recv, axis, index):
    return pltpu.make_async_remote_copy(
        src_ref=src, dst_ref=dst, send_sem=send, recv_sem=recv, device_id={axis: index},
        device_id_type=MESH,
    )


def begin_kernel(
    shards, x_ref, qkv_ref, wo_ref, gains_ref, order_ref, n_ref, qkv_full_ref, wo_full_ref, gain_out_ref,
    qkv_full, wo_full, normed, rows_in, gain_buf, zs, zr, xs, xr, gs, gr, own_sem, in_sem, out_sem,
):
    del order_ref
    me, piece = lax.axis_index("fsdp"), lax.axis_index("ctx")
    fulls, sources = (qkv_full, wo_full), (qkv_ref, wo_ref)
    shard = qkv_ref.shape[0]
    half = shard // 2
    tokens = normed.shape[0]
    rows = rows_in.shape[1]
    steps = tokens // rows

    def read(i):
        return pltpu.make_async_copy(
            x_ref.at[pl.ds(i * rows, rows)], rows_in.at[i % 2], in_sem.at[i % 2]
        )

    read(0).start()
    keeps = [
        pltpu.make_async_copy(src, full.at[pl.ds(pl.multiple_of(me * shard, shard), shard)], own_sem.at[a])
        for a, (src, full) in enumerate(zip(sources, fulls))
    ]
    for copy in keeps:
        copy.start()
    keep_gain = pltpu.make_async_copy(gains_ref, gain_buf.at[me], own_sem.at[2])
    keep_gain.start()
    barrier = pltpu.get_barrier_semaphore()
    for k in range(1, shards):
        pl.semaphore_signal(
            barrier, inc=1, device_id={"fsdp": lax.rem(me + k, shards)}, device_id_type=MESH
        )
    pl.semaphore_signal(barrier, inc=1, device_id={"ctx": 1 - piece}, device_id_type=MESH)
    pl.semaphore_wait(barrier, shards)

    def place(a, s, which):
        return fulls[a].at[half_rows(s, which, half)]

    def own_half(a):
        return sources[a].at[pl.ds(pl.multiple_of(piece * half, half), half)]

    def along(a, s, step, mine):
        way = 0 if step > 0 else 1
        src = own_half(a) if mine else place(a, s, piece)
        return shard_copy(
            src, place(a, s, piece), zs.at[a, way, s], zr.at[a, s], "fsdp",
            lax.rem(me + step + shards, shards),
        )

    def across(a, s):
        return shard_copy(
            place(a, s, piece), place(a, s, piece), xs.at[a, s], xr.at[a, s], "ctx", 1 - piece
        )

    gain_copies = [
        shard_copy(
            gains_ref, gain_buf.at[me], gs.at[k], gr.at[k], "fsdp", lax.rem(me + k, shards)
        )
        for k in range(1, shards)
    ]
    for copy in gain_copies:
        copy.start()
    for a in range(2):
        for step, there in ((1, me < shards - 1), (-1, me > 0)):
            @pl.when(there)
            def _():
                along(a, me, step, True).start()

    for copy in gain_copies:
        copy.wait()
    keep_gain.wait()
    gain_out_ref[...] = jnp.concatenate([gain_buf[s] for s in range(shards)], axis=1)
    for i in range(steps):
        if i + 1 < steps:
            read(i + 1).start()
        read(i).wait()
        x = rows_in[i % 2]
        factor = lax.rsqrt(row_mean(x * x) + EPSILON)
        normed[i * rows : (i + 1) * rows, :] = (x * factor * gain_out_ref[0:1, :]).astype(BF16)
    write_normed = pltpu.make_async_copy(normed, n_ref, out_sem.at[0])
    write_normed.start()

    def arrival(d, step):
        s = me - step * d
        there = (s >= 0) & (s <= shards - 1)
        s = jnp.minimum(jnp.maximum(s, 0), shards - 1)
        onward = (me < shards - 1) if step > 0 else (me > 0)

        @pl.when(there)
        def _():
            for a in range(2):
                along(a, s, step, False).wait_recv()
                across(a, s).start()

        @pl.when(there & onward)
        def _():
            for a in range(2):
                along(a, s, step, False).start()

    for d in range(1, shards):
        arrival(d, 1)
        arrival(d, -1)
    for copy in keeps:
        copy.wait()
    for k in range(1, shards):
        s = lax.rem(me + k, shards)
        for a in range(2):
            across(a, s).wait_recv()
    writes = [
        pltpu.make_async_copy(qkv_full, qkv_full_ref, out_sem.at[1]),
        pltpu.make_async_copy(wo_full, wo_full_ref, out_sem.at[2]),
    ]
    for copy in writes:
        copy.start()
    for a in range(2):
        for s in range(shards):
            @pl.when((me >= s) & (me < shards - 1))
            def _():
                along(a, s, 1, False).wait_send()

            @pl.when((me <= s) & (me > 0))
            def _():
                along(a, s, -1, False).wait_send()

        for k in range(1, shards):
            across(a, lax.rem(me + k, shards)).wait_send()
    write_normed.wait()
    for copy in writes:
        copy.wait()


def begin(shards, x, qkv, wo, gains, order):
    tokens, model = x.shape
    rows = math.gcd(tokens, 256)
    vmem, hbm = pl.BlockSpec(memory_space=pltpu.VMEM), pl.BlockSpec(memory_space=pl.ANY)
    sem = pltpu.SemaphoreType.DMA
    return pl.pallas_call(
        functools.partial(begin_kernel, shards),
        in_specs=[hbm, vmem, vmem, vmem, hbm],
        out_specs=[hbm, hbm, hbm, vmem],
        out_shape=[
            jax.ShapeDtypeStruct((tokens, model), BF16),
            jax.ShapeDtypeStruct((model, qkv.shape[1]), BF16),
            jax.ShapeDtypeStruct((model, wo.shape[1]), BF16),
            jax.ShapeDtypeStruct((gains.shape[0], model), F32),
        ],
        scratch_shapes=[
            pltpu.VMEM((model, qkv.shape[1]), BF16),
            pltpu.VMEM((model, wo.shape[1]), BF16),
            pltpu.VMEM((tokens, model), BF16),
            pltpu.VMEM((2, rows, model), F32),
            pltpu.VMEM((shards,) + gains.shape, F32),
            sem((2, 2, shards)), sem((2, shards)), sem((2, shards)), sem((2, shards)),
            sem((shards,)), sem((shards,)), sem((3,)), sem((2,)), sem((3,)),
        ],
        compiler_params=pltpu.CompilerParams(
            vmem_limit_bytes=48 << 20, collective_id=4, has_side_effects=True
        ),
        cost_estimate=pl.CostEstimate(flops=0, bytes_accessed=120 << 20, transcendentals=0),
        name="norm_and_gather",
    )(x, qkv, wo, gains, order)


def project_kernel(
    q_heads, n_ref, qkv_ref, spread_ref, cos_ref, sin_ref, krow_ref, vrow_ref, pick_ref, q_ref, kv_ref,
    dense_ref, wide
):
    @pl.when(pl.program_id(0) == 0)
    def _():
        model = qkv_ref.shape[0]
        block = math.gcd(model, 512)
        for r in range(0, model, block):
            wide[r : r + block, :] = dot(qkv_ref[r : r + block, :], spread_ref[...]).astype(BF16)

    kv_heads = kv_ref.shape[1] // LANES // 2
    cos, sin = cos_ref[...], sin_ref[...]
    out = dot(n_ref[...], wide[...])
    plain = []
    for h in range(q_heads + 2 * kv_heads):
        part = out[:, h * LANES : (h + 1) * LANES]
        if h < q_heads + kv_heads:
            part = part * cos + pltpu.roll(part, LANES // 2, 1) * sin
        if h < q_heads:
            q_ref[:, h * LANES : (h + 1) * LANES] = part.astype(BF16)
        else:
            plain.append(part.astype(BF16))
            part = part + (krow_ref[...] if h < q_heads + kv_heads else vrow_ref[...])
            kv_ref[:, (h - q_heads) * LANES : (h - q_heads + 1) * LANES] = part.astype(BF16)
    dense_ref[...] = dot(jnp.concatenate(plain, axis=1), pick_ref[...]).astype(BF16)


def project(normed, qkv, spread, cos, sin, krow, vrow, pick, q_heads, kv_heads):
    tokens, model = normed.shape
    wide = spread.shape[1]
    bm = math.gcd(tokens, 256)
    whole = lambda a: pl.BlockSpec(a.shape, lambda i: (0, 0))
    row = lambda w: pl.BlockSpec((bm, w), lambda i: (i, 0))
    return pl.pallas_call(
        functools.partial(project_kernel, q_heads),
        grid=(tokens // bm,),
        in_specs=[row(model), whole(qkv), whole(spread), row(LANES), row(LANES), whole(krow), whole(vrow),
            whole(pick)],
        out_specs=[row(q_heads * LANES), row(2 * kv_heads * LANES), row(pick.shape[1])],
        out_shape=[
            jax.ShapeDtypeStruct((tokens, q_heads * LANES), BF16),
            jax.ShapeDtypeStruct((tokens, 2 * kv_heads * LANES), BF16),
            jax.ShapeDtypeStruct((tokens, pick.shape[1]), BF16),
        ],
        scratch_shapes=[pltpu.VMEM((model, wide), BF16)],
        compiler_params=pltpu.CompilerParams(vmem_limit_bytes=40 << 20),
        cost_estimate=pl.CostEstimate(
            flops=2 * tokens * model * wide, bytes_accessed=16 << 20, transcendentals=0
        ),
        name="project_qkv",
    )(normed, qkv, spread, cos, sin, krow, vrow, pick)


def dense_kernel(
    chips, dq_ref, dkv_ref, after_ref, cos_ref, sin_ref, rotk_ref, valk_ref, att_ref, n_ref, *rest
):
    blocks, rest = rest[:chips], rest[chips:]
    dense_ref, grad_ref, normed, branch, send, recv, local = rest
    ranks = Ranks(2 * chips)
    fetch = pltpu.make_async_copy(n_ref, normed, local.at[chips])
    fetch.start()
    sem = pltpu.get_barrier_semaphore()
    pl.semaphore_signal(sem, inc=1, device_id={"tp": ranks.peer(0, 1)}, device_id_type=MESH)
    pl.semaphore_wait(sem, 1)
    copies = both_cores(ranks, blocks, branch, send, recv, local)
    for copy in copies:
        copy.start()
    width = dense_ref.shape[1]
    lanes = dkv_ref.shape[1] // 2
    cos, sin = cos_ref[...], sin_ref[...]
    turned = []
    for h in range(lanes // LANES):
        at = slice(h * LANES, (h + 1) * LANES)
        key = dkv_ref[:, at] + after_ref[:, at].astype(F32)
        turned.append((key * cos - pltpu.roll(key, LANES // 2, 1) * sin).astype(BF16))
    dk = dot(jnp.concatenate(turned, axis=1), rotk_ref[...]).astype(BF16)
    dv = (dkv_ref[:, lanes:] + after_ref[:, lanes:].astype(F32)).astype(BF16)
    dv = dot(dv, valk_ref[...]).astype(BF16)
    dense_ref[...] = jnp.concatenate([dq_ref[...], dk, dv], axis=1)
    fetch.wait()
    model = normed.shape[1]
    cols = math.gcd(model, 384)
    for d in range(0, model, cols):
        grad_ref[d : d + cols, :width] = dot(
            normed[:, d : d + cols], dense_ref[...], TN
        ).astype(BF16)
    for copy in copies:
        copy.wait()
    for d in range(0, model, cols):
        grad_ref[d : d + cols, width:] = dot(branch[:, d : d + cols], att_ref[...], TN).astype(BF16)


def dense_gradients(dq, dkv, after, cos, sin, rot_k, val_k, attended, normed, blocks):
    tokens, model = normed.shape
    chips = len(blocks)
    width = dq.shape[1] + 2 * rot_k.shape[1]
    total = width + attended.shape[1]
    vmem, hbm = pl.BlockSpec(memory_space=pltpu.VMEM), pl.BlockSpec(memory_space=pl.ANY)
    sem = pltpu.SemaphoreType.DMA
    return pl.pallas_call(
        functools.partial(dense_kernel, chips),
        in_specs=[vmem] * 8 + [hbm] * (1 + chips),
        out_specs=[vmem, vmem],
        out_shape=[
            jax.ShapeDtypeStruct((tokens, width), BF16),
            jax.ShapeDtypeStruct((model, total), BF16),
        ],
        scratch_shapes=[
            pltpu.VMEM((tokens, model), BF16),
            pltpu.VMEM((tokens, model), BF16),
            sem((chips,)), sem((chips,)), sem((chips + 1,)),
        ],
        compiler_params=pltpu.CompilerParams(
            vmem_limit_bytes=48 << 20, collective_id=5, has_side_effects=True
        ),
        cost_estimate=pl.CostEstimate(
            flops=2 * tokens * model * total, bytes_accessed=24 << 20, transcendentals=0
        ),
        name="dense_gradients",
    )(dq, dkv, after, cos, sin, rot_k, val_k, attended, normed, *blocks)


def close_kernel(
    count, shards, dense_ref, w_ref, x_ref, mg_ref, gain_ref, gain_two_ref, grad_ref, gate_ref, *rest
):
    layers, rest = rest[: count // 2], rest[count // 2 :]
    (
        out_ref, gain_grad_ref, half_ref, lay_ref, gate_out_ref, rows_in, rows_out, sums, c_send, c_recv, y_send,
        y_recv, x_mine, x_recv, gate_mine, gate_recv, t_send, t_recv, cs, cr, ys, yr, g_send, g_recv, xs, xr, x_sem,
        ls, lr, lay_sem, ts, tr, gate_sem, local,
    ) = rest
    ranks = Ranks(count)
    own = rows_in.shape[0]
    halves = 2
    rows = own // halves
    steps = ranks.chips * halves
    fetch = pltpu.make_async_copy(
        x_ref.at[pl.ds(pl.multiple_of(ranks.me * own, own), own)], rows_in, local.at[0]
    )
    fetch.start()
    def tile(at):
        return dot(dense_ref[pl.ds(at, rows), :], w_ref[...], NT)

    piece = lax.axis_index("ctx")
    half = grad_ref.shape[0] // (2 * shards)
    keeps = [
        pltpu.make_async_copy(
            grad_ref.at[half_rows(s, piece, half)], x_mine.at[pl.ds(s * half, half)], x_sem.at[s]
        )
        for s in range(shards)
    ]
    keeps.append(pltpu.make_async_copy(gate_ref, gate_mine, gate_sem.at[0]))
    for copy in keeps:
        copy.start()
    me = lax.axis_index("fsdp")
    barrier = pltpu.get_barrier_semaphore()
    for k, j in ranks.others():
        pl.semaphore_signal(barrier, inc=1, device_id={"tp": ranks.peer(k, j)}, device_id_type=MESH)
    for k in range(1, shards):
        pl.semaphore_signal(
            barrier, inc=1, device_id={"fsdp": lax.rem(me + k, shards)}, device_id_type=MESH
        )
    pl.semaphore_signal(barrier, inc=1, device_id={"ctx": 1 - piece}, device_id_type=MESH)
    pl.semaphore_wait(barrier, count + shards - 1)
    swaps = swap_halves(grad_ref, x_recv, xs, xr, shards)
    swaps.append(
        pltpu.make_async_remote_copy(
            src_ref=gate_ref, dst_ref=gate_recv, send_sem=gate_sem.at[1], recv_sem=gate_sem.at[2],
            device_id={"ctx": 1 - piece}, device_id_type=MESH,
        )
    )
    for copy in swaps:
        copy.start()
    forward = both_cores(ranks, layers, lay_ref, ls, lr, lay_sem)
    for copy in forward:
        copy.start()
    neighbour = ranks.peer(0, 1)

    def to_core(i):
        return remote(c_send.at[i], c_recv.at[i], cs.at[i], cr.at[i], neighbour)

    def to_chip(i, k):
        return remote(y_send.at[i], y_recv.at[i], ys.at[i], yr.at[i], ranks.peer(k, 0))

    def send_step(i, carry):
        k, u, at_mine, at_other = scatter_order(ranks, halves, own, i)
        c_send[i] = tile(at_other).astype(BF16)
        to_core(i).start()
        return carry

    def sum_step(i, carry):
        k, u, at_mine, at_other = scatter_order(ranks, halves, own, i)
        grad = tile(at_mine)
        to_core(i).wait_recv()
        grad = grad + c_recv[i].astype(F32)

        @pl.when(k != 0)
        def _():
            y_send[i] = grad.astype(BF16)
            to_chip(i, k).start()

        @pl.when(k == 0)
        def _():
            sums[u] = grad

        return carry

    lax.fori_loop(0, steps, send_step, 0)
    lax.fori_loop(0, steps, sum_step, 0)
    fetch.wait()
    gain = gain_ref[...]
    gain_total = None
    for u in range(halves):
        total = sums[u]
        for k in range(1, ranks.chips):
            i = (k - 1) * halves + u
            to_chip(i, k).wait_recv()
            total = total + y_recv[i].astype(F32)
        x = rows_in[u * rows : (u + 1) * rows]
        factor = lax.rsqrt(row_mean(x * x) + EPSILON)
        hat = x * factor
        term = jnp.sum(total * hat, axis=0, keepdims=True)
        gain_total = term if gain_total is None else gain_total + term
        inner = total * gain
        grad = mg_ref[u * rows : (u + 1) * rows] + factor * (inner - hat * row_mean(inner * hat))
        rows_out[u * rows : (u + 1) * rows] = grad.astype(BF16)
    gather = GatherRows(ranks, rows_out, out_ref, g_send, g_recv, local.at[0])
    gather.start()
    total = jnp.concatenate([gain_total, gain_two_ref[...], jnp.zeros((6, gain_total.shape[1]), F32)], axis=0)
    hops = [[{"tp": ranks.peer(0, 1)}], [{"tp": ranks.peer(k, 0)} for k in range(1, ranks.chips)]]
    hops += [[{"ctx": 1 - piece}], [{"fsdp": lax.rem(me + k, shards)} for k in range(1, shards)]]
    slot, sent = 0, []
    for n, peers in enumerate(hops):
        t_send[n] = total
        copies = []
        for peer in peers:
            copies.append(
                pltpu.make_async_remote_copy(
                    src_ref=t_send.at[n], dst_ref=t_recv.at[slot], send_sem=ts.at[slot],
                    recv_sem=tr.at[slot], device_id=peer, device_id_type=MESH,
                )
            )
            copies[-1].start()
            slot += 1
        for copy, at in zip(copies, range(slot - len(copies), slot)):
            copy.wait_recv()
            total = total + t_recv[at]
        sent += copies
    gain_grad_ref[...] = total
    for copy in sent:
        copy.wait_send()
    gather.finish()
    for copy in forward:
        copy.wait()
    for s in range(shards):
        keeps[s].wait()
        swaps[s].wait_recv()
        here = slice(s * half, (s + 1) * half)
        half_ref[here, :] = (x_mine[here, :].astype(F32) + x_recv[here, :].astype(F32)).astype(BF16)
    keeps[shards].wait()
    swaps[shards].wait_recv()
    gate_out_ref[...] = gate_mine[...].astype(F32) + gate_recv[...].astype(F32)
    for copy in swaps:
        copy.wait_send()
    for i in range(steps):
        to_core(i).wait_send()
    for i in range(steps - halves):
        to_chip(i, i // halves + 1).wait_send()


def close(count, shards, dense, weight, layer_input, middle_grad, gain, gain_two, grad, gate, layers):
    tokens, model = layer_input.shape
    own = tokens // count
    rows, steps, chips = own // 2, count, count // 2
    vmem, hbm = pl.BlockSpec(memory_space=pltpu.VMEM), pl.BlockSpec(memory_space=pl.ANY)
    sem = pltpu.SemaphoreType.DMA
    return pl.pallas_call(
        functools.partial(close_kernel, count, shards),
        in_specs=[vmem, vmem, hbm, vmem, vmem, vmem, hbm, hbm] + [hbm] * chips,
        out_specs=[hbm, vmem, vmem, hbm, vmem],
        out_shape=[
            jax.ShapeDtypeStruct((tokens, model), BF16),
            jax.ShapeDtypeStruct((8, model), F32),
            jax.ShapeDtypeStruct((model // 2, grad.shape[1]), BF16),
            jax.ShapeDtypeStruct((tokens, model), BF16),
            jax.ShapeDtypeStruct(gate.shape, F32),
        ],
        scratch_shapes=[
            pltpu.VMEM((own, model), F32),
            pltpu.VMEM((own, model), BF16),
            pltpu.VMEM((2, rows, model), F32),
        ]
        + [pltpu.VMEM((steps, rows, model), BF16)] * 2
        + [pltpu.VMEM((steps - 2, rows, model), BF16)] * 2
        + [pltpu.VMEM((model // 2, grad.shape[1]), BF16)] * 2
        + [
            pltpu.VMEM(gate.shape, BF16),
            pltpu.VMEM(gate.shape, BF16),
            pltpu.VMEM((4, 8, model), F32),
            pltpu.VMEM((chips + shards, 8, model), F32),
            sem((steps,)), sem((steps,)), sem((steps - 2,)), sem((steps - 2,)),
            sem((2, chips)), sem((2, chips)), sem((shards,)), sem((shards,)), sem((shards,)),
            sem((chips,)), sem((chips,)), sem((chips,)), sem((chips + shards,)),
            sem((chips + shards,)), sem((3,)), sem((2,)),
        ],
        compiler_params=pltpu.CompilerParams(
            vmem_limit_bytes=48 << 20, collective_id=3, has_side_effects=True
        ),
        cost_estimate=pl.CostEstimate(
            flops=2 * tokens * model * dense.shape[1], bytes_accessed=200 << 20, transcendentals=0
        ),
        name="close_layer",
    )(dense, weight, layer_input, middle_grad, gain, gain_two, grad, gate, *layers)


def per_device(
    sizes,
    layer_input,
    doc_lengths,
    attention_gain,
    query_weight,
    key_matrix,
    value_matrix,
    output_weight,
    feedforward_gain,
    gate_weight,
    up_weight,
    down_weight,
    output_cotangent,
):
    shards, pieces, ranks = sizes
    assert pieces == 2 and ranks % 2 == 0
    chips = ranks // 2
    tokens, model = layer_input.shape
    own = tokens // ranks
    head_dim = HEAD_SIZE
    q_heads = query_weight.shape[1] // head_dim
    kv_heads = key_matrix.shape[1] // head_dim
    q_width, kv_width = q_heads * head_dim, kv_heads * head_dim
    piece = lax.axis_index("ctx")
    rank = lax.axis_index("tp")
    chip, core = rank // 2, rank % 2
    me = lax.axis_index("fsdp")
    scale = 1.0 / math.sqrt(head_dim)

    swap_x = [(0, 1), (1, 0)]
    swap_core = [(i, i ^ 1) for i in range(ranks)]

    def chip_shift(k):
        return [(i, (i + 2 * k) % ranks) for i in range(ranks)]

    def shard_shift(k):
        return [(i, (i + k) % shards) for i in range(shards)]

    def pick(array, index, axis=0):
        return lax.dynamic_index_in_dim(array, index, axis, keepdims=False)

    def half_of(shard):
        rows = shard.shape[0] // 2
        return lax.dynamic_slice_in_dim(shard, piece * rows, rows, 0)

    both_axes = ("fsdp", "ctx")

    def reduce_fsdp(part):
        return lax.psum_scatter(part, "fsdp", scatter_dimension=0, tiled=True)

    def add_pieces(mine):
        return mine.astype(F32) + lax.ppermute(mine, "ctx", swap_x).astype(F32)

    def whole_shard(mine):
        other = lax.ppermute(mine, "ctx", swap_x)
        pair = jnp.where(
            piece == 0, jnp.concatenate([mine, other], 0), jnp.concatenate([other, mine], 0)
        )
        return pair.astype(F32)

    cut = up_weight.shape[1] // 2
    ff_half = half_of(jnp.concatenate([gate_weight, up_weight[:, :cut]], axis=1))
    ff_later = jnp.concatenate([up_weight[:, cut:], down_weight.T], axis=1)
    gain_shard = jnp.stack([attention_gain, feedforward_gain]).astype(F32)
    gain_shard = jnp.pad(gain_shard, ((0, 6), (0, 0)))
    qkv_shard = jnp.concatenate([query_weight, key_matrix, value_matrix], axis=1)
    positions = doc_positions(doc_lengths[0], piece * tokens, tokens)
    cos, sin = rotary_lanes(positions, head_dim)
    lane = np.arange(LANES)[None, :]
    half_dim = head_dim // 2
    krow = np.where((lane >= half_dim) & (lane < half_dim + 3), -1.0, 0.0).astype(np.float32)
    vrow = np.where((lane >= head_dim) & (lane < head_dim + 3), 1.0, 0.0).astype(np.float32)
    rot_q, rot_k = select_rotary(q_heads, head_dim), select_rotary(kv_heads, head_dim)
    val_q, val_k = select_value(q_heads, head_dim), select_value(kv_heads, head_dim)
    val_q_wide = np.ascontiguousarray(val_q.T)
    spread = np.zeros((q_width + 2 * kv_width, (q_heads + 2 * kv_heads) * LANES), rot_q.dtype)
    at_key, at_value = q_heads * LANES, (q_heads + kv_heads) * LANES
    spread[:q_width, :at_key] = rot_q.T
    spread[q_width : q_width + kv_width, at_key:at_value] = rot_k.T
    spread[q_width + kv_width :, at_value:] = val_k.T
    normed_one, qkv_full, out_own, gains_full = begin(
        shards, layer_input, qkv_shard, output_weight.T, gain_shard, ff_half
    )
    widen_kv = np.ascontiguousarray(spread[q_width:, at_key:])
    marks = np.concatenate([krow] * kv_heads + [vrow] * kv_heads, axis=1)
    queries, keys_values, dense_kv = project(
        normed_one, qkv_full, spread, cos, sin, krow, vrow, np.ascontiguousarray(widen_kv.T), q_heads, kv_heads
    )
    ff_half, gains_full = lax.optimization_barrier((ff_half, gains_full))
    ff_full = lax.all_gather(ff_half, both_axes, axis=0, tiled=True)
    gain_one, gain_two = gains_full[0:1], gains_full[1:2]
    before = lax.ppermute(dense_kv, "ctx", [(0, 1)])
    base = -(piece - 1) * tokens
    ends = jnp.cumsum(doc_lengths[0]).astype(jnp.int32) + base
    base = base.astype(jnp.int32).reshape(1)
    state = attention_forward(ends, base, queries, keys_values, head_dim, tokens)
    attended, marked = attention_forward(
        ends, base, queries, before, head_dim, 0, state, (widen_kv, marks, val_q)
    )
    wo = [out_own] + [lax.ppermute(out_own, "tp", chip_shift(k)) for k in range(1, chips)]
    normed_two, middle, wo_others, ff_rest = mix(
        ranks, shards, attended, layer_input, gain_two, ff_later, wo
    )
    (
        feed_sums, middle_grad, branch_grad, gain_two_grad, attended_grad, gate_part, feed_part,
    ) = feedforward(
        ranks, normed_two, output_cotangent, middle, gain_two, ff_full, ff_rest, wo, wo_others
    )
    gate_own, feed_own = reduce_fsdp(gate_part), reduce_fsdp(feed_part)
    cut = feed_sums.reshape(chips, own, model)
    feed_sums = [lax.ppermute(cut[k - 1], "tp", chip_shift(k)) for k in range(1, chips)]
    dq_part, dkv_before = attention_backward(
        ends, base, marked, attended_grad, attended, before, val_q_wide, head_dim, 0,
        extra=(widen_kv, marks),
    )
    after = lax.ppermute(dkv_before, "ctx", [(1, 0)])
    dq, dkv = attention_backward(
        ends, base, marked, attended_grad, attended, keys_values, val_q_wide, head_dim, tokens,
        (dq_part, cos, sin, rot_q),
    )

    feed_sums, dq = lax.optimization_barrier((feed_sums, dq))
    layer_rows = middle + cut[chips - 1].astype(F32)
    for block in feed_sums:
        layer_rows = layer_rows + block.astype(F32)
    layer_rows = layer_rows.astype(BF16)

    def from_chips(rows):
        return [rows] + [lax.ppermute(rows, "tp", chip_shift(k)) for k in range(1, chips)]

    dqkv, attention_part = dense_gradients(
        dq, dkv, after, cos, sin, rot_k, val_k, attended, normed_one, from_chips(branch_grad)
    )
    input_gradient, gains, attention_half, layer_output, gate = close(
        ranks, shards, dqkv, qkv_full, layer_input, middle_grad, gain_one, gain_two_grad,
        attention_part, gate_own, from_chips(layer_rows),
    )
    attention_half, feed_own = lax.optimization_barrier((attention_half, feed_own))
    attention = whole_shard(reduce_fsdp(attention_half))
    feed = add_pieces(feed_own)
    layer_output, input_gradient = layer_output.astype(F32), input_gradient.astype(F32)
    ff_width = gate_weight.shape[1]
    gains = lax.dynamic_slice_in_dim(gains, me * gain_shard.shape[1], gain_shard.shape[1], 1)

    return (
        layer_output,
        input_gradient,
        gains[0],
        attention[:, :q_width],
        attention[:, q_width : q_width + kv_width],
        attention[:, q_width + kv_width : q_width + 2 * kv_width],
        attention[:, q_width + 2 * kv_width :].T,
        gains[1],
        gate,
        feed[:, :ff_width],
        feed[:, ff_width:].T,
    )


def solution(mesh):
    rows = P(("fsdp", "ctx"), None)
    into, out_of = P("fsdp", "tp"), P("tp", "fsdp")
    sizes = (mesh.shape["fsdp"], mesh.shape["ctx"], mesh.shape["tp"])
    return jax.shard_map(
        functools.partial(per_device, sizes),
        mesh=mesh,
        in_specs=(
            rows, P("fsdp", None), P("fsdp"), into, into, into, out_of, P("fsdp"), into, into,
            out_of, rows,
        ),
        out_specs=(
            rows, rows, P("fsdp"), into, into, into, out_of, P("fsdp"), into, into, out_of,
        ),
        check_vma=False,
    )
```

```python
import functools
import math

import jax
import jax.numpy as jnp
import ml_dtypes
import numpy as np
from jax import lax
from jax.experimental import pallas as pl
from jax.experimental.pallas import tpu as pltpu
from jax.sharding import PartitionSpec as P

HEAD_SIZE = 96
EPSILON = 1e-05
THETA = 100000.0
NEGATIVE = -1e30
LOG2E = 1.4426950408889634
LANES = 128
F32 = jnp.float32
BF16 = jnp.bfloat16
NN = (((1,), (0,)), ((), ()))
NT = (((1,), (1,)), ((), ()))
TN = (((0,), (0,)), ((), ()))


def dot(left, right, dims=NN):
    return lax.dot_general(left, right, dims, preferred_element_type=F32)


def select_rotary(heads, head_dim):
    col = np.arange(heads * head_dim)
    half = head_dim // 2
    within = col % head_dim
    lane = np.where(within < half, within, within - half + LANES // 2)
    return select_lanes(heads, (col // head_dim) * LANES + lane)


def select_value(heads, head_dim):
    col = np.arange(heads * head_dim)
    return select_lanes(heads, (col // head_dim) * LANES + col % head_dim)


def select_lanes(heads, want):
    return (np.arange(heads * LANES)[:, None] == want[None, :]).astype(ml_dtypes.bfloat16)


def rotary_lanes(positions, head_dim):
    half = head_dim // 2
    freqs = THETA ** (-(jnp.arange(half, dtype=F32) * 2.0 / head_dim))
    angles = positions.astype(F32)[:, None] * freqs[None, :]
    cos, sin = jnp.cos(angles), jnp.sin(angles)
    pad = jnp.zeros((positions.shape[0], LANES // 2 - half), F32)
    return (
        jnp.concatenate([cos, pad, cos, pad], axis=1),
        jnp.concatenate([-sin, pad, sin, pad], axis=1),
    )


def doc_positions(lengths, first, count):
    ends = jnp.cumsum(lengths)
    starts = ends - lengths
    index = first + jnp.arange(count, dtype=jnp.int32)
    document = jnp.sum((index[None, :] >= ends[:, None]).astype(jnp.int32), axis=0)
    chosen = document[None, :] == jnp.arange(lengths.shape[0], dtype=jnp.int32)[:, None]
    start_of = jnp.sum(jnp.where(chosen, starts[:, None], 0), axis=0)
    return index - start_of


def doc_start(ends_ref, base, rows):
    start = base if jnp.ndim(rows) == 0 else jnp.zeros_like(rows) + base
    for j in range(ends_ref.shape[0]):
        end = ends_ref[j]
        start = jnp.where(rows >= end, jnp.maximum(start, end), start)
    return start


def put_lanes(rows, column, lane):
    at = lax.broadcasted_iota(jnp.int32, rows.shape, 1)
    high = column.astype(BF16).astype(F32)
    rest = column - high
    mid = rest.astype(BF16).astype(F32)
    low = rest - mid
    wide = rows.astype(F32)
    wide = jnp.where(at == lane, high, wide)
    wide = jnp.where(at == lane + 1, mid, wide)
    return jnp.where(at == lane + 2, low, wide).astype(BF16)


def block_ranges(first_row, rows, block, low, last_low, key_base, key_count):
    begin = (jnp.maximum(low, key_base) - key_base) // block
    stop = jnp.minimum((first_row + rows - key_base + block - 1) // block, key_count // block)
    inner = jnp.minimum(jnp.maximum((last_low - key_base + block - 1) // block, begin), stop)
    diagonal = jnp.minimum(jnp.maximum((first_row - key_base) // block, inner), stop)
    return begin, inner, diagonal, stop


def stack_heads(ref, kv, group):
    parts = [ref[:, (kv * group + g) * LANES : (kv * group + g + 1) * LANES] for g in range(group)]
    return jnp.concatenate(parts, axis=0)


def row_marks(ends_ref, base, first_row, bq, group):
    rows = lax.broadcasted_iota(jnp.int32, (1, bq), 1) + first_row
    starts = doc_start(ends_ref, base, rows)
    return jnp.concatenate([rows] * group, axis=1), jnp.concatenate([starts] * group, axis=1)


def widen(dense_ref, spread_ref, mark_ref, wide_ref):
    @pl.when(pl.program_id(0) == 0)
    def _():
        wide = dot(dense_ref[...], spread_ref[...]) + mark_ref[...]
        wide_ref[...] = wide.astype(BF16)

    return wide_ref


def attention_forward_kernel(
    first, key_base, tokens, bq, bk, head_dim, group, ends_ref, base_ref, q_ref, kv_ref, *rest
):
    if first:
        max_ref, acc_ref = rest
    else:
        spread_ref, mark_ref, sel_ref, max_in, acc_in, o_ref, qa_ref, max_ref, acc_ref, wide = rest
        kv_ref = widen(kv_ref, spread_ref, mark_ref, wide)
    first_row = tokens + pl.program_id(0) * bq
    base = base_ref[0]
    low = doc_start(ends_ref, base, first_row)
    last_low = doc_start(ends_ref, base, first_row + bq - 1)
    rows, starts = row_marks(ends_ref, base, first_row, bq, group)
    kv_heads = kv_ref.shape[1] // LANES // 2
    unit = LOG2E / math.sqrt(head_dim)
    queries = [stack_heads(q_ref, h, group) for h in range(kv_heads)]
    if first:
        max_ref[...] = jnp.full(max_ref.shape, NEGATIVE, F32)
        acc_ref[...] = jnp.zeros(acc_ref.shape, F32)
    else:
        max_ref[...] = max_in[...]
        acc_ref[...] = acc_in[...]

    def body(masked, index, carry):
        at = pl.multiple_of(index * bk, bk)
        if masked:
            keys = lax.broadcasted_iota(jnp.int32, (bk, group * bq), 0) + (at + key_base)
            keep = (keys <= rows) & (keys >= starts)
        for h in range(kv_heads):
            key = kv_ref[pl.ds(at, bk), h * LANES : (h + 1) * LANES]
            value = kv_ref[pl.ds(at, bk), (kv_heads + h) * LANES : (kv_heads + h + 1) * LANES]
            scores = dot(key, queries[h], NT)
            if masked:
                scores = jnp.where(keep, scores, NEGATIVE)
            old = max_ref[0, h]
            new = jnp.maximum(old, jnp.max(scores, axis=0, keepdims=True))
            probs = jnp.exp2((scores - new) * unit)
            if masked:
                probs = jnp.where(keep, probs, 0.0)
            acc_ref[0, h] = acc_ref[0, h] * jnp.exp2((old - new) * unit) + dot(
                value, probs.astype(BF16), TN
            )
            max_ref[0, h] = new
        return carry

    begin, inner, diagonal, stop = block_ranges(
        first_row, bq, bk, low, last_low, key_base, kv_ref.shape[0]
    )
    lax.fori_loop(begin, inner, functools.partial(body, True), 0)
    lax.fori_loop(inner, diagonal, functools.partial(body, False), 0)
    lax.fori_loop(diagonal, stop, functools.partial(body, True), 0)
    if first:
        return
    outs = []
    for h in range(kv_heads):
        acc = acc_ref[0, h]
        total = acc[head_dim : head_dim + 1, :]
        out = jnp.transpose(acc * (1.0 / total)).astype(BF16)
        logsum = jnp.broadcast_to(max_ref[0, h] + jnp.log2(total) * (1.0 / unit), (8, group * bq))
        marked = put_lanes(queries[h], jnp.transpose(logsum)[:, :1], head_dim // 2)
        for g in range(group):
            head = h * group + g
            qa_ref[:, head * LANES : (head + 1) * LANES] = marked[g * bq : (g + 1) * bq]
            outs.append(out[g * bq : (g + 1) * bq])
    o_ref[...] = dot(jnp.concatenate(outs, axis=1), sel_ref[...]).astype(BF16)


def attention_forward(ends, base, q, kv, head_dim, key_base, state=None, extra=None):
    tokens, width = q.shape
    kv_heads = (kv if state is None else extra[0]).shape[1] // LANES // 2
    group = width // LANES // kv_heads
    bq = bk = math.gcd(tokens, 512)
    steps = tokens // bq
    whole = lambda a: pl.BlockSpec(a.shape, lambda i, *_: (0, 0))
    row = lambda w: pl.BlockSpec((bq, w), lambda i, *_: (i, 0))
    shapes = [(steps, kv_heads, 1, group * bq), (steps, kv_heads, LANES, group * bq)]
    kept = [pl.BlockSpec((1,) + a[1:], lambda i, *_: (i, 0, 0, 0)) for a in shapes]
    pairs = tokens * tokens * group * kv_heads // 2
    if state is None:
        in_specs, operands = [row(width), whole(kv)], (q, kv)
        out_specs, out_shape = kept, [jax.ShapeDtypeStruct(a, F32) for a in shapes]
        scratch = []
    else:
        select = extra[2]
        in_specs = [row(width), whole(kv)] + [whole(a) for a in extra] + kept
        operands = (q, kv) + tuple(extra) + tuple(state)
        out_specs = [row(select.shape[1]), row(width)]
        out_shape = [
            jax.ShapeDtypeStruct((tokens, select.shape[1]), BF16),
            jax.ShapeDtypeStruct(q.shape, BF16),
        ]
        scratch = [pltpu.VMEM((1,) + a[1:], F32) for a in shapes]
        scratch.append(pltpu.VMEM((tokens, extra[0].shape[1]), BF16))
    return pl.pallas_call(
        functools.partial(
            attention_forward_kernel, state is None, key_base, tokens, bq, bk, head_dim, group
        ),
        grid_spec=pltpu.PrefetchScalarGridSpec(
            num_scalar_prefetch=2, grid=(steps,), in_specs=in_specs, out_specs=out_specs,
            scratch_shapes=scratch,
        ),
        out_shape=out_shape,
        compiler_params=pltpu.CompilerParams(vmem_limit_bytes=40 << 20),
        cost_estimate=pl.CostEstimate(
            flops=pairs * 1024, bytes_accessed=8 << 20, transcendentals=pairs
        ),
        name="attention_forward",
    )(ends, base, *operands)


def attention_backward_kernel(
    first, key_base, tokens, bq, bk, head_dim, group,
    ends_ref, base_ref, qa_ref, do_ref, o_ref, kv_ref, spread_ref, *rest
):
    if first:
        widen_ref, mark_ref, dq_ref, dkv_ref, dk_acc, dv_acc, dq_acc, wide = rest
        kv_ref = widen(kv_ref, widen_ref, mark_ref, wide)
    else:
        part_ref, cos_ref, sin_ref, sel_ref, dq_ref, dkv_ref, dk_acc, dv_acc, dq_acc = rest
    step = pl.program_id(0)
    first_row = tokens + step * bq
    base = base_ref[0]
    low = doc_start(ends_ref, base, first_row)
    last_low = doc_start(ends_ref, base, first_row + bq - 1)
    kv_heads = kv_ref.shape[1] // LANES // 2
    scale = 1.0 / math.sqrt(head_dim)
    unit = LOG2E * scale
    begin, inner, diagonal, stop = block_ranges(
        first_row, bq, bk, low, last_low, key_base, kv_ref.shape[0]
    )

    @pl.when(step == 0)
    def _():
        dk_acc[...] = jnp.zeros(dk_acc.shape, F32)
        dv_acc[...] = jnp.zeros(dv_acc.shape, F32)

    if first:
        dq_acc[...] = jnp.zeros(dq_acc.shape, F32)
    else:
        for h in range(kv_heads):
            dq_acc[h] = stack_heads(part_ref, h, group)

    @pl.when(begin < stop)
    def _():
        rows, starts = row_marks(ends_ref, base, first_row, bq, group)
        grads_wide = dot(do_ref[...], spread_ref[...])
        outs_wide = dot(o_ref[...], spread_ref[...])
        queries, grads = [], []
        for h in range(kv_heads):
            queries.append(stack_heads(qa_ref, h, group))
            grad = stack_heads(grads_wide, h, group)
            inner_sum = jnp.sum(grad * stack_heads(outs_wide, h, group), axis=1, keepdims=True)
            grads.append(put_lanes(grad, -inner_sum, head_dim))

        def body(masked, index, carry):
            at = pl.multiple_of(index * bk, bk)
            if masked:
                keys = lax.broadcasted_iota(jnp.int32, (bk, group * bq), 0) + (at + key_base)
                keep = (keys <= rows) & (keys >= starts)
            for h in range(kv_heads):
                key = kv_ref[pl.ds(at, bk), h * LANES : (h + 1) * LANES]
                value = kv_ref[pl.ds(at, bk), (kv_heads + h) * LANES : (kv_heads + h + 1) * LANES]
                probs = jnp.exp2(dot(key, queries[h], NT) * unit)
                if masked:
                    probs = jnp.where(keep, probs, 0.0)
                slope = (probs * dot(value, grads[h], NT)).astype(BF16)
                dv_acc[h, pl.ds(at, bk), :] += dot(probs.astype(BF16), grads[h])
                dk_acc[h, pl.ds(at, bk), :] += dot(slope, queries[h])
                dq_acc[h] += dot(slope, key, TN)
            return carry

        lax.fori_loop(begin, inner, functools.partial(body, True), 0)
        lax.fori_loop(inner, diagonal, functools.partial(body, False), 0)
        lax.fori_loop(diagonal, stop, functools.partial(body, True), 0)

    outs = []
    for h in range(kv_heads):
        for g in range(group):
            grad = dq_acc[h, g * bq : (g + 1) * bq, :]
            if first:
                dq_ref[:, (h * group + g) * LANES : (h * group + g + 1) * LANES] = grad
            else:
                grad = grad * scale
                outs.append(
                    (grad * cos_ref[...] - pltpu.roll(grad, LANES // 2, 1) * sin_ref[...]).astype(BF16)
                )
    if not first:
        dq_ref[...] = dot(jnp.concatenate(outs, axis=1), sel_ref[...]).astype(BF16)

    @pl.when(step == pl.num_programs(0) - 1)
    def _():
        for h in range(kv_heads):
            dkv_ref[:, h * LANES : (h + 1) * LANES] = (dk_acc[h] * scale).astype(dkv_ref.dtype)
            dkv_ref[:, (kv_heads + h) * LANES : (kv_heads + h + 1) * LANES] = dv_acc[h].astype(dkv_ref.dtype)


def attention_backward(ends, base, qa, grad, out, kv, spread, head_dim, key_base, rest=None, extra=None):
    tokens, width = qa.shape
    keys = kv.shape[0]
    kv_lanes = (kv if rest is not None else extra[0]).shape[1]
    kv_heads = kv_lanes // LANES // 2
    group = width // LANES // kv_heads
    bq = bk = math.gcd(tokens, 512)
    whole = lambda a: pl.BlockSpec(a.shape, lambda i, *_: (0, 0))
    row = lambda w: pl.BlockSpec((bq, w), lambda i, *_: (i, 0))
    pairs = tokens * tokens * group * kv_heads // 2
    in_specs = [row(width), row(grad.shape[1]), row(out.shape[1]), whole(kv), whole(spread)]
    operands = (qa, grad, out, kv, spread)
    scratch = []
    if rest is None:
        in_specs += [whole(a) for a in extra]
        operands += tuple(extra)
        scratch = [pltpu.VMEM((keys, kv_lanes), BF16)]
        dq_width, dq_type, dkv_type = width, F32, BF16
    else:
        part, cos, sin, select = rest
        in_specs += [row(width), row(LANES), row(LANES), whole(select)]
        operands += (part, cos, sin, select)
        dq_width, dq_type, dkv_type = select.shape[1], BF16, F32
    return pl.pallas_call(
        functools.partial(
            attention_backward_kernel, rest is None, key_base, tokens, bq, bk, head_dim, group
        ),
        grid_spec=pltpu.PrefetchScalarGridSpec(
            num_scalar_prefetch=2,
            grid=(tokens // bq,),
            in_specs=in_specs,
            out_specs=[row(dq_width), pl.BlockSpec((keys, kv_lanes), lambda i, *_: (0, 0))],
            scratch_shapes=[
                pltpu.VMEM((kv_heads, keys, LANES), F32),
                pltpu.VMEM((kv_heads, keys, LANES), F32),
                pltpu.VMEM((kv_heads, group * bq, LANES), F32),
            ]
            + scratch,
        ),
        out_shape=[
            jax.ShapeDtypeStruct((tokens, dq_width), dq_type),
            jax.ShapeDtypeStruct((keys, kv_lanes), dkv_type),
        ],
        compiler_params=pltpu.CompilerParams(vmem_limit_bytes=48 << 20),
        cost_estimate=pl.CostEstimate(
            flops=pairs * 2560, bytes_accessed=12 << 20, transcendentals=pairs
        ),
        name="attention_backward",
    )(ends, base, qa, grad, out, kv, spread, *operands[5:])


MESH = pl.DeviceIdType.MESH


class Ranks:
    def __init__(self, count):
        self.count, self.chips = count, count // 2
        self.me = lax.axis_index("tp")
        self.chip, self.core = self.me // 2, self.me % 2

    def peer(self, k, j):
        return lax.rem(self.chip + k + self.chips, self.chips) * 2 + lax.rem(self.core + j, 2)

    def others(self):
        return [(k, j) for k in range(self.chips) for j in range(2) if k or j]

    def barrier(self):
        sem = pltpu.get_barrier_semaphore()
        for k, j in self.others():
            pl.semaphore_signal(sem, inc=1, device_id={"tp": self.peer(k, j)}, device_id_type=MESH)
        pl.semaphore_wait(sem, self.count - 1)


def remote(src, dst, send, recv, rank):
    return pltpu.make_async_remote_copy(
        src_ref=src, dst_ref=dst, send_sem=send, recv_sem=recv, device_id={"tp": rank},
        device_id_type=MESH,
    )


def row_mean(x):
    return jnp.sum(x, axis=-1, keepdims=True) * (1.0 / x.shape[-1])


class GatherRows:
    def __init__(self, ranks, rows_ref, out_ref, send, recv, local):
        own = rows_ref.shape[0]
        self.ranks, self.send, self.recv = ranks, send, recv
        self.at = lambda rank: out_ref.at[pl.ds(pl.multiple_of(rank * own, own), own)]
        self.keep = pltpu.make_async_copy(rows_ref, self.at(ranks.me), local)
        self.copies = []
        for k in list(range(1, ranks.chips)) + [0]:
            peer = ranks.peer(k, 0) if k else ranks.peer(0, 1)
            self.copies.append(remote(rows_ref, self.at(ranks.me), send.at[0, k], recv.at[0, k], peer))

    def start(self):
        for copy in self.copies:
            copy.start()
        self.keep.start()

    def finish(self):
        ranks, passed = self.ranks, []
        for k, copy in zip(range(1, ranks.chips), self.copies):
            copy.wait_recv()
            held = self.at(ranks.peer(-k, 0))
            passed.append(
                remote(held, held, self.send.at[1, k], self.recv.at[1, k], ranks.peer(0, 1))
            )
            passed[-1].start()
        self.copies[-1].wait_recv()
        for copy in self.copies:
            copy.wait_send()
        for copy in passed:
            copy.wait()
        self.keep.wait()


def both_cores(ranks, blocks, out_ref, send, recv, local):
    own = blocks[0].shape[0]
    copies = []
    for k, block in enumerate(blocks):
        there = out_ref.at[pl.ds(pl.multiple_of(ranks.peer(-k, 0) * own, own), own)]
        copies.append(remote(block, there, send.at[k], recv.at[k], ranks.peer(0, 1)))
        copies.append(pltpu.make_async_copy(block, there, local.at[k]))
    return copies


def mix_kernel(count, att_ref, x_ref, gain_ref, *rest):
    chips = count // 2
    blocks, rest = rest[:chips], rest[chips:]
    (
        n2_ref, mid_ref, other_ref, heads, rows_in, rows_out, others, a_send, a_recv, b_send, b_recv,
        g_send, g_recv, local,
    ) = rest
    ranks = Ranks(count)
    own = rows_in.shape[0]
    mine_at = pl.ds(pl.multiple_of(ranks.me * own, own), own)
    fetch = pltpu.make_async_copy(x_ref.at[mine_at], rows_in, local.at[0])
    fetch.start()
    mine = pltpu.make_async_copy(att_ref.at[mine_at], heads.at[0], local.at[1])
    mine.start()
    ranks.barrier()
    copies = {}
    for k, j in ranks.others()[::-1]:
        peer, slot = ranks.peer(k, j), 2 * k + j
        copies[slot] = remote(
            att_ref.at[pl.ds(pl.multiple_of(peer * own, own), own)], heads.at[slot],
            a_send.at[slot], a_recv.at[slot], peer,
        )
        copies[slot].start()
    swaps = [
        remote(blocks[k], others.at[k], b_send.at[k], b_recv.at[k], ranks.peer(0, 1))
        for k in range(chips)
    ]
    for copy in swaps:
        copy.start()
    fetch.wait()
    mine.wait()
    mid_ref[...] = rows_in[...] + dot(heads[0], blocks[0][...], NT)
    keeps = []
    for slot in range(1, count):
        k = slot // 2
        if slot % 2:
            swaps[k].wait_recv()
            keeps.append(pltpu.make_async_copy(others.at[k], other_ref.at[k], local.at[2 + k]))
            keeps[-1].start()
        copies[slot].wait_recv()
        mid_ref[...] += dot(heads[slot], others[k] if slot % 2 else blocks[k][...], NT)
    mid = mid_ref[...]
    factor = lax.rsqrt(row_mean(mid * mid) + EPSILON)
    rows_out[...] = (mid * factor * gain_ref[...]).astype(BF16)
    gather = GatherRows(ranks, rows_out, n2_ref, g_send, g_recv, local.at[0])
    gather.start()
    for slot in range(1, count):
        copies[slot].wait_send()
    for copy in swaps:
        copy.wait_send()
    for copy in keeps:
        copy.wait()
    gather.finish()


def mix(count, attended, layer_input, gain, blocks):
    tokens, model = layer_input.shape
    own = tokens // count
    chips = count // 2
    width = attended.shape[1]
    vmem, hbm = pl.BlockSpec(memory_space=pltpu.VMEM), pl.BlockSpec(memory_space=pl.ANY)
    sem = pltpu.SemaphoreType.DMA
    return pl.pallas_call(
        functools.partial(mix_kernel, count),
        in_specs=[hbm, hbm, vmem] + [vmem] * chips,
        out_specs=[hbm, vmem, hbm],
        out_shape=[
            jax.ShapeDtypeStruct((tokens, model), BF16),
            jax.ShapeDtypeStruct((own, model), F32),
            jax.ShapeDtypeStruct((chips, model, width), BF16),
        ],
        scratch_shapes=[
            pltpu.VMEM((count, own, width), BF16),
            pltpu.VMEM((own, model), F32),
            pltpu.VMEM((own, model), BF16),
            pltpu.VMEM((chips, model, width), BF16),
            sem((count,)), sem((count,)), sem((chips,)), sem((chips,)), sem((2, chips)),
            sem((2, chips)), sem((2 + chips,)),
        ],
        compiler_params=pltpu.CompilerParams(
            vmem_limit_bytes=40 << 20, collective_id=1, has_side_effects=True
        ),
        cost_estimate=pl.CostEstimate(
            flops=2 * tokens * model * model, bytes_accessed=150 << 20, transcendentals=0
        ),
        name="mix_heads",
    )(attended, layer_input, gain, *blocks)


def scatter_order(ranks, halves, own, i):
    k = lax.rem(i // halves + 1, ranks.chips)
    half = lax.rem(i, halves)
    rows = own // halves
    at = lambda j: pl.multiple_of(ranks.peer(k, j) * own + half * rows, rows)
    return k, half, at(0), at(1)


def half_rows(shard, which, half):
    return pl.ds(pl.multiple_of((shard * 2 + which) * half, half), half)


def swap_halves(src, dst, send, recv, shards):
    piece = lax.axis_index("ctx")
    half = src.shape[0] // (2 * shards)
    return [
        pltpu.make_async_remote_copy(
            src_ref=src.at[half_rows(s, 1 - piece, half)], dst_ref=dst.at[pl.ds(s * half, half)],
            send_sem=send.at[s], recv_sem=recv.at[s], device_id={"ctx": 1 - piece},
            device_id_type=MESH,
        )
        for s in range(shards)
    ]


def signal_piece(count):
    ranks = Ranks(count)
    sem = pltpu.get_barrier_semaphore()
    for k, j in ranks.others():
        pl.semaphore_signal(sem, inc=1, device_id={"tp": ranks.peer(k, j)}, device_id_type=MESH)
    pl.semaphore_signal(sem, inc=1, device_id={"ctx": 1 - lax.axis_index("ctx")}, device_id_type=MESH)
    pl.semaphore_wait(sem, count)


def feedforward_kernel(count, n2_ref, cot_ref, mid_ref, gain_ref, other_in, weight_ref, *rest):
    blocks_in, rest = rest[: count // 2], rest[count // 2 :]
    (
        ffb_ref, mg_ref, bg_ref, gain_grad_ref, da_ref, grad_ref, grads_ref,
        gate_w, up_w, down_w, n2, fg, hid, gu, rows_in, ffb_out,
        c_send, c_recv, y_send, y_recv, f_send, f_recv, heads, other_ref, blocks,
        w_sem, in_sem, out_sem, cs, cr, ys, yr, fs, fr, hs, hr, local,
    ) = rest
    ranks = Ranks(count)
    own = mg_ref.shape[0]
    halves = 2
    rows = own // halves
    steps = ranks.chips * halves
    width = gate_w.shape[1]
    model = n2.shape[1]
    loads = [pltpu.make_async_copy(n2_ref, n2, w_sem.at[3])] + [
        pltpu.make_async_copy(weight_ref.at[:, pl.ds(w * width, width)], full, w_sem.at[w])
        for w, full in enumerate((gate_w, up_w, down_w))
    ]
    late = [pltpu.make_async_copy(other_in, other_ref, w_sem.at[4])] + [
        pltpu.make_async_copy(block, blocks.at[k], w_sem.at[5 + k])
        for k, block in enumerate(blocks_in)
    ]
    for load in loads + late:
        load.start()

    def read(at, slot):
        return pltpu.make_async_copy(cot_ref.at[pl.ds(at, rows)], rows_in.at[slot], in_sem.at[slot])

    def tile(at, slot, begin):
        here = pl.ds(at, rows)

        def ready(n):
            if begin is not None:
                @pl.when(begin)
                def _():
                    loads[n].wait()

        ready(0)
        ready(1)
        n = n2[here, :]
        grad = rows_in[slot].astype(BF16)
        fg[here, :] = grad
        gate = dot(n, gate_w[...])
        ready(2)
        up = dot(n, up_w[...])
        ready(3)
        back = dot(grad, down_w[...])
        sig = 1.0 / (1.0 + jnp.exp(-gate))
        act = gate * sig
        hidden = (act * up).astype(BF16)
        hid[here, :] = hidden
        gg = (back * up * (sig * (1.0 + gate * (1.0 - sig)))).astype(BF16)
        gu[here, :width] = gg
        ug = (back * act).astype(BF16)
        gu[here, width:] = ug
        return dot(gg, gate_w[...], NT) + dot(ug, up_w[...], NT), dot(hidden, down_w[...], NT)

    read(scatter_order(ranks, halves, own, 0)[3], 0).start()
    ranks.barrier()
    neighbour = ranks.peer(0, 1)

    def to_core(i):
        slot = lax.rem(i, 2)
        return [
            remote(c_send.at[slot], c_recv.at[slot], cs.at[slot], cr.at[slot], neighbour),
            remote(f_send.at[slot], f_recv.at[slot], fs.at[slot], fr.at[slot], neighbour),
        ]

    def to_chip(i, k):
        return remote(y_send.at[i], y_recv.at[i], ys.at[i], yr.at[i], ranks.peer(k, 0))

    def ffb_write(i):
        return pltpu.make_async_copy(ffb_out, ffb_ref.at[i], out_sem.at[0])

    def step(i, carry):
        k, u, at_mine, at_other = scatter_order(ranks, halves, own, i)
        slot = lax.rem(i, 2)
        read(at_mine, 1).start()
        read(at_other, 0).wait()
        grad, forward = tile(at_other, 0, i == 0)

        @pl.when(i + 1 < steps)
        def _():
            read(scatter_order(ranks, halves, own, i + 1)[3], 0).start()

        @pl.when(i > 1)
        def _():
            for copy in to_core(i):
                copy.wait_send()

        c_send[slot] = grad.astype(BF16)
        f_send[slot] = forward.astype(BF16)
        for copy in to_core(i):
            copy.start()
        read(at_mine, 1).wait()
        grad, forward = tile(at_mine, 1, None)

        @pl.when(i > 0)
        def _():
            ffb_write(i).wait()

        for copy in to_core(i):
            copy.wait_recv()
        grad = grad + c_recv[slot].astype(F32)
        ffb_out[...] = (forward + f_recv[slot].astype(F32)).astype(BF16)
        ffb_write(i).start()

        @pl.when(k != 0)
        def _():
            y_send[i] = grad.astype(BF16)
            to_chip(i, k).start()

        @pl.when(k == 0)
        def _():
            mg_ref[pl.ds(pl.multiple_of(u * rows, rows), rows), :] = grad

        return carry

    lax.fori_loop(0, steps, step, 0)
    mine_at = pl.multiple_of(ranks.me * own, own)
    fetch = lambda u: [
        pltpu.make_async_copy(mid_ref.at[pl.ds(u * rows, rows)], rows_in.at[0], in_sem.at[0]),
        read(mine_at + u * rows, 1),
    ]
    for copy in fetch(0):
        copy.start()
    cols = math.gcd(model, 384)
    writes = []

    def product(left, right, full, dst, n):
        for d in range(model // cols):
            full[d * cols : (d + 1) * cols, :] = dot(
                left[:, d * cols : (d + 1) * cols], right, TN
            ).astype(BF16)
        writes.append(pltpu.make_async_copy(full, dst, out_sem.at[1 + n]))
        writes[-1].start()

    product(n2, gu[:, :width], gate_w, grad_ref, 0)
    gain = gain_ref[...]
    gain_total = None
    for u in range(halves):
        here = slice(u * rows, (u + 1) * rows)
        total = mg_ref[here, :]
        for k in range(1, ranks.chips):
            i = (k - 1) * halves + u
            to_chip(i, k).wait_recv()
            total = total + y_recv[i].astype(F32)
        for copy in fetch(u):
            copy.wait()
        mid = rows_in[0]
        factor = lax.rsqrt(row_mean(mid * mid) + EPSILON)
        hat = mid * factor
        term = jnp.sum(total * hat, axis=0, keepdims=True)
        gain_total = term if gain_total is None else gain_total + term
        inner = total * gain
        grad = rows_in[1] + factor * (inner - hat * row_mean(inner * hat))
        mg_ref[here, :] = grad
        bg_ref[here, :] = grad.astype(BF16)
        if u + 1 < halves:
            for copy in fetch(u + 1):
                copy.start()
    gain_grad_ref[...] = gain_total
    for load in late:
        load.wait()
    back = []
    for k, j in ranks.others()[::-1]:
        slot, peer = 2 * k + j, ranks.peer(-k, j)
        heads[slot] = dot(bg_ref[...], other_ref[k] if j else blocks[k]).astype(BF16)
        back.append(
            remote(heads.at[slot], da_ref.at[pl.ds(mine_at, own)], hs.at[slot], hr.at[slot], peer)
        )
        back[-1].start()
    heads[0] = dot(bg_ref[...], blocks[0]).astype(BF16)
    keep = pltpu.make_async_copy(heads.at[0], da_ref.at[pl.ds(mine_at, own)], local.at[0])
    keep.start()
    product(n2, gu[:, width:], up_w, grads_ref.at[:, pl.ds(0, width)], 1)
    product(fg, hid[...], down_w, grads_ref.at[:, pl.ds(width, width)], 2)
    for i in (steps - 2, steps - 1):
        for copy in to_core(i):
            copy.wait_send()
    for i in range(steps - halves):
        to_chip(i, i // halves + 1).wait_send()
    ffb_write(steps - 1).wait()
    for copy in back:
        copy.wait()
    keep.wait()
    for copy in writes:
        copy.wait()


def feedforward(count, n2, cotangent, middle, gain, weights, blocks, others):
    tokens, model = n2.shape
    own = tokens // count
    hidden = weights.shape[1] // 3
    width = blocks[0].shape[1]
    rows, steps = own // 2, count
    vmem, hbm = pl.BlockSpec(memory_space=pltpu.VMEM), pl.BlockSpec(memory_space=pl.ANY)
    sem = pltpu.SemaphoreType.DMA
    return pl.pallas_call(
        functools.partial(feedforward_kernel, count),
        in_specs=[hbm, hbm, hbm, vmem, hbm, hbm] + [hbm] * (count // 2),
        out_specs=[hbm, vmem, vmem, vmem, hbm, hbm, hbm],
        out_shape=[
            jax.ShapeDtypeStruct((steps, rows, model), BF16),
            jax.ShapeDtypeStruct((own, model), F32),
            jax.ShapeDtypeStruct((own, model), BF16),
            jax.ShapeDtypeStruct((1, model), F32),
            jax.ShapeDtypeStruct((tokens, width), BF16),
            jax.ShapeDtypeStruct((model, hidden), BF16),
            jax.ShapeDtypeStruct((model, 2 * hidden), BF16),
        ],
        scratch_shapes=[pltpu.VMEM((model, hidden), BF16)] * 3
        + [
            pltpu.VMEM((tokens, model), BF16),
            pltpu.VMEM((tokens, model), BF16),
            pltpu.VMEM((tokens, hidden), BF16),
            pltpu.VMEM((tokens, 2 * hidden), BF16),
            pltpu.VMEM((2, rows, model), F32),
            pltpu.VMEM((rows, model), BF16),
        ]
        + [pltpu.VMEM((2, rows, model), BF16)] * 2
        + [pltpu.VMEM((steps - 2, rows, model), BF16)] * 2
        + [pltpu.VMEM((2, rows, model), BF16)] * 2
        + [
            pltpu.VMEM((count, own, width), BF16),
            pltpu.VMEM(others.shape, BF16),
            pltpu.VMEM(others.shape, BF16),
            sem((5 + count // 2,)), sem((2,)), sem((4,)),
            sem((2,)), sem((2,)), sem((steps - 2,)), sem((steps - 2,)),
            sem((2,)), sem((2,)), sem((count,)), sem((count,)), sem((1,)),
        ],
        compiler_params=pltpu.CompilerParams(
            vmem_limit_bytes=63 << 20, collective_id=2, has_side_effects=True
        ),
        cost_estimate=pl.CostEstimate(
            flops=2 * tokens * model * hidden * 9, bytes_accessed=280 << 20,
            transcendentals=tokens * hidden,
        ),
        name="feed_forward",
    )(n2, cotangent, middle, gain, others, weights, *blocks)


def shard_copy(src, dst, send, recv, axis, index):
    return pltpu.make_async_remote_copy(
        src_ref=src, dst_ref=dst, send_sem=send, recv_sem=recv, device_id={axis: index},
        device_id_type=MESH,
    )


def begin_kernel(
    shards, x_ref, qkv_ref, wo_ref, gains_ref, order_ref, n_ref, qkv_full_ref, wo_full_ref, gain_out_ref,
    qkv_full, wo_full, normed, rows_in, gain_buf, zs, zr, xs, xr, gs, gr, own_sem, in_sem, out_sem,
):
    del order_ref
    me, piece = lax.axis_index("fsdp"), lax.axis_index("ctx")
    fulls, sources = (qkv_full, wo_full), (qkv_ref, wo_ref)
    shard = qkv_ref.shape[0]
    half = shard // 2
    tokens = normed.shape[0]
    rows = rows_in.shape[1]
    steps = tokens // rows

    def read(i):
        return pltpu.make_async_copy(
            x_ref.at[pl.ds(i * rows, rows)], rows_in.at[i % 2], in_sem.at[i % 2]
        )

    read(0).start()
    keeps = [
        pltpu.make_async_copy(src, full.at[pl.ds(pl.multiple_of(me * shard, shard), shard)], own_sem.at[a])
        for a, (src, full) in enumerate(zip(sources, fulls))
    ]
    for copy in keeps:
        copy.start()
    keep_gain = pltpu.make_async_copy(gains_ref, gain_buf.at[me], own_sem.at[2])
    keep_gain.start()
    barrier = pltpu.get_barrier_semaphore()
    for k in range(1, shards):
        pl.semaphore_signal(
            barrier, inc=1, device_id={"fsdp": lax.rem(me + k, shards)}, device_id_type=MESH
        )
    pl.semaphore_signal(barrier, inc=1, device_id={"ctx": 1 - piece}, device_id_type=MESH)
    pl.semaphore_wait(barrier, shards)

    def place(a, s, which):
        return fulls[a].at[half_rows(s, which, half)]

    def own_half(a):
        return sources[a].at[pl.ds(pl.multiple_of(piece * half, half), half)]

    def along(a, s, step, mine):
        way = 0 if step > 0 else 1
        src = own_half(a) if mine else place(a, s, piece)
        return shard_copy(
            src, place(a, s, piece), zs.at[a, way, s], zr.at[a, s], "fsdp",
            lax.rem(me + step + shards, shards),
        )

    def across(a, s):
        return shard_copy(
            place(a, s, piece), place(a, s, piece), xs.at[a, s], xr.at[a, s], "ctx", 1 - piece
        )

    gain_copies = [
        shard_copy(
            gains_ref, gain_buf.at[me], gs.at[k], gr.at[k], "fsdp", lax.rem(me + k, shards)
        )
        for k in range(1, shards)
    ]
    for copy in gain_copies:
        copy.start()
    for a in range(2):
        for step, there in ((1, me < shards - 1), (-1, me > 0)):
            @pl.when(there)
            def _():
                along(a, me, step, True).start()

    for copy in gain_copies:
        copy.wait()
    keep_gain.wait()
    gain_out_ref[...] = jnp.concatenate([gain_buf[s] for s in range(shards)], axis=1)
    for i in range(steps):
        if i + 1 < steps:
            read(i + 1).start()
        read(i).wait()
        x = rows_in[i % 2]
        factor = lax.rsqrt(row_mean(x * x) + EPSILON)
        normed[i * rows : (i + 1) * rows, :] = (x * factor * gain_out_ref[0:1, :]).astype(BF16)
    write_normed = pltpu.make_async_copy(normed, n_ref, out_sem.at[0])
    write_normed.start()

    def arrival(d, step):
        s = me - step * d
        there = (s >= 0) & (s <= shards - 1)
        s = jnp.minimum(jnp.maximum(s, 0), shards - 1)
        onward = (me < shards - 1) if step > 0 else (me > 0)

        @pl.when(there)
        def _():
            for a in range(2):
                along(a, s, step, False).wait_recv()
                across(a, s).start()

        @pl.when(there & onward)
        def _():
            for a in range(2):
                along(a, s, step, False).start()

    for d in range(1, shards):
        arrival(d, 1)
        arrival(d, -1)
    for copy in keeps:
        copy.wait()
    for k in range(1, shards):
        s = lax.rem(me + k, shards)
        for a in range(2):
            across(a, s).wait_recv()
    writes = [
        pltpu.make_async_copy(qkv_full, qkv_full_ref, out_sem.at[1]),
        pltpu.make_async_copy(wo_full, wo_full_ref, out_sem.at[2]),
    ]
    for copy in writes:
        copy.start()
    for a in range(2):
        for s in range(shards):
            @pl.when((me >= s) & (me < shards - 1))
            def _():
                along(a, s, 1, False).wait_send()

            @pl.when((me <= s) & (me > 0))
            def _():
                along(a, s, -1, False).wait_send()

        for k in range(1, shards):
            across(a, lax.rem(me + k, shards)).wait_send()
    write_normed.wait()
    for copy in writes:
        copy.wait()


def begin(shards, x, qkv, wo, gains, order):
    tokens, model = x.shape
    rows = math.gcd(tokens, 256)
    vmem, hbm = pl.BlockSpec(memory_space=pltpu.VMEM), pl.BlockSpec(memory_space=pl.ANY)
    sem = pltpu.SemaphoreType.DMA
    return pl.pallas_call(
        functools.partial(begin_kernel, shards),
        in_specs=[hbm, vmem, vmem, vmem, hbm],
        out_specs=[hbm, hbm, hbm, vmem],
        out_shape=[
            jax.ShapeDtypeStruct((tokens, model), BF16),
            jax.ShapeDtypeStruct((model, qkv.shape[1]), BF16),
            jax.ShapeDtypeStruct((model, wo.shape[1]), BF16),
            jax.ShapeDtypeStruct((gains.shape[0], model), F32),
        ],
        scratch_shapes=[
            pltpu.VMEM((model, qkv.shape[1]), BF16),
            pltpu.VMEM((model, wo.shape[1]), BF16),
            pltpu.VMEM((tokens, model), BF16),
            pltpu.VMEM((2, rows, model), F32),
            pltpu.VMEM((shards,) + gains.shape, F32),
            sem((2, 2, shards)), sem((2, shards)), sem((2, shards)), sem((2, shards)),
            sem((shards,)), sem((shards,)), sem((3,)), sem((2,)), sem((3,)),
        ],
        compiler_params=pltpu.CompilerParams(
            vmem_limit_bytes=48 << 20, collective_id=4, has_side_effects=True
        ),
        cost_estimate=pl.CostEstimate(flops=0, bytes_accessed=120 << 20, transcendentals=0),
        name="norm_and_gather",
    )(x, qkv, wo, gains, order)


def project_kernel(
    q_heads, n_ref, qkv_ref, spread_ref, cos_ref, sin_ref, krow_ref, vrow_ref, pick_ref, q_ref, kv_ref,
    dense_ref, wide
):
    @pl.when(pl.program_id(0) == 0)
    def _():
        model = qkv_ref.shape[0]
        block = math.gcd(model, 512)
        for r in range(0, model, block):
            wide[r : r + block, :] = dot(qkv_ref[r : r + block, :], spread_ref[...]).astype(BF16)

    kv_heads = kv_ref.shape[1] // LANES // 2
    cos, sin = cos_ref[...], sin_ref[...]
    out = dot(n_ref[...], wide[...])
    plain = []
    for h in range(q_heads + 2 * kv_heads):
        part = out[:, h * LANES : (h + 1) * LANES]
        if h < q_heads + kv_heads:
            part = part * cos + pltpu.roll(part, LANES // 2, 1) * sin
        if h < q_heads:
            q_ref[:, h * LANES : (h + 1) * LANES] = part.astype(BF16)
        else:
            plain.append(part.astype(BF16))
            part = part + (krow_ref[...] if h < q_heads + kv_heads else vrow_ref[...])
            kv_ref[:, (h - q_heads) * LANES : (h - q_heads + 1) * LANES] = part.astype(BF16)
    dense_ref[...] = dot(jnp.concatenate(plain, axis=1), pick_ref[...]).astype(BF16)


def project(normed, qkv, spread, cos, sin, krow, vrow, pick, q_heads, kv_heads):
    tokens, model = normed.shape
    wide = spread.shape[1]
    bm = math.gcd(tokens, 256)
    whole = lambda a: pl.BlockSpec(a.shape, lambda i: (0, 0))
    row = lambda w: pl.BlockSpec((bm, w), lambda i: (i, 0))
    return pl.pallas_call(
        functools.partial(project_kernel, q_heads),
        grid=(tokens // bm,),
        in_specs=[row(model), whole(qkv), whole(spread), row(LANES), row(LANES), whole(krow), whole(vrow),
            whole(pick)],
        out_specs=[row(q_heads * LANES), row(2 * kv_heads * LANES), row(pick.shape[1])],
        out_shape=[
            jax.ShapeDtypeStruct((tokens, q_heads * LANES), BF16),
            jax.ShapeDtypeStruct((tokens, 2 * kv_heads * LANES), BF16),
            jax.ShapeDtypeStruct((tokens, pick.shape[1]), BF16),
        ],
        scratch_shapes=[pltpu.VMEM((model, wide), BF16)],
        compiler_params=pltpu.CompilerParams(vmem_limit_bytes=40 << 20),
        cost_estimate=pl.CostEstimate(
            flops=2 * tokens * model * wide, bytes_accessed=16 << 20, transcendentals=0
        ),
        name="project_qkv",
    )(normed, qkv, spread, cos, sin, krow, vrow, pick)


def dense_kernel(
    chips, dq_ref, dkv_ref, after_ref, cos_ref, sin_ref, rotk_ref, valk_ref, att_ref, n_ref, *rest
):
    blocks, rest = rest[:chips], rest[chips:]
    dense_ref, grad_ref, normed, branch, send, recv, local = rest
    ranks = Ranks(2 * chips)
    fetch = pltpu.make_async_copy(n_ref, normed, local.at[chips])
    fetch.start()
    sem = pltpu.get_barrier_semaphore()
    pl.semaphore_signal(sem, inc=1, device_id={"tp": ranks.peer(0, 1)}, device_id_type=MESH)
    pl.semaphore_wait(sem, 1)
    copies = both_cores(ranks, blocks, branch, send, recv, local)
    for copy in copies:
        copy.start()
    width = dense_ref.shape[1]
    lanes = dkv_ref.shape[1] // 2
    cos, sin = cos_ref[...], sin_ref[...]
    turned = []
    for h in range(lanes // LANES):
        at = slice(h * LANES, (h + 1) * LANES)
        key = dkv_ref[:, at] + after_ref[:, at].astype(F32)
        turned.append((key * cos - pltpu.roll(key, LANES // 2, 1) * sin).astype(BF16))
    dk = dot(jnp.concatenate(turned, axis=1), rotk_ref[...]).astype(BF16)
    dv = (dkv_ref[:, lanes:] + after_ref[:, lanes:].astype(F32)).astype(BF16)
    dv = dot(dv, valk_ref[...]).astype(BF16)
    dense_ref[...] = jnp.concatenate([dq_ref[...], dk, dv], axis=1)
    fetch.wait()
    model = normed.shape[1]
    cols = math.gcd(model, 384)
    for d in range(0, model, cols):
        grad_ref[d : d + cols, :width] = dot(
            normed[:, d : d + cols], dense_ref[...], TN
        ).astype(BF16)
    for copy in copies:
        copy.wait()
    for d in range(0, model, cols):
        grad_ref[d : d + cols, width:] = dot(branch[:, d : d + cols], att_ref[...], TN).astype(BF16)


def dense_gradients(dq, dkv, after, cos, sin, rot_k, val_k, attended, normed, blocks):
    tokens, model = normed.shape
    chips = len(blocks)
    width = dq.shape[1] + 2 * rot_k.shape[1]
    total = width + attended.shape[1]
    vmem, hbm = pl.BlockSpec(memory_space=pltpu.VMEM), pl.BlockSpec(memory_space=pl.ANY)
    sem = pltpu.SemaphoreType.DMA
    return pl.pallas_call(
        functools.partial(dense_kernel, chips),
        in_specs=[vmem] * 8 + [hbm] * (1 + chips),
        out_specs=[vmem, vmem],
        out_shape=[
            jax.ShapeDtypeStruct((tokens, width), BF16),
            jax.ShapeDtypeStruct((model, total), BF16),
        ],
        scratch_shapes=[
            pltpu.VMEM((tokens, model), BF16),
            pltpu.VMEM((tokens, model), BF16),
            sem((chips,)), sem((chips,)), sem((chips + 1,)),
        ],
        compiler_params=pltpu.CompilerParams(
            vmem_limit_bytes=48 << 20, collective_id=5, has_side_effects=True
        ),
        cost_estimate=pl.CostEstimate(
            flops=2 * tokens * model * total, bytes_accessed=24 << 20, transcendentals=0
        ),
        name="dense_gradients",
    )(dq, dkv, after, cos, sin, rot_k, val_k, attended, normed, *blocks)


def close_kernel(
    count, shards, dense_ref, w_ref, x_ref, mg_ref, gain_ref, gain_two_ref, grad_ref, gate_ref, *rest
):
    layers, rest = rest[: count // 2], rest[count // 2 :]
    (
        out_ref, gain_grad_ref, half_ref, lay_ref, gate_out_ref, rows_in, rows_out, sums, c_send, c_recv, y_send,
        y_recv, x_mine, x_recv, gate_mine, gate_recv, t_send, t_recv, cs, cr, ys, yr, g_send, g_recv, xs, xr, x_sem,
        ls, lr, lay_sem, ts, tr, gate_sem, local,
    ) = rest
    ranks = Ranks(count)
    own = rows_in.shape[0]
    halves = 2
    rows = own // halves
    steps = ranks.chips * halves
    fetch = pltpu.make_async_copy(
        x_ref.at[pl.ds(pl.multiple_of(ranks.me * own, own), own)], rows_in, local.at[0]
    )
    fetch.start()
    def tile(at):
        return dot(dense_ref[pl.ds(at, rows), :], w_ref[...], NT)

    piece = lax.axis_index("ctx")
    half = grad_ref.shape[0] // (2 * shards)
    keeps = [
        pltpu.make_async_copy(
            grad_ref.at[half_rows(s, piece, half)], x_mine.at[pl.ds(s * half, half)], x_sem.at[s]
        )
        for s in range(shards)
    ]
    keeps.append(pltpu.make_async_copy(gate_ref, gate_mine, gate_sem.at[0]))
    for copy in keeps:
        copy.start()
    me = lax.axis_index("fsdp")
    barrier = pltpu.get_barrier_semaphore()
    for k, j in ranks.others():
        pl.semaphore_signal(barrier, inc=1, device_id={"tp": ranks.peer(k, j)}, device_id_type=MESH)
    for k in range(1, shards):
        pl.semaphore_signal(
            barrier, inc=1, device_id={"fsdp": lax.rem(me + k, shards)}, device_id_type=MESH
        )
    pl.semaphore_signal(barrier, inc=1, device_id={"ctx": 1 - piece}, device_id_type=MESH)
    pl.semaphore_wait(barrier, count + shards - 1)
    swaps = swap_halves(grad_ref, x_recv, xs, xr, shards)
    swaps.append(
        pltpu.make_async_remote_copy(
            src_ref=gate_ref, dst_ref=gate_recv, send_sem=gate_sem.at[1], recv_sem=gate_sem.at[2],
            device_id={"ctx": 1 - piece}, device_id_type=MESH,
        )
    )
    for copy in swaps:
        copy.start()
    forward = both_cores(ranks, layers, lay_ref, ls, lr, lay_sem)
    for copy in forward:
        copy.start()
    neighbour = ranks.peer(0, 1)

    def to_core(i):
        return remote(c_send.at[i], c_recv.at[i], cs.at[i], cr.at[i], neighbour)

    def to_chip(i, k):
        return remote(y_send.at[i], y_recv.at[i], ys.at[i], yr.at[i], ranks.peer(k, 0))

    def send_step(i, carry):
        k, u, at_mine, at_other = scatter_order(ranks, halves, own, i)
        c_send[i] = tile(at_other).astype(BF16)
        to_core(i).start()
        return carry

    def sum_step(i, carry):
        k, u, at_mine, at_other = scatter_order(ranks, halves, own, i)
        grad = tile(at_mine)
        to_core(i).wait_recv()
        grad = grad + c_recv[i].astype(F32)

        @pl.when(k != 0)
        def _():
            y_send[i] = grad.astype(BF16)
            to_chip(i, k).start()

        @pl.when(k == 0)
        def _():
            sums[u] = grad

        return carry

    lax.fori_loop(0, steps, send_step, 0)
    lax.fori_loop(0, steps, sum_step, 0)
    fetch.wait()
    gain = gain_ref[...]
    gain_total = None
    for u in range(halves):
        total = sums[u]
        for k in range(1, ranks.chips):
            i = (k - 1) * halves + u
            to_chip(i, k).wait_recv()
            total = total + y_recv[i].astype(F32)
        x = rows_in[u * rows : (u + 1) * rows]
        factor = lax.rsqrt(row_mean(x * x) + EPSILON)
        hat = x * factor
        term = jnp.sum(total * hat, axis=0, keepdims=True)
        gain_total = term if gain_total is None else gain_total + term
        inner = total * gain
        grad = mg_ref[u * rows : (u + 1) * rows] + factor * (inner - hat * row_mean(inner * hat))
        rows_out[u * rows : (u + 1) * rows] = grad.astype(BF16)
    gather = GatherRows(ranks, rows_out, out_ref, g_send, g_recv, local.at[0])
    gather.start()
    total = jnp.concatenate([gain_total, gain_two_ref[...], jnp.zeros((6, gain_total.shape[1]), F32)], axis=0)
    hops = [[{"tp": ranks.peer(0, 1)}], [{"tp": ranks.peer(k, 0)} for k in range(1, ranks.chips)]]
    hops += [[{"ctx": 1 - piece}], [{"fsdp": lax.rem(me + k, shards)} for k in range(1, shards)]]
    slot, sent = 0, []
    for n, peers in enumerate(hops):
        t_send[n] = total
        copies = []
        for peer in peers:
            copies.append(
                pltpu.make_async_remote_copy(
                    src_ref=t_send.at[n], dst_ref=t_recv.at[slot], send_sem=ts.at[slot],
                    recv_sem=tr.at[slot], device_id=peer, device_id_type=MESH,
                )
            )
            copies[-1].start()
            slot += 1
        for copy, at in zip(copies, range(slot - len(copies), slot)):
            copy.wait_recv()
            total = total + t_recv[at]
        sent += copies
    gain_grad_ref[...] = total
    for copy in sent:
        copy.wait_send()
    gather.finish()
    for copy in forward:
        copy.wait()
    for s in range(shards):
        keeps[s].wait()
        swaps[s].wait_recv()
        here = slice(s * half, (s + 1) * half)
        half_ref[here, :] = (x_mine[here, :].astype(F32) + x_recv[here, :].astype(F32)).astype(BF16)
    keeps[shards].wait()
    swaps[shards].wait_recv()
    gate_out_ref[...] = gate_mine[...].astype(F32) + gate_recv[...].astype(F32)
    for copy in swaps:
        copy.wait_send()
    for i in range(steps):
        to_core(i).wait_send()
    for i in range(steps - halves):
        to_chip(i, i // halves + 1).wait_send()


def close(count, shards, dense, weight, layer_input, middle_grad, gain, gain_two, grad, gate, layers):
    tokens, model = layer_input.shape
    own = tokens // count
    rows, steps, chips = own // 2, count, count // 2
    vmem, hbm = pl.BlockSpec(memory_space=pltpu.VMEM), pl.BlockSpec(memory_space=pl.ANY)
    sem = pltpu.SemaphoreType.DMA
    return pl.pallas_call(
        functools.partial(close_kernel, count, shards),
        in_specs=[vmem, vmem, hbm, vmem, vmem, vmem, hbm, hbm] + [hbm] * chips,
        out_specs=[hbm, vmem, vmem, hbm, vmem],
        out_shape=[
            jax.ShapeDtypeStruct((tokens, model), BF16),
            jax.ShapeDtypeStruct((8, model), F32),
            jax.ShapeDtypeStruct((model // 2, grad.shape[1]), BF16),
            jax.ShapeDtypeStruct((tokens, model), BF16),
            jax.ShapeDtypeStruct(gate.shape, F32),
        ],
        scratch_shapes=[
            pltpu.VMEM((own, model), F32),
            pltpu.VMEM((own, model), BF16),
            pltpu.VMEM((2, rows, model), F32),
        ]
        + [pltpu.VMEM((steps, rows, model), BF16)] * 2
        + [pltpu.VMEM((steps - 2, rows, model), BF16)] * 2
        + [pltpu.VMEM((model // 2, grad.shape[1]), BF16)] * 2
        + [
            pltpu.VMEM(gate.shape, BF16),
            pltpu.VMEM(gate.shape, BF16),
            pltpu.VMEM((4, 8, model), F32),
            pltpu.VMEM((chips + shards, 8, model), F32),
            sem((steps,)), sem((steps,)), sem((steps - 2,)), sem((steps - 2,)),
            sem((2, chips)), sem((2, chips)), sem((shards,)), sem((shards,)), sem((shards,)),
            sem((chips,)), sem((chips,)), sem((chips,)), sem((chips + shards,)),
            sem((chips + shards,)), sem((3,)), sem((2,)),
        ],
        compiler_params=pltpu.CompilerParams(
            vmem_limit_bytes=48 << 20, collective_id=3, has_side_effects=True
        ),
        cost_estimate=pl.CostEstimate(
            flops=2 * tokens * model * dense.shape[1], bytes_accessed=200 << 20, transcendentals=0
        ),
        name="close_layer",
    )(dense, weight, layer_input, middle_grad, gain, gain_two, grad, gate, *layers)


def per_device(
    sizes,
    layer_input,
    doc_lengths,
    attention_gain,
    query_weight,
    key_matrix,
    value_matrix,
    output_weight,
    feedforward_gain,
    gate_weight,
    up_weight,
    down_weight,
    output_cotangent,
):
    shards, pieces, ranks = sizes
    assert pieces == 2 and ranks % 2 == 0
    chips = ranks // 2
    tokens, model = layer_input.shape
    own = tokens // ranks
    head_dim = HEAD_SIZE
    q_heads = query_weight.shape[1] // head_dim
    kv_heads = key_matrix.shape[1] // head_dim
    q_width, kv_width = q_heads * head_dim, kv_heads * head_dim
    piece = lax.axis_index("ctx")
    rank = lax.axis_index("tp")
    chip, core = rank // 2, rank % 2
    me = lax.axis_index("fsdp")
    scale = 1.0 / math.sqrt(head_dim)

    swap_x = [(0, 1), (1, 0)]
    swap_core = [(i, i ^ 1) for i in range(ranks)]

    def chip_shift(k):
        return [(i, (i + 2 * k) % ranks) for i in range(ranks)]

    def shard_shift(k):
        return [(i, (i + k) % shards) for i in range(shards)]

    def pick(array, index, axis=0):
        return lax.dynamic_index_in_dim(array, index, axis, keepdims=False)

    def half_of(shard):
        rows = shard.shape[0] // 2
        return lax.dynamic_slice_in_dim(shard, piece * rows, rows, 0)

    both_axes = ("fsdp", "ctx")

    def reduce_fsdp(part):
        return lax.psum_scatter(part, "fsdp", scatter_dimension=0, tiled=True)

    def add_pieces(mine):
        return mine.astype(F32) + lax.ppermute(mine, "ctx", swap_x).astype(F32)

    def whole_shard(mine):
        other = lax.ppermute(mine, "ctx", swap_x)
        pair = jnp.where(
            piece == 0, jnp.concatenate([mine, other], 0), jnp.concatenate([other, mine], 0)
        )
        return pair.astype(F32)

    ff_half = half_of(jnp.concatenate([gate_weight, up_weight, down_weight.T], axis=1))
    gain_shard = jnp.stack([attention_gain, feedforward_gain]).astype(F32)
    gain_shard = jnp.pad(gain_shard, ((0, 6), (0, 0)))
    qkv_shard = jnp.concatenate([query_weight, key_matrix, value_matrix], axis=1)
    positions = doc_positions(doc_lengths[0], piece * tokens, tokens)
    cos, sin = rotary_lanes(positions, head_dim)
    lane = np.arange(LANES)[None, :]
    half_dim = head_dim // 2
    krow = np.where((lane >= half_dim) & (lane < half_dim + 3), -1.0, 0.0).astype(np.float32)
    vrow = np.where((lane >= head_dim) & (lane < head_dim + 3), 1.0, 0.0).astype(np.float32)
    rot_q, rot_k = select_rotary(q_heads, head_dim), select_rotary(kv_heads, head_dim)
    val_q, val_k = select_value(q_heads, head_dim), select_value(kv_heads, head_dim)
    val_q_wide = np.ascontiguousarray(val_q.T)
    spread = np.zeros((q_width + 2 * kv_width, (q_heads + 2 * kv_heads) * LANES), rot_q.dtype)
    at_key, at_value = q_heads * LANES, (q_heads + kv_heads) * LANES
    spread[:q_width, :at_key] = rot_q.T
    spread[q_width : q_width + kv_width, at_key:at_value] = rot_k.T
    spread[q_width + kv_width :, at_value:] = val_k.T
    normed_one, qkv_full, out_own, gains_full = begin(
        shards, layer_input, qkv_shard, output_weight.T, gain_shard, ff_half
    )
    widen_kv = np.ascontiguousarray(spread[q_width:, at_key:])
    marks = np.concatenate([krow] * kv_heads + [vrow] * kv_heads, axis=1)
    queries, keys_values, dense_kv = project(
        normed_one, qkv_full, spread, cos, sin, krow, vrow, np.ascontiguousarray(widen_kv.T), q_heads, kv_heads
    )
    ff_half, gains_full = lax.optimization_barrier((ff_half, gains_full))
    ff_full = lax.all_gather(ff_half, both_axes, axis=0, tiled=True)
    gain_one, gain_two = gains_full[0:1], gains_full[1:2]
    before = lax.ppermute(dense_kv, "ctx", [(0, 1)])
    base = -(piece - 1) * tokens
    ends = jnp.cumsum(doc_lengths[0]).astype(jnp.int32) + base
    base = base.astype(jnp.int32).reshape(1)
    state = attention_forward(ends, base, queries, keys_values, head_dim, tokens)
    attended, marked = attention_forward(
        ends, base, queries, before, head_dim, 0, state, (widen_kv, marks, val_q)
    )
    wo = [out_own] + [lax.ppermute(out_own, "tp", chip_shift(k)) for k in range(1, chips)]
    normed_two, middle, wo_others = mix(ranks, attended, layer_input, gain_two, wo)
    (
        feed_sums, middle_grad, branch_grad, gain_two_grad, attended_grad, gate_part, feed_part,
    ) = feedforward(
        ranks, normed_two, output_cotangent, middle, gain_two, ff_full, wo, wo_others
    )
    gate_own, feed_own = reduce_fsdp(gate_part), reduce_fsdp(feed_part)
    cut = feed_sums.reshape(chips, own, model)
    feed_sums = [lax.ppermute(cut[k - 1], "tp", chip_shift(k)) for k in range(1, chips)]
    dq_part, dkv_before = attention_backward(
        ends, base, marked, attended_grad, attended, before, val_q_wide, head_dim, 0,
        extra=(widen_kv, marks),
    )
    after = lax.ppermute(dkv_before, "ctx", [(1, 0)])
    dq, dkv = attention_backward(
        ends, base, marked, attended_grad, attended, keys_values, val_q_wide, head_dim, tokens,
        (dq_part, cos, sin, rot_q),
    )

    feed_sums, dq = lax.optimization_barrier((feed_sums, dq))
    layer_rows = middle + cut[chips - 1].astype(F32)
    for block in feed_sums:
        layer_rows = layer_rows + block.astype(F32)
    layer_rows = layer_rows.astype(BF16)

    def from_chips(rows):
        return [rows] + [lax.ppermute(rows, "tp", chip_shift(k)) for k in range(1, chips)]

    dqkv, attention_part = dense_gradients(
        dq, dkv, after, cos, sin, rot_k, val_k, attended, normed_one, from_chips(branch_grad)
    )
    input_gradient, gains, attention_half, layer_output, gate = close(
        ranks, shards, dqkv, qkv_full, layer_input, middle_grad, gain_one, gain_two_grad,
        attention_part, gate_own, from_chips(layer_rows),
    )
    attention_half, feed_own = lax.optimization_barrier((attention_half, feed_own))
    attention = whole_shard(reduce_fsdp(attention_half))
    feed = add_pieces(feed_own)
    layer_output, input_gradient = layer_output.astype(F32), input_gradient.astype(F32)
    ff_width = gate_weight.shape[1]
    gains = lax.dynamic_slice_in_dim(gains, me * gain_shard.shape[1], gain_shard.shape[1], 1)

    return (
        layer_output,
        input_gradient,
        gains[0],
        attention[:, :q_width],
        attention[:, q_width : q_width + kv_width],
        attention[:, q_width + kv_width : q_width + 2 * kv_width],
        attention[:, q_width + 2 * kv_width :].T,
        gains[1],
        gate,
        feed[:, :ff_width],
        feed[:, ff_width:].T,
    )


def solution(mesh):
    rows = P(("fsdp", "ctx"), None)
    into, out_of = P("fsdp", "tp"), P("tp", "fsdp")
    sizes = (mesh.shape["fsdp"], mesh.shape["ctx"], mesh.shape["tp"])
    return jax.shard_map(
        functools.partial(per_device, sizes),
        mesh=mesh,
        in_specs=(
            rows, P("fsdp", None), P("fsdp"), into, into, into, out_of, P("fsdp"), into, into,
            out_of, rows,
        ),
        out_specs=(
            rows, rows, P("fsdp"), into, into, into, out_of, P("fsdp"), into, into, out_of,
        ),
        check_vma=False,
    )
```

```python
import functools
import math

import jax
import jax.numpy as jnp
import ml_dtypes
import numpy as np
from jax import lax
from jax.experimental import pallas as pl
from jax.experimental.pallas import tpu as pltpu
from jax.sharding import PartitionSpec as P

HEAD_SIZE = 96
EPSILON = 1e-05
THETA = 100000.0
NEGATIVE = -1e30
LOG2E = 1.4426950408889634
LANES = 128
F32 = jnp.float32
BF16 = jnp.bfloat16
NN = (((1,), (0,)), ((), ()))
NT = (((1,), (1,)), ((), ()))
TN = (((0,), (0,)), ((), ()))


def dot(left, right, dims=NN):
    return lax.dot_general(left, right, dims, preferred_element_type=F32)


def select_rotary(heads, head_dim):
    col = np.arange(heads * head_dim)
    half = head_dim // 2
    within = col % head_dim
    lane = np.where(within < half, within, within - half + LANES // 2)
    return select_lanes(heads, (col // head_dim) * LANES + lane)


def select_value(heads, head_dim):
    col = np.arange(heads * head_dim)
    return select_lanes(heads, (col // head_dim) * LANES + col % head_dim)


def select_lanes(heads, want):
    return (np.arange(heads * LANES)[:, None] == want[None, :]).astype(ml_dtypes.bfloat16)


def rotary_lanes(positions, head_dim):
    half = head_dim // 2
    freqs = THETA ** (-(jnp.arange(half, dtype=F32) * 2.0 / head_dim))
    angles = positions.astype(F32)[:, None] * freqs[None, :]
    cos, sin = jnp.cos(angles), jnp.sin(angles)
    pad = jnp.zeros((positions.shape[0], LANES // 2 - half), F32)
    return (
        jnp.concatenate([cos, pad, cos, pad], axis=1),
        jnp.concatenate([-sin, pad, sin, pad], axis=1),
    )


def doc_positions(lengths, first, count):
    ends = jnp.cumsum(lengths)
    starts = ends - lengths
    index = first + jnp.arange(count, dtype=jnp.int32)
    document = jnp.sum((index[None, :] >= ends[:, None]).astype(jnp.int32), axis=0)
    chosen = document[None, :] == jnp.arange(lengths.shape[0], dtype=jnp.int32)[:, None]
    start_of = jnp.sum(jnp.where(chosen, starts[:, None], 0), axis=0)
    return index - start_of


def doc_start(ends_ref, base, rows):
    start = base if jnp.ndim(rows) == 0 else jnp.zeros_like(rows) + base
    for j in range(ends_ref.shape[0]):
        end = ends_ref[j]
        start = jnp.where(rows >= end, jnp.maximum(start, end), start)
    return start


def put_lanes(rows, column, lane):
    at = lax.broadcasted_iota(jnp.int32, rows.shape, 1)
    high = column.astype(BF16).astype(F32)
    rest = column - high
    mid = rest.astype(BF16).astype(F32)
    low = rest - mid
    wide = rows.astype(F32)
    wide = jnp.where(at == lane, high, wide)
    wide = jnp.where(at == lane + 1, mid, wide)
    return jnp.where(at == lane + 2, low, wide).astype(BF16)


def block_ranges(first_row, rows, block, low, last_low, key_base, key_count):
    begin = (jnp.maximum(low, key_base) - key_base) // block
    stop = jnp.minimum((first_row + rows - key_base + block - 1) // block, key_count // block)
    inner = jnp.minimum(jnp.maximum((last_low - key_base + block - 1) // block, begin), stop)
    diagonal = jnp.minimum(jnp.maximum((first_row - key_base) // block, inner), stop)
    return begin, inner, diagonal, stop


def stack_heads(ref, kv, group):
    parts = [ref[:, (kv * group + g) * LANES : (kv * group + g + 1) * LANES] for g in range(group)]
    return jnp.concatenate(parts, axis=0)


def row_marks(ends_ref, base, first_row, bq, group):
    rows = lax.broadcasted_iota(jnp.int32, (1, bq), 1) + first_row
    starts = doc_start(ends_ref, base, rows)
    return jnp.concatenate([rows] * group, axis=1), jnp.concatenate([starts] * group, axis=1)


def widen(dense_ref, spread_ref, mark_ref, wide_ref):
    @pl.when(pl.program_id(0) == 0)
    def _():
        wide = dot(dense_ref[...], spread_ref[...]) + mark_ref[...]
        wide_ref[...] = wide.astype(BF16)

    return wide_ref


def attention_forward_kernel(
    first, key_base, tokens, bq, bk, head_dim, group, ends_ref, base_ref, q_ref, kv_ref, *rest
):
    if first:
        max_ref, acc_ref = rest
    else:
        spread_ref, mark_ref, sel_ref, max_in, acc_in, o_ref, qa_ref, max_ref, acc_ref, wide = rest
        kv_ref = widen(kv_ref, spread_ref, mark_ref, wide)
    first_row = tokens + pl.program_id(0) * bq
    base = base_ref[0]
    low = doc_start(ends_ref, base, first_row)
    last_low = doc_start(ends_ref, base, first_row + bq - 1)
    rows, starts = row_marks(ends_ref, base, first_row, bq, group)
    kv_heads = kv_ref.shape[1] // LANES // 2
    unit = LOG2E / math.sqrt(head_dim)
    queries = [stack_heads(q_ref, h, group) for h in range(kv_heads)]
    if first:
        max_ref[...] = jnp.full(max_ref.shape, NEGATIVE, F32)
        acc_ref[...] = jnp.zeros(acc_ref.shape, F32)
    else:
        max_ref[...] = max_in[...]
        acc_ref[...] = acc_in[...]

    def body(masked, index, carry):
        at = pl.multiple_of(index * bk, bk)
        if masked:
            keys = lax.broadcasted_iota(jnp.int32, (bk, group * bq), 0) + (at + key_base)
            keep = (keys <= rows) & (keys >= starts)
        for h in range(kv_heads):
            key = kv_ref[pl.ds(at, bk), h * LANES : (h + 1) * LANES]
            value = kv_ref[pl.ds(at, bk), (kv_heads + h) * LANES : (kv_heads + h + 1) * LANES]
            scores = dot(key, queries[h], NT)
            if masked:
                scores = jnp.where(keep, scores, NEGATIVE)
            old = max_ref[0, h]
            new = jnp.maximum(old, jnp.max(scores, axis=0, keepdims=True))
            probs = jnp.exp2((scores - new) * unit)
            if masked:
                probs = jnp.where(keep, probs, 0.0)
            acc_ref[0, h] = acc_ref[0, h] * jnp.exp2((old - new) * unit) + dot(
                value, probs.astype(BF16), TN
            )
            max_ref[0, h] = new
        return carry

    begin, inner, diagonal, stop = block_ranges(
        first_row, bq, bk, low, last_low, key_base, kv_ref.shape[0]
    )
    lax.fori_loop(begin, inner, functools.partial(body, True), 0)
    lax.fori_loop(inner, diagonal, functools.partial(body, False), 0)
    lax.fori_loop(diagonal, stop, functools.partial(body, True), 0)
    if first:
        return
    outs = []
    for h in range(kv_heads):
        acc = acc_ref[0, h]
        total = acc[head_dim : head_dim + 1, :]
        out = jnp.transpose(acc * (1.0 / total)).astype(BF16)
        logsum = jnp.broadcast_to(max_ref[0, h] + jnp.log2(total) * (1.0 / unit), (8, group * bq))
        marked = put_lanes(queries[h], jnp.transpose(logsum)[:, :1], head_dim // 2)
        for g in range(group):
            head = h * group + g
            qa_ref[:, head * LANES : (head + 1) * LANES] = marked[g * bq : (g + 1) * bq]
            outs.append(out[g * bq : (g + 1) * bq])
    o_ref[...] = dot(jnp.concatenate(outs, axis=1), sel_ref[...]).astype(BF16)


def attention_forward(ends, base, q, kv, head_dim, key_base, state=None, extra=None):
    tokens, width = q.shape
    kv_heads = (kv if state is None else extra[0]).shape[1] // LANES // 2
    group = width // LANES // kv_heads
    bq = bk = math.gcd(tokens, 512)
    steps = tokens // bq
    whole = lambda a: pl.BlockSpec(a.shape, lambda i, *_: (0, 0))
    row = lambda w: pl.BlockSpec((bq, w), lambda i, *_: (i, 0))
    shapes = [(steps, kv_heads, 1, group * bq), (steps, kv_heads, LANES, group * bq)]
    kept = [pl.BlockSpec((1,) + a[1:], lambda i, *_: (i, 0, 0, 0)) for a in shapes]
    pairs = tokens * tokens * group * kv_heads // 2
    if state is None:
        in_specs, operands = [row(width), whole(kv)], (q, kv)
        out_specs, out_shape = kept, [jax.ShapeDtypeStruct(a, F32) for a in shapes]
        scratch = []
    else:
        select = extra[2]
        in_specs = [row(width), whole(kv)] + [whole(a) for a in extra] + kept
        operands = (q, kv) + tuple(extra) + tuple(state)
        out_specs = [row(select.shape[1]), row(width)]
        out_shape = [
            jax.ShapeDtypeStruct((tokens, select.shape[1]), BF16),
            jax.ShapeDtypeStruct(q.shape, BF16),
        ]
        scratch = [pltpu.VMEM((1,) + a[1:], F32) for a in shapes]
        scratch.append(pltpu.VMEM((tokens, extra[0].shape[1]), BF16))
    return pl.pallas_call(
        functools.partial(
            attention_forward_kernel, state is None, key_base, tokens, bq, bk, head_dim, group
        ),
        grid_spec=pltpu.PrefetchScalarGridSpec(
            num_scalar_prefetch=2, grid=(steps,), in_specs=in_specs, out_specs=out_specs,
            scratch_shapes=scratch,
        ),
        out_shape=out_shape,
        compiler_params=pltpu.CompilerParams(vmem_limit_bytes=40 << 20),
        cost_estimate=pl.CostEstimate(
            flops=pairs * 1024, bytes_accessed=8 << 20, transcendentals=pairs
        ),
        name="attention_forward",
    )(ends, base, *operands)


def attention_backward_kernel(
    first, key_base, tokens, bq, bk, head_dim, group,
    ends_ref, base_ref, qa_ref, do_ref, o_ref, kv_ref, spread_ref, *rest
):
    if first:
        widen_ref, mark_ref, dq_ref, dkv_ref, dk_acc, dv_acc, dq_acc, wide = rest
        kv_ref = widen(kv_ref, widen_ref, mark_ref, wide)
    else:
        part_ref, cos_ref, sin_ref, sel_ref, dq_ref, dkv_ref, dk_acc, dv_acc, dq_acc = rest
    step = pl.program_id(0)
    first_row = tokens + step * bq
    base = base_ref[0]
    low = doc_start(ends_ref, base, first_row)
    last_low = doc_start(ends_ref, base, first_row + bq - 1)
    kv_heads = kv_ref.shape[1] // LANES // 2
    scale = 1.0 / math.sqrt(head_dim)
    unit = LOG2E * scale
    begin, inner, diagonal, stop = block_ranges(
        first_row, bq, bk, low, last_low, key_base, kv_ref.shape[0]
    )

    @pl.when(step == 0)
    def _():
        dk_acc[...] = jnp.zeros(dk_acc.shape, F32)
        dv_acc[...] = jnp.zeros(dv_acc.shape, F32)

    if first:
        dq_acc[...] = jnp.zeros(dq_acc.shape, F32)
    else:
        for h in range(kv_heads):
            dq_acc[h] = stack_heads(part_ref, h, group)

    @pl.when(begin < stop)
    def _():
        rows, starts = row_marks(ends_ref, base, first_row, bq, group)
        grads_wide = dot(do_ref[...], spread_ref[...])
        outs_wide = dot(o_ref[...], spread_ref[...])
        queries, grads = [], []
        for h in range(kv_heads):
            queries.append(stack_heads(qa_ref, h, group))
            grad = stack_heads(grads_wide, h, group)
            inner_sum = jnp.sum(grad * stack_heads(outs_wide, h, group), axis=1, keepdims=True)
            grads.append(put_lanes(grad, -inner_sum, head_dim))

        def body(masked, index, carry):
            at = pl.multiple_of(index * bk, bk)
            if masked:
                keys = lax.broadcasted_iota(jnp.int32, (bk, group * bq), 0) + (at + key_base)
                keep = (keys <= rows) & (keys >= starts)
            for h in range(kv_heads):
                key = kv_ref[pl.ds(at, bk), h * LANES : (h + 1) * LANES]
                value = kv_ref[pl.ds(at, bk), (kv_heads + h) * LANES : (kv_heads + h + 1) * LANES]
                probs = jnp.exp2(dot(key, queries[h], NT) * unit)
                if masked:
                    probs = jnp.where(keep, probs, 0.0)
                slope = (probs * dot(value, grads[h], NT)).astype(BF16)
                dv_acc[h, pl.ds(at, bk), :] += dot(probs.astype(BF16), grads[h])
                dk_acc[h, pl.ds(at, bk), :] += dot(slope, queries[h])
                dq_acc[h] += dot(slope, key, TN)
            return carry

        lax.fori_loop(begin, inner, functools.partial(body, True), 0)
        lax.fori_loop(inner, diagonal, functools.partial(body, False), 0)
        lax.fori_loop(diagonal, stop, functools.partial(body, True), 0)

    outs = []
    for h in range(kv_heads):
        for g in range(group):
            grad = dq_acc[h, g * bq : (g + 1) * bq, :]
            if first:
                dq_ref[:, (h * group + g) * LANES : (h * group + g + 1) * LANES] = grad
            else:
                grad = grad * scale
                outs.append(
                    (grad * cos_ref[...] - pltpu.roll(grad, LANES // 2, 1) * sin_ref[...]).astype(BF16)
                )
    if not first:
        dq_ref[...] = dot(jnp.concatenate(outs, axis=1), sel_ref[...]).astype(BF16)

    @pl.when(step == pl.num_programs(0) - 1)
    def _():
        for h in range(kv_heads):
            dkv_ref[:, h * LANES : (h + 1) * LANES] = (dk_acc[h] * scale).astype(dkv_ref.dtype)
            dkv_ref[:, (kv_heads + h) * LANES : (kv_heads + h + 1) * LANES] = dv_acc[h].astype(dkv_ref.dtype)


def attention_backward(ends, base, qa, grad, out, kv, spread, head_dim, key_base, rest=None, extra=None):
    tokens, width = qa.shape
    keys = kv.shape[0]
    kv_lanes = (kv if rest is not None else extra[0]).shape[1]
    kv_heads = kv_lanes // LANES // 2
    group = width // LANES // kv_heads
    bq = bk = math.gcd(tokens, 512)
    whole = lambda a: pl.BlockSpec(a.shape, lambda i, *_: (0, 0))
    row = lambda w: pl.BlockSpec((bq, w), lambda i, *_: (i, 0))
    pairs = tokens * tokens * group * kv_heads // 2
    in_specs = [row(width), row(grad.shape[1]), row(out.shape[1]), whole(kv), whole(spread)]
    operands = (qa, grad, out, kv, spread)
    scratch = []
    if rest is None:
        in_specs += [whole(a) for a in extra]
        operands += tuple(extra)
        scratch = [pltpu.VMEM((keys, kv_lanes), BF16)]
        dq_width, dq_type, dkv_type = width, F32, BF16
    else:
        part, cos, sin, select = rest
        in_specs += [row(width), row(LANES), row(LANES), whole(select)]
        operands += (part, cos, sin, select)
        dq_width, dq_type, dkv_type = select.shape[1], BF16, F32
    return pl.pallas_call(
        functools.partial(
            attention_backward_kernel, rest is None, key_base, tokens, bq, bk, head_dim, group
        ),
        grid_spec=pltpu.PrefetchScalarGridSpec(
            num_scalar_prefetch=2,
            grid=(tokens // bq,),
            in_specs=in_specs,
            out_specs=[row(dq_width), pl.BlockSpec((keys, kv_lanes), lambda i, *_: (0, 0))],
            scratch_shapes=[
                pltpu.VMEM((kv_heads, keys, LANES), F32),
                pltpu.VMEM((kv_heads, keys, LANES), F32),
                pltpu.VMEM((kv_heads, group * bq, LANES), F32),
            ]
            + scratch,
        ),
        out_shape=[
            jax.ShapeDtypeStruct((tokens, dq_width), dq_type),
            jax.ShapeDtypeStruct((keys, kv_lanes), dkv_type),
        ],
        compiler_params=pltpu.CompilerParams(vmem_limit_bytes=48 << 20),
        cost_estimate=pl.CostEstimate(
            flops=pairs * 2560, bytes_accessed=12 << 20, transcendentals=pairs
        ),
        name="attention_backward",
    )(ends, base, qa, grad, out, kv, spread, *operands[5:])


MESH = pl.DeviceIdType.MESH


class Ranks:
    def __init__(self, count):
        self.count, self.chips = count, count // 2
        self.me = lax.axis_index("tp")
        self.chip, self.core = self.me // 2, self.me % 2

    def peer(self, k, j):
        return lax.rem(self.chip + k + self.chips, self.chips) * 2 + lax.rem(self.core + j, 2)

    def others(self):
        return [(k, j) for k in range(self.chips) for j in range(2) if k or j]

    def barrier(self):
        sem = pltpu.get_barrier_semaphore()
        for k, j in self.others():
            pl.semaphore_signal(sem, inc=1, device_id={"tp": self.peer(k, j)}, device_id_type=MESH)
        pl.semaphore_wait(sem, self.count - 1)


def remote(src, dst, send, recv, rank):
    return pltpu.make_async_remote_copy(
        src_ref=src, dst_ref=dst, send_sem=send, recv_sem=recv, device_id={"tp": rank},
        device_id_type=MESH,
    )


def row_mean(x):
    return jnp.sum(x, axis=-1, keepdims=True) * (1.0 / x.shape[-1])


class GatherRows:
    def __init__(self, ranks, rows_ref, out_ref, send, recv, local):
        own = rows_ref.shape[0]
        self.ranks, self.send, self.recv = ranks, send, recv
        self.at = lambda rank: out_ref.at[pl.ds(pl.multiple_of(rank * own, own), own)]
        self.keep = pltpu.make_async_copy(rows_ref, self.at(ranks.me), local)
        self.copies = []
        for k in list(range(1, ranks.chips)) + [0]:
            peer = ranks.peer(k, 0) if k else ranks.peer(0, 1)
            self.copies.append(remote(rows_ref, self.at(ranks.me), send.at[0, k], recv.at[0, k], peer))

    def start(self):
        for copy in self.copies:
            copy.start()
        self.keep.start()

    def finish(self):
        ranks, passed = self.ranks, []
        for k, copy in zip(range(1, ranks.chips), self.copies):
            copy.wait_recv()
            held = self.at(ranks.peer(-k, 0))
            passed.append(
                remote(held, held, self.send.at[1, k], self.recv.at[1, k], ranks.peer(0, 1))
            )
            passed[-1].start()
        self.copies[-1].wait_recv()
        for copy in self.copies:
            copy.wait_send()
        for copy in passed:
            copy.wait()
        self.keep.wait()


def both_cores(ranks, blocks, out_ref, send, recv, local):
    own = blocks[0].shape[0]
    copies = []
    for k, block in enumerate(blocks):
        there = out_ref.at[pl.ds(pl.multiple_of(ranks.peer(-k, 0) * own, own), own)]
        copies.append(remote(block, there, send.at[k], recv.at[k], ranks.peer(0, 1)))
        copies.append(pltpu.make_async_copy(block, there, local.at[k]))
    return copies


def mix_kernel(count, att_ref, x_ref, gain_ref, *rest):
    chips = count // 2
    blocks, rest = rest[:chips], rest[chips:]
    (
        n2_ref, mid_ref, other_ref, heads, rows_in, rows_out, others, a_send, a_recv, b_send, b_recv,
        g_send, g_recv, local,
    ) = rest
    ranks = Ranks(count)
    own = rows_in.shape[0]
    mine_at = pl.ds(pl.multiple_of(ranks.me * own, own), own)
    fetch = pltpu.make_async_copy(x_ref.at[mine_at], rows_in, local.at[0])
    fetch.start()
    mine = pltpu.make_async_copy(att_ref.at[mine_at], heads.at[0], local.at[1])
    mine.start()
    ranks.barrier()
    copies = {}
    for k, j in ranks.others()[::-1]:
        peer, slot = ranks.peer(k, j), 2 * k + j
        copies[slot] = remote(
            att_ref.at[pl.ds(pl.multiple_of(peer * own, own), own)], heads.at[slot],
            a_send.at[slot], a_recv.at[slot], peer,
        )
        copies[slot].start()
    swaps = [
        remote(blocks[k], others.at[k], b_send.at[k], b_recv.at[k], ranks.peer(0, 1))
        for k in range(chips)
    ]
    for copy in swaps:
        copy.start()
    fetch.wait()
    mine.wait()
    mid_ref[...] = rows_in[...] + dot(heads[0], blocks[0][...], NT)
    keeps = []
    for slot in range(1, count):
        k = slot // 2
        if slot % 2:
            swaps[k].wait_recv()
            keeps.append(pltpu.make_async_copy(others.at[k], other_ref.at[k], local.at[2 + k]))
            keeps[-1].start()
        copies[slot].wait_recv()
        mid_ref[...] += dot(heads[slot], others[k] if slot % 2 else blocks[k][...], NT)
    mid = mid_ref[...]
    factor = lax.rsqrt(row_mean(mid * mid) + EPSILON)
    rows_out[...] = (mid * factor * gain_ref[...]).astype(BF16)
    gather = GatherRows(ranks, rows_out, n2_ref, g_send, g_recv, local.at[0])
    gather.start()
    for slot in range(1, count):
        copies[slot].wait_send()
    for copy in swaps:
        copy.wait_send()
    for copy in keeps:
        copy.wait()
    gather.finish()


def mix(count, attended, layer_input, gain, blocks):
    tokens, model = layer_input.shape
    own = tokens // count
    chips = count // 2
    width = attended.shape[1]
    vmem, hbm = pl.BlockSpec(memory_space=pltpu.VMEM), pl.BlockSpec(memory_space=pl.ANY)
    sem = pltpu.SemaphoreType.DMA
    return pl.pallas_call(
        functools.partial(mix_kernel, count),
        in_specs=[hbm, hbm, vmem] + [vmem] * chips,
        out_specs=[hbm, vmem, hbm],
        out_shape=[
            jax.ShapeDtypeStruct((tokens, model), BF16),
            jax.ShapeDtypeStruct((own, model), F32),
            jax.ShapeDtypeStruct((chips, model, width), BF16),
        ],
        scratch_shapes=[
            pltpu.VMEM((count, own, width), BF16),
            pltpu.VMEM((own, model), F32),
            pltpu.VMEM((own, model), BF16),
            pltpu.VMEM((chips, model, width), BF16),
            sem((count,)), sem((count,)), sem((chips,)), sem((chips,)), sem((2, chips)),
            sem((2, chips)), sem((2 + chips,)),
        ],
        compiler_params=pltpu.CompilerParams(
            vmem_limit_bytes=40 << 20, collective_id=1, has_side_effects=True
        ),
        cost_estimate=pl.CostEstimate(
            flops=2 * tokens * model * model, bytes_accessed=150 << 20, transcendentals=0
        ),
        name="mix_heads",
    )(attended, layer_input, gain, *blocks)


def scatter_order(ranks, halves, own, i):
    k = lax.rem(i // halves + 1, ranks.chips)
    half = lax.rem(i, halves)
    rows = own // halves
    at = lambda j: pl.multiple_of(ranks.peer(k, j) * own + half * rows, rows)
    return k, half, at(0), at(1)


def half_rows(shard, which, half):
    return pl.ds(pl.multiple_of((shard * 2 + which) * half, half), half)


def swap_halves(src, dst, send, recv, shards):
    piece = lax.axis_index("ctx")
    half = src.shape[0] // (2 * shards)
    return [
        pltpu.make_async_remote_copy(
            src_ref=src.at[half_rows(s, 1 - piece, half)], dst_ref=dst.at[pl.ds(s * half, half)],
            send_sem=send.at[s], recv_sem=recv.at[s], device_id={"ctx": 1 - piece},
            device_id_type=MESH,
        )
        for s in range(shards)
    ]


def signal_piece(count):
    ranks = Ranks(count)
    sem = pltpu.get_barrier_semaphore()
    for k, j in ranks.others():
        pl.semaphore_signal(sem, inc=1, device_id={"tp": ranks.peer(k, j)}, device_id_type=MESH)
    pl.semaphore_signal(sem, inc=1, device_id={"ctx": 1 - lax.axis_index("ctx")}, device_id_type=MESH)
    pl.semaphore_wait(sem, count)


def feedforward_kernel(count, n2_ref, cot_ref, mid_ref, gain_ref, other_in, weight_ref, ff_ref, *rest):
    blocks_in, rest = rest[: count // 2], rest[count // 2 :]
    (
        ffb_ref, mg_ref, bg_ref, gain_grad_ref, da_ref, grad_ref, grads_ref,
        gate_w, up_w, down_w, n2, fg, hid, gu, rows_in, ffb_out,
        c_send, c_recv, y_send, y_recv, f_send, f_recv, heads, other_ref, blocks,
        w_sem, in_sem, out_sem, cs, cr, ys, yr, fs, fr, hs, hr, local,
    ) = rest
    ranks = Ranks(count)
    own = mg_ref.shape[0]
    halves = 2
    rows = own // halves
    steps = ranks.chips * halves
    width = gate_w.shape[1]
    model = n2.shape[1]
    cut = width - ff_ref.shape[1]
    loads = [
        pltpu.make_async_copy(n2_ref, n2, w_sem.at[0]),
        pltpu.make_async_copy(weight_ref.at[:, pl.ds(0, width)], gate_w, w_sem.at[1]),
        pltpu.make_async_copy(weight_ref.at[:, pl.ds(width, width)], up_w, w_sem.at[2]),
        pltpu.make_async_copy(
            weight_ref.at[:, pl.ds(2 * width, cut)], down_w.at[:, pl.ds(0, cut)], w_sem.at[3]
        ),
        pltpu.make_async_copy(ff_ref, down_w.at[:, pl.ds(cut, width - cut)], w_sem.at[4]),
    ]
    late = [pltpu.make_async_copy(other_in, other_ref, w_sem.at[5])] + [
        pltpu.make_async_copy(block, blocks.at[k], w_sem.at[6 + k])
        for k, block in enumerate(blocks_in)
    ]
    for load in loads + late:
        load.start()

    def read(at, slot):
        return pltpu.make_async_copy(cot_ref.at[pl.ds(at, rows)], rows_in.at[slot], in_sem.at[slot])

    def tile(at, slot, begin):
        here = pl.ds(at, rows)

        def ready(n):
            if begin is not None:
                @pl.when(begin)
                def _():
                    loads[n].wait()

        ready(0)
        ready(1)
        n = n2[here, :]
        grad = rows_in[slot].astype(BF16)
        fg[here, :] = grad
        gate = dot(n, gate_w[...])
        ready(2)
        up = dot(n, up_w[...])
        ready(3)
        ready(4)
        back = dot(grad, down_w[...])
        sig = 1.0 / (1.0 + jnp.exp(-gate))
        act = gate * sig
        hidden = (act * up).astype(BF16)
        hid[here, :] = hidden
        gg = (back * up * (sig * (1.0 + gate * (1.0 - sig)))).astype(BF16)
        gu[here, :width] = gg
        ug = (back * act).astype(BF16)
        gu[here, width:] = ug
        return dot(gg, gate_w[...], NT) + dot(ug, up_w[...], NT), dot(hidden, down_w[...], NT)

    read(scatter_order(ranks, halves, own, 0)[3], 0).start()
    ranks.barrier()
    neighbour = ranks.peer(0, 1)

    def to_core(i):
        slot = lax.rem(i, 2)
        return [
            remote(c_send.at[slot], c_recv.at[slot], cs.at[slot], cr.at[slot], neighbour),
            remote(f_send.at[slot], f_recv.at[slot], fs.at[slot], fr.at[slot], neighbour),
        ]

    def to_chip(i, k):
        return remote(y_send.at[i], y_recv.at[i], ys.at[i], yr.at[i], ranks.peer(k, 0))

    def ffb_write(i):
        return pltpu.make_async_copy(ffb_out, ffb_ref.at[i], out_sem.at[0])

    def step(i, carry):
        k, u, at_mine, at_other = scatter_order(ranks, halves, own, i)
        slot = lax.rem(i, 2)
        read(at_mine, 1).start()
        read(at_other, 0).wait()
        grad, forward = tile(at_other, 0, i == 0)

        @pl.when(i + 1 < steps)
        def _():
            read(scatter_order(ranks, halves, own, i + 1)[3], 0).start()

        @pl.when(i > 1)
        def _():
            for copy in to_core(i):
                copy.wait_send()

        c_send[slot] = grad.astype(BF16)
        f_send[slot] = forward.astype(BF16)
        for copy in to_core(i):
            copy.start()
        read(at_mine, 1).wait()
        grad, forward = tile(at_mine, 1, None)

        @pl.when(i > 0)
        def _():
            ffb_write(i).wait()

        for copy in to_core(i):
            copy.wait_recv()
        grad = grad + c_recv[slot].astype(F32)
        ffb_out[...] = (forward + f_recv[slot].astype(F32)).astype(BF16)
        ffb_write(i).start()

        @pl.when(k != 0)
        def _():
            y_send[i] = grad.astype(BF16)
            to_chip(i, k).start()

        @pl.when(k == 0)
        def _():
            mg_ref[pl.ds(pl.multiple_of(u * rows, rows), rows), :] = grad

        return carry

    lax.fori_loop(0, steps, step, 0)
    mine_at = pl.multiple_of(ranks.me * own, own)
    fetch = lambda u: [
        pltpu.make_async_copy(mid_ref.at[pl.ds(u * rows, rows)], rows_in.at[0], in_sem.at[0]),
        read(mine_at + u * rows, 1),
    ]
    for copy in fetch(0):
        copy.start()
    cols = math.gcd(model, 384)
    writes = []

    def product(left, right, full, dst, n):
        for d in range(model // cols):
            full[d * cols : (d + 1) * cols, :] = dot(
                left[:, d * cols : (d + 1) * cols], right, TN
            ).astype(BF16)
        writes.append(pltpu.make_async_copy(full, dst, out_sem.at[1 + n]))
        writes[-1].start()

    product(n2, gu[:, :width], gate_w, grad_ref, 0)
    gain = gain_ref[...]
    gain_total = None
    for u in range(halves):
        here = slice(u * rows, (u + 1) * rows)
        total = mg_ref[here, :]
        for k in range(1, ranks.chips):
            i = (k - 1) * halves + u
            to_chip(i, k).wait_recv()
            total = total + y_recv[i].astype(F32)
        for copy in fetch(u):
            copy.wait()
        mid = rows_in[0]
        factor = lax.rsqrt(row_mean(mid * mid) + EPSILON)
        hat = mid * factor
        term = jnp.sum(total * hat, axis=0, keepdims=True)
        gain_total = term if gain_total is None else gain_total + term
        inner = total * gain
        grad = rows_in[1] + factor * (inner - hat * row_mean(inner * hat))
        mg_ref[here, :] = grad
        bg_ref[here, :] = grad.astype(BF16)
        if u + 1 < halves:
            for copy in fetch(u + 1):
                copy.start()
    gain_grad_ref[...] = gain_total
    for load in late:
        load.wait()
    back = []
    for k, j in ranks.others()[::-1]:
        slot, peer = 2 * k + j, ranks.peer(-k, j)
        heads[slot] = dot(bg_ref[...], other_ref[k] if j else blocks[k]).astype(BF16)
        back.append(
            remote(heads.at[slot], da_ref.at[pl.ds(mine_at, own)], hs.at[slot], hr.at[slot], peer)
        )
        back[-1].start()
    heads[0] = dot(bg_ref[...], blocks[0]).astype(BF16)
    keep = pltpu.make_async_copy(heads.at[0], da_ref.at[pl.ds(mine_at, own)], local.at[0])
    keep.start()
    product(n2, gu[:, width:], up_w, grads_ref.at[:, pl.ds(0, width)], 1)
    product(fg, hid[...], down_w, grads_ref.at[:, pl.ds(width, width)], 2)
    for i in (steps - 2, steps - 1):
        for copy in to_core(i):
            copy.wait_send()
    for i in range(steps - halves):
        to_chip(i, i // halves + 1).wait_send()
    ffb_write(steps - 1).wait()
    for copy in back:
        copy.wait()
    keep.wait()
    for copy in writes:
        copy.wait()


def feedforward(count, n2, cotangent, middle, gain, weights, first, blocks, others):
    tokens, model = n2.shape
    own = tokens // count
    hidden = (weights.shape[1] + first.shape[1]) // 3
    width = blocks[0].shape[1]
    rows, steps = own // 2, count
    vmem, hbm = pl.BlockSpec(memory_space=pltpu.VMEM), pl.BlockSpec(memory_space=pl.ANY)
    sem = pltpu.SemaphoreType.DMA
    return pl.pallas_call(
        functools.partial(feedforward_kernel, count),
        in_specs=[hbm, hbm, hbm, vmem, hbm, hbm, hbm] + [hbm] * (count // 2),
        out_specs=[hbm, vmem, vmem, vmem, hbm, hbm, hbm],
        out_shape=[
            jax.ShapeDtypeStruct((steps, rows, model), BF16),
            jax.ShapeDtypeStruct((own, model), F32),
            jax.ShapeDtypeStruct((own, model), BF16),
            jax.ShapeDtypeStruct((1, model), F32),
            jax.ShapeDtypeStruct((tokens, width), BF16),
            jax.ShapeDtypeStruct((model, hidden), BF16),
            jax.ShapeDtypeStruct((model, 2 * hidden), BF16),
        ],
        scratch_shapes=[pltpu.VMEM((model, hidden), BF16)] * 3
        + [
            pltpu.VMEM((tokens, model), BF16),
            pltpu.VMEM((tokens, model), BF16),
            pltpu.VMEM((tokens, hidden), BF16),
            pltpu.VMEM((tokens, 2 * hidden), BF16),
            pltpu.VMEM((2, rows, model), F32),
            pltpu.VMEM((rows, model), BF16),
        ]
        + [pltpu.VMEM((2, rows, model), BF16)] * 2
        + [pltpu.VMEM((steps - 2, rows, model), BF16)] * 2
        + [pltpu.VMEM((2, rows, model), BF16)] * 2
        + [
            pltpu.VMEM((count, own, width), BF16),
            pltpu.VMEM(others.shape, BF16),
            pltpu.VMEM(others.shape, BF16),
            sem((6 + count // 2,)), sem((2,)), sem((4,)),
            sem((2,)), sem((2,)), sem((steps - 2,)), sem((steps - 2,)),
            sem((2,)), sem((2,)), sem((count,)), sem((count,)), sem((1,)),
        ],
        compiler_params=pltpu.CompilerParams(
            vmem_limit_bytes=63 << 20, collective_id=2, has_side_effects=True
        ),
        cost_estimate=pl.CostEstimate(
            flops=2 * tokens * model * hidden * 9, bytes_accessed=280 << 20,
            transcendentals=tokens * hidden,
        ),
        name="feed_forward",
    )(n2, cotangent, middle, gain, others, weights, first, *blocks)


def shard_copy(src, dst, send, recv, axis, index):
    return pltpu.make_async_remote_copy(
        src_ref=src, dst_ref=dst, send_sem=send, recv_sem=recv, device_id={axis: index},
        device_id_type=MESH,
    )


def begin_kernel(
    shards, x_ref, qkv_ref, wo_ref, ff_ref, gains_ref, order_ref, n_ref, qkv_full_ref, wo_full_ref,
    ff_full_ref, gain_out_ref, qkv_full, wo_full, ff_full, normed, rows_in, gain_buf, zs, zr, xs, xr, gs, gr, own_sem, in_sem, out_sem,
):
    del order_ref
    me, piece = lax.axis_index("fsdp"), lax.axis_index("ctx")
    fulls, sources = (qkv_full, wo_full, ff_full), (qkv_ref, wo_ref, ff_ref)
    arrays = range(len(fulls))
    shard = qkv_ref.shape[0]
    half = shard // 2
    tokens = normed.shape[0]
    rows = rows_in.shape[1]
    steps = tokens // rows

    def read(i):
        return pltpu.make_async_copy(
            x_ref.at[pl.ds(i * rows, rows)], rows_in.at[i % 2], in_sem.at[i % 2]
        )

    read(0).start()
    keeps = [
        pltpu.make_async_copy(src, full.at[pl.ds(pl.multiple_of(me * shard, shard), shard)], own_sem.at[a])
        for a, (src, full) in enumerate(zip(sources, fulls))
    ]
    for copy in keeps:
        copy.start()
    keep_gain = pltpu.make_async_copy(gains_ref, gain_buf.at[me], own_sem.at[3])
    keep_gain.start()
    barrier = pltpu.get_barrier_semaphore()
    for k in range(1, shards):
        pl.semaphore_signal(
            barrier, inc=1, device_id={"fsdp": lax.rem(me + k, shards)}, device_id_type=MESH
        )
    pl.semaphore_signal(barrier, inc=1, device_id={"ctx": 1 - piece}, device_id_type=MESH)
    pl.semaphore_wait(barrier, shards)

    def place(a, s, which):
        return fulls[a].at[half_rows(s, which, half)]

    def own_half(a):
        return sources[a].at[pl.ds(pl.multiple_of(piece * half, half), half)]

    def along(a, s, step, mine):
        way = 0 if step > 0 else 1
        src = own_half(a) if mine else place(a, s, piece)
        return shard_copy(
            src, place(a, s, piece), zs.at[a, way, s], zr.at[a, s], "fsdp",
            lax.rem(me + step + shards, shards),
        )

    def across(a, s):
        return shard_copy(
            place(a, s, piece), place(a, s, piece), xs.at[a, s], xr.at[a, s], "ctx", 1 - piece
        )

    gain_copies = [
        shard_copy(
            gains_ref, gain_buf.at[me], gs.at[k], gr.at[k], "fsdp", lax.rem(me + k, shards)
        )
        for k in range(1, shards)
    ]
    for copy in gain_copies:
        copy.start()
    for a in arrays:
        for step, there in ((1, me < shards - 1), (-1, me > 0)):
            @pl.when(there)
            def _():
                along(a, me, step, True).start()

    for copy in gain_copies:
        copy.wait()
    keep_gain.wait()
    gain_out_ref[...] = jnp.concatenate([gain_buf[s] for s in range(shards)], axis=1)
    for i in range(steps):
        if i + 1 < steps:
            read(i + 1).start()
        read(i).wait()
        x = rows_in[i % 2]
        factor = lax.rsqrt(row_mean(x * x) + EPSILON)
        normed[i * rows : (i + 1) * rows, :] = (x * factor * gain_out_ref[0:1, :]).astype(BF16)
    write_normed = pltpu.make_async_copy(normed, n_ref, out_sem.at[0])
    write_normed.start()

    def arrival(d, step):
        s = me - step * d
        there = (s >= 0) & (s <= shards - 1)
        s = jnp.minimum(jnp.maximum(s, 0), shards - 1)
        onward = (me < shards - 1) if step > 0 else (me > 0)

        @pl.when(there)
        def _():
            for a in arrays:
                along(a, s, step, False).wait_recv()
                across(a, s).start()

        @pl.when(there & onward)
        def _():
            for a in arrays:
                along(a, s, step, False).start()

    for d in range(1, shards):
        arrival(d, 1)
        arrival(d, -1)
    for copy in keeps:
        copy.wait()
    for k in range(1, shards):
        s = lax.rem(me + k, shards)
        for a in arrays:
            across(a, s).wait_recv()
    writes = [
        pltpu.make_async_copy(qkv_full, qkv_full_ref, out_sem.at[1]),
        pltpu.make_async_copy(wo_full, wo_full_ref, out_sem.at[2]),
        pltpu.make_async_copy(ff_full, ff_full_ref, out_sem.at[3]),
    ]
    for copy in writes:
        copy.start()
    for a in arrays:
        for s in range(shards):
            @pl.when((me >= s) & (me < shards - 1))
            def _():
                along(a, s, 1, False).wait_send()

            @pl.when((me <= s) & (me > 0))
            def _():
                along(a, s, -1, False).wait_send()

        for k in range(1, shards):
            across(a, lax.rem(me + k, shards)).wait_send()
    write_normed.wait()
    for copy in writes:
        copy.wait()


def begin(shards, x, qkv, wo, ff, gains, order):
    tokens, model = x.shape
    rows = math.gcd(tokens, 256)
    vmem, hbm = pl.BlockSpec(memory_space=pltpu.VMEM), pl.BlockSpec(memory_space=pl.ANY)
    sem = pltpu.SemaphoreType.DMA
    return pl.pallas_call(
        functools.partial(begin_kernel, shards),
        in_specs=[hbm, vmem, vmem, vmem, vmem, hbm],
        out_specs=[hbm, hbm, hbm, hbm, vmem],
        out_shape=[
            jax.ShapeDtypeStruct((tokens, model), BF16),
            jax.ShapeDtypeStruct((model, qkv.shape[1]), BF16),
            jax.ShapeDtypeStruct((model, wo.shape[1]), BF16),
            jax.ShapeDtypeStruct((model, ff.shape[1]), BF16),
            jax.ShapeDtypeStruct((gains.shape[0], model), F32),
        ],
        scratch_shapes=[
            pltpu.VMEM((model, qkv.shape[1]), BF16),
            pltpu.VMEM((model, wo.shape[1]), BF16),
            pltpu.VMEM((model, ff.shape[1]), BF16),
            pltpu.VMEM((tokens, model), BF16),
            pltpu.VMEM((2, rows, model), F32),
            pltpu.VMEM((shards,) + gains.shape, F32),
            sem((3, 2, shards)), sem((3, shards)), sem((3, shards)), sem((3, shards)),
            sem((shards,)), sem((shards,)), sem((4,)), sem((2,)), sem((4,)),
        ],
        compiler_params=pltpu.CompilerParams(
            vmem_limit_bytes=48 << 20, collective_id=4, has_side_effects=True
        ),
        cost_estimate=pl.CostEstimate(flops=0, bytes_accessed=120 << 20, transcendentals=0),
        name="norm_and_gather",
    )(x, qkv, wo, ff, gains, order)


def project_kernel(
    q_heads, n_ref, qkv_ref, spread_ref, cos_ref, sin_ref, krow_ref, vrow_ref, pick_ref, q_ref, kv_ref,
    dense_ref, wide
):
    @pl.when(pl.program_id(0) == 0)
    def _():
        model = qkv_ref.shape[0]
        block = math.gcd(model, 512)
        for r in range(0, model, block):
            wide[r : r + block, :] = dot(qkv_ref[r : r + block, :], spread_ref[...]).astype(BF16)

    kv_heads = kv_ref.shape[1] // LANES // 2
    cos, sin = cos_ref[...], sin_ref[...]
    out = dot(n_ref[...], wide[...])
    plain = []
    for h in range(q_heads + 2 * kv_heads):
        part = out[:, h * LANES : (h + 1) * LANES]
        if h < q_heads + kv_heads:
            part = part * cos + pltpu.roll(part, LANES // 2, 1) * sin
        if h < q_heads:
            q_ref[:, h * LANES : (h + 1) * LANES] = part.astype(BF16)
        else:
            plain.append(part.astype(BF16))
            part = part + (krow_ref[...] if h < q_heads + kv_heads else vrow_ref[...])
            kv_ref[:, (h - q_heads) * LANES : (h - q_heads + 1) * LANES] = part.astype(BF16)
    dense_ref[...] = dot(jnp.concatenate(plain, axis=1), pick_ref[...]).astype(BF16)


def project(normed, qkv, spread, cos, sin, krow, vrow, pick, q_heads, kv_heads):
    tokens, model = normed.shape
    wide = spread.shape[1]
    bm = math.gcd(tokens, 256)
    whole = lambda a: pl.BlockSpec(a.shape, lambda i: (0, 0))
    row = lambda w: pl.BlockSpec((bm, w), lambda i: (i, 0))
    return pl.pallas_call(
        functools.partial(project_kernel, q_heads),
        grid=(tokens // bm,),
        in_specs=[row(model), whole(qkv), whole(spread), row(LANES), row(LANES), whole(krow), whole(vrow),
            whole(pick)],
        out_specs=[row(q_heads * LANES), row(2 * kv_heads * LANES), row(pick.shape[1])],
        out_shape=[
            jax.ShapeDtypeStruct((tokens, q_heads * LANES), BF16),
            jax.ShapeDtypeStruct((tokens, 2 * kv_heads * LANES), BF16),
            jax.ShapeDtypeStruct((tokens, pick.shape[1]), BF16),
        ],
        scratch_shapes=[pltpu.VMEM((model, wide), BF16)],
        compiler_params=pltpu.CompilerParams(vmem_limit_bytes=40 << 20),
        cost_estimate=pl.CostEstimate(
            flops=2 * tokens * model * wide, bytes_accessed=16 << 20, transcendentals=0
        ),
        name="project_qkv",
    )(normed, qkv, spread, cos, sin, krow, vrow, pick)


def dense_kernel(
    chips, dq_ref, dkv_ref, after_ref, cos_ref, sin_ref, rotk_ref, valk_ref, att_ref, n_ref, *rest
):
    blocks, rest = rest[:chips], rest[chips:]
    dense_ref, grad_ref, normed, branch, send, recv, local = rest
    ranks = Ranks(2 * chips)
    fetch = pltpu.make_async_copy(n_ref, normed, local.at[chips])
    fetch.start()
    sem = pltpu.get_barrier_semaphore()
    pl.semaphore_signal(sem, inc=1, device_id={"tp": ranks.peer(0, 1)}, device_id_type=MESH)
    pl.semaphore_wait(sem, 1)
    copies = both_cores(ranks, blocks, branch, send, recv, local)
    for copy in copies:
        copy.start()
    width = dense_ref.shape[1]
    lanes = dkv_ref.shape[1] // 2
    cos, sin = cos_ref[...], sin_ref[...]
    turned = []
    for h in range(lanes // LANES):
        at = slice(h * LANES, (h + 1) * LANES)
        key = dkv_ref[:, at] + after_ref[:, at].astype(F32)
        turned.append((key * cos - pltpu.roll(key, LANES // 2, 1) * sin).astype(BF16))
    dk = dot(jnp.concatenate(turned, axis=1), rotk_ref[...]).astype(BF16)
    dv = (dkv_ref[:, lanes:] + after_ref[:, lanes:].astype(F32)).astype(BF16)
    dv = dot(dv, valk_ref[...]).astype(BF16)
    dense_ref[...] = jnp.concatenate([dq_ref[...], dk, dv], axis=1)
    fetch.wait()
    model = normed.shape[1]
    cols = math.gcd(model, 384)
    for d in range(0, model, cols):
        grad_ref[d : d + cols, :width] = dot(
            normed[:, d : d + cols], dense_ref[...], TN
        ).astype(BF16)
    for copy in copies:
        copy.wait()
    for d in range(0, model, cols):
        grad_ref[d : d + cols, width:] = dot(branch[:, d : d + cols], att_ref[...], TN).astype(BF16)


def dense_gradients(dq, dkv, after, cos, sin, rot_k, val_k, attended, normed, blocks):
    tokens, model = normed.shape
    chips = len(blocks)
    width = dq.shape[1] + 2 * rot_k.shape[1]
    total = width + attended.shape[1]
    vmem, hbm = pl.BlockSpec(memory_space=pltpu.VMEM), pl.BlockSpec(memory_space=pl.ANY)
    sem = pltpu.SemaphoreType.DMA
    return pl.pallas_call(
        functools.partial(dense_kernel, chips),
        in_specs=[vmem] * 8 + [hbm] * (1 + chips),
        out_specs=[vmem, vmem],
        out_shape=[
            jax.ShapeDtypeStruct((tokens, width), BF16),
            jax.ShapeDtypeStruct((model, total), BF16),
        ],
        scratch_shapes=[
            pltpu.VMEM((tokens, model), BF16),
            pltpu.VMEM((tokens, model), BF16),
            sem((chips,)), sem((chips,)), sem((chips + 1,)),
        ],
        compiler_params=pltpu.CompilerParams(
            vmem_limit_bytes=48 << 20, collective_id=5, has_side_effects=True
        ),
        cost_estimate=pl.CostEstimate(
            flops=2 * tokens * model * total, bytes_accessed=24 << 20, transcendentals=0
        ),
        name="dense_gradients",
    )(dq, dkv, after, cos, sin, rot_k, val_k, attended, normed, *blocks)


def close_kernel(
    count, shards, dense_ref, w_ref, x_ref, mg_ref, gain_ref, gain_two_ref, grad_ref, gate_ref, *rest
):
    layers, rest = rest[: count // 2], rest[count // 2 :]
    (
        out_ref, gain_grad_ref, half_ref, lay_ref, gate_out_ref, rows_in, rows_out, sums, c_send, c_recv, y_send,
        y_recv, x_mine, x_recv, gate_mine, gate_recv, t_send, t_recv, cs, cr, ys, yr, g_send, g_recv, xs, xr, x_sem,
        ls, lr, lay_sem, ts, tr, gate_sem, local,
    ) = rest
    ranks = Ranks(count)
    own = rows_in.shape[0]
    halves = 2
    rows = own // halves
    steps = ranks.chips * halves
    fetch = pltpu.make_async_copy(
        x_ref.at[pl.ds(pl.multiple_of(ranks.me * own, own), own)], rows_in, local.at[0]
    )
    fetch.start()
    def tile(at):
        return dot(dense_ref[pl.ds(at, rows), :], w_ref[...], NT)

    piece = lax.axis_index("ctx")
    half = grad_ref.shape[0] // (2 * shards)
    keeps = [
        pltpu.make_async_copy(
            grad_ref.at[half_rows(s, piece, half)], x_mine.at[pl.ds(s * half, half)], x_sem.at[s]
        )
        for s in range(shards)
    ]
    keeps.append(pltpu.make_async_copy(gate_ref, gate_mine, gate_sem.at[0]))
    for copy in keeps:
        copy.start()
    me = lax.axis_index("fsdp")
    barrier = pltpu.get_barrier_semaphore()
    for k, j in ranks.others():
        pl.semaphore_signal(barrier, inc=1, device_id={"tp": ranks.peer(k, j)}, device_id_type=MESH)
    for k in range(1, shards):
        pl.semaphore_signal(
            barrier, inc=1, device_id={"fsdp": lax.rem(me + k, shards)}, device_id_type=MESH
        )
    pl.semaphore_signal(barrier, inc=1, device_id={"ctx": 1 - piece}, device_id_type=MESH)
    pl.semaphore_wait(barrier, count + shards - 1)
    swaps = swap_halves(grad_ref, x_recv, xs, xr, shards)
    swaps.append(
        pltpu.make_async_remote_copy(
            src_ref=gate_ref, dst_ref=gate_recv, send_sem=gate_sem.at[1], recv_sem=gate_sem.at[2],
            device_id={"ctx": 1 - piece}, device_id_type=MESH,
        )
    )
    for copy in swaps:
        copy.start()
    forward = both_cores(ranks, layers, lay_ref, ls, lr, lay_sem)
    for copy in forward:
        copy.start()
    neighbour = ranks.peer(0, 1)

    def to_core(i):
        return remote(c_send.at[i], c_recv.at[i], cs.at[i], cr.at[i], neighbour)

    def to_chip(i, k):
        return remote(y_send.at[i], y_recv.at[i], ys.at[i], yr.at[i], ranks.peer(k, 0))

    def send_step(i, carry):
        k, u, at_mine, at_other = scatter_order(ranks, halves, own, i)
        c_send[i] = tile(at_other).astype(BF16)
        to_core(i).start()
        return carry

    def sum_step(i, carry):
        k, u, at_mine, at_other = scatter_order(ranks, halves, own, i)
        grad = tile(at_mine)
        to_core(i).wait_recv()
        grad = grad + c_recv[i].astype(F32)

        @pl.when(k != 0)
        def _():
            y_send[i] = grad.astype(BF16)
            to_chip(i, k).start()

        @pl.when(k == 0)
        def _():
            sums[u] = grad

        return carry

    lax.fori_loop(0, steps, send_step, 0)
    lax.fori_loop(0, steps, sum_step, 0)
    fetch.wait()
    gain = gain_ref[...]
    gain_total = None
    for u in range(halves):
        total = sums[u]
        for k in range(1, ranks.chips):
            i = (k - 1) * halves + u
            to_chip(i, k).wait_recv()
            total = total + y_recv[i].astype(F32)
        x = rows_in[u * rows : (u + 1) * rows]
        factor = lax.rsqrt(row_mean(x * x) + EPSILON)
        hat = x * factor
        term = jnp.sum(total * hat, axis=0, keepdims=True)
        gain_total = term if gain_total is None else gain_total + term
        inner = total * gain
        grad = mg_ref[u * rows : (u + 1) * rows] + factor * (inner - hat * row_mean(inner * hat))
        rows_out[u * rows : (u + 1) * rows] = grad.astype(BF16)
    gather = GatherRows(ranks, rows_out, out_ref, g_send, g_recv, local.at[0])
    gather.start()
    total = jnp.concatenate([gain_total, gain_two_ref[...], jnp.zeros((6, gain_total.shape[1]), F32)], axis=0)
    hops = [[{"tp": ranks.peer(0, 1)}], [{"tp": ranks.peer(k, 0)} for k in range(1, ranks.chips)]]
    hops += [[{"ctx": 1 - piece}], [{"fsdp": lax.rem(me + k, shards)} for k in range(1, shards)]]
    slot, sent = 0, []
    for n, peers in enumerate(hops):
        t_send[n] = total
        copies = []
        for peer in peers:
            copies.append(
                pltpu.make_async_remote_copy(
                    src_ref=t_send.at[n], dst_ref=t_recv.at[slot], send_sem=ts.at[slot],
                    recv_sem=tr.at[slot], device_id=peer, device_id_type=MESH,
                )
            )
            copies[-1].start()
            slot += 1
        for copy, at in zip(copies, range(slot - len(copies), slot)):
            copy.wait_recv()
            total = total + t_recv[at]
        sent += copies
    gain_grad_ref[...] = total
    for copy in sent:
        copy.wait_send()
    gather.finish()
    for copy in forward:
        copy.wait()
    for s in range(shards):
        keeps[s].wait()
        swaps[s].wait_recv()
        here = slice(s * half, (s + 1) * half)
        half_ref[here, :] = (x_mine[here, :].astype(F32) + x_recv[here, :].astype(F32)).astype(BF16)
    keeps[shards].wait()
    swaps[shards].wait_recv()
    gate_out_ref[...] = gate_mine[...].astype(F32) + gate_recv[...].astype(F32)
    for copy in swaps:
        copy.wait_send()
    for i in range(steps):
        to_core(i).wait_send()
    for i in range(steps - halves):
        to_chip(i, i // halves + 1).wait_send()


def close(count, shards, dense, weight, layer_input, middle_grad, gain, gain_two, grad, gate, layers):
    tokens, model = layer_input.shape
    own = tokens // count
    rows, steps, chips = own // 2, count, count // 2
    vmem, hbm = pl.BlockSpec(memory_space=pltpu.VMEM), pl.BlockSpec(memory_space=pl.ANY)
    sem = pltpu.SemaphoreType.DMA
    return pl.pallas_call(
        functools.partial(close_kernel, count, shards),
        in_specs=[vmem, vmem, hbm, vmem, vmem, vmem, hbm, hbm] + [hbm] * chips,
        out_specs=[hbm, vmem, vmem, hbm, vmem],
        out_shape=[
            jax.ShapeDtypeStruct((tokens, model), BF16),
            jax.ShapeDtypeStruct((8, model), F32),
            jax.ShapeDtypeStruct((model // 2, grad.shape[1]), BF16),
            jax.ShapeDtypeStruct((tokens, model), BF16),
            jax.ShapeDtypeStruct(gate.shape, F32),
        ],
        scratch_shapes=[
            pltpu.VMEM((own, model), F32),
            pltpu.VMEM((own, model), BF16),
            pltpu.VMEM((2, rows, model), F32),
        ]
        + [pltpu.VMEM((steps, rows, model), BF16)] * 2
        + [pltpu.VMEM((steps - 2, rows, model), BF16)] * 2
        + [pltpu.VMEM((model // 2, grad.shape[1]), BF16)] * 2
        + [
            pltpu.VMEM(gate.shape, BF16),
            pltpu.VMEM(gate.shape, BF16),
            pltpu.VMEM((4, 8, model), F32),
            pltpu.VMEM((chips + shards, 8, model), F32),
            sem((steps,)), sem((steps,)), sem((steps - 2,)), sem((steps - 2,)),
            sem((2, chips)), sem((2, chips)), sem((shards,)), sem((shards,)), sem((shards,)),
            sem((chips,)), sem((chips,)), sem((chips,)), sem((chips + shards,)),
            sem((chips + shards,)), sem((3,)), sem((2,)),
        ],
        compiler_params=pltpu.CompilerParams(
            vmem_limit_bytes=48 << 20, collective_id=3, has_side_effects=True
        ),
        cost_estimate=pl.CostEstimate(
            flops=2 * tokens * model * dense.shape[1], bytes_accessed=200 << 20, transcendentals=0
        ),
        name="close_layer",
    )(dense, weight, layer_input, middle_grad, gain, gain_two, grad, gate, *layers)


def per_device(
    sizes,
    layer_input,
    doc_lengths,
    attention_gain,
    query_weight,
    key_matrix,
    value_matrix,
    output_weight,
    feedforward_gain,
    gate_weight,
    up_weight,
    down_weight,
    output_cotangent,
):
    shards, pieces, ranks = sizes
    assert pieces == 2 and ranks % 2 == 0
    chips = ranks // 2
    tokens, model = layer_input.shape
    own = tokens // ranks
    head_dim = HEAD_SIZE
    q_heads = query_weight.shape[1] // head_dim
    kv_heads = key_matrix.shape[1] // head_dim
    q_width, kv_width = q_heads * head_dim, kv_heads * head_dim
    piece = lax.axis_index("ctx")
    rank = lax.axis_index("tp")
    chip, core = rank // 2, rank % 2
    me = lax.axis_index("fsdp")
    scale = 1.0 / math.sqrt(head_dim)

    swap_x = [(0, 1), (1, 0)]
    swap_core = [(i, i ^ 1) for i in range(ranks)]

    def chip_shift(k):
        return [(i, (i + 2 * k) % ranks) for i in range(ranks)]

    def shard_shift(k):
        return [(i, (i + k) % shards) for i in range(shards)]

    def pick(array, index, axis=0):
        return lax.dynamic_index_in_dim(array, index, axis, keepdims=False)

    def half_of(shard):
        rows = shard.shape[0] // 2
        return lax.dynamic_slice_in_dim(shard, piece * rows, rows, 0)

    both_axes = ("fsdp", "ctx")

    def reduce_fsdp(part):
        return lax.psum_scatter(part, "fsdp", scatter_dimension=0, tiled=True)

    def add_pieces(mine):
        return mine.astype(F32) + lax.ppermute(mine, "ctx", swap_x).astype(F32)

    def whole_shard(mine):
        other = lax.ppermute(mine, "ctx", swap_x)
        pair = jnp.where(
            piece == 0, jnp.concatenate([mine, other], 0), jnp.concatenate([other, mine], 0)
        )
        return pair.astype(F32)

    cut = down_weight.shape[0] // 2
    down_columns = down_weight.T
    ff_half = half_of(jnp.concatenate([gate_weight, up_weight, down_columns[:, :cut]], axis=1))
    gain_shard = jnp.stack([attention_gain, feedforward_gain]).astype(F32)
    gain_shard = jnp.pad(gain_shard, ((0, 6), (0, 0)))
    qkv_shard = jnp.concatenate([query_weight, key_matrix, value_matrix], axis=1)
    positions = doc_positions(doc_lengths[0], piece * tokens, tokens)
    cos, sin = rotary_lanes(positions, head_dim)
    lane = np.arange(LANES)[None, :]
    half_dim = head_dim // 2
    krow = np.where((lane >= half_dim) & (lane < half_dim + 3), -1.0, 0.0).astype(np.float32)
    vrow = np.where((lane >= head_dim) & (lane < head_dim + 3), 1.0, 0.0).astype(np.float32)
    rot_q, rot_k = select_rotary(q_heads, head_dim), select_rotary(kv_heads, head_dim)
    val_q, val_k = select_value(q_heads, head_dim), select_value(kv_heads, head_dim)
    val_q_wide = np.ascontiguousarray(val_q.T)
    spread = np.zeros((q_width + 2 * kv_width, (q_heads + 2 * kv_heads) * LANES), rot_q.dtype)
    at_key, at_value = q_heads * LANES, (q_heads + kv_heads) * LANES
    spread[:q_width, :at_key] = rot_q.T
    spread[q_width : q_width + kv_width, at_key:at_value] = rot_k.T
    spread[q_width + kv_width :, at_value:] = val_k.T
    normed_one, qkv_full, out_own, ff_first, gains_full = begin(
        shards, layer_input, qkv_shard, output_weight.T, down_columns[:, cut:], gain_shard, ff_half
    )
    widen_kv = np.ascontiguousarray(spread[q_width:, at_key:])
    marks = np.concatenate([krow] * kv_heads + [vrow] * kv_heads, axis=1)
    queries, keys_values, dense_kv = project(
        normed_one, qkv_full, spread, cos, sin, krow, vrow, np.ascontiguousarray(widen_kv.T), q_heads, kv_heads
    )
    ff_half, gains_full = lax.optimization_barrier((ff_half, gains_full))
    ff_full = lax.all_gather(ff_half, both_axes, axis=0, tiled=True)
    gain_one, gain_two = gains_full[0:1], gains_full[1:2]
    before = lax.ppermute(dense_kv, "ctx", [(0, 1)])
    base = -(piece - 1) * tokens
    ends = jnp.cumsum(doc_lengths[0]).astype(jnp.int32) + base
    base = base.astype(jnp.int32).reshape(1)
    state = attention_forward(ends, base, queries, keys_values, head_dim, tokens)
    attended, marked = attention_forward(
        ends, base, queries, before, head_dim, 0, state, (widen_kv, marks, val_q)
    )
    wo = [out_own] + [lax.ppermute(out_own, "tp", chip_shift(k)) for k in range(1, chips)]
    normed_two, middle, wo_others = mix(ranks, attended, layer_input, gain_two, wo)
    (
        feed_sums, middle_grad, branch_grad, gain_two_grad, attended_grad, gate_part, feed_part,
    ) = feedforward(
        ranks, normed_two, output_cotangent, middle, gain_two, ff_full, ff_first, wo, wo_others
    )
    gate_own, feed_own = reduce_fsdp(gate_part), reduce_fsdp(feed_part)
    cut = feed_sums.reshape(chips, own, model)
    feed_sums = [lax.ppermute(cut[k - 1], "tp", chip_shift(k)) for k in range(1, chips)]
    dq_part, dkv_before = attention_backward(
        ends, base, marked, attended_grad, attended, before, val_q_wide, head_dim, 0,
        extra=(widen_kv, marks),
    )
    after = lax.ppermute(dkv_before, "ctx", [(1, 0)])
    dq, dkv = attention_backward(
        ends, base, marked, attended_grad, attended, keys_values, val_q_wide, head_dim, tokens,
        (dq_part, cos, sin, rot_q),
    )

    feed_sums, dq = lax.optimization_barrier((feed_sums, dq))
    layer_rows = middle + cut[chips - 1].astype(F32)
    for block in feed_sums:
        layer_rows = layer_rows + block.astype(F32)
    layer_rows = layer_rows.astype(BF16)

    def from_chips(rows):
        return [rows] + [lax.ppermute(rows, "tp", chip_shift(k)) for k in range(1, chips)]

    dqkv, attention_part = dense_gradients(
        dq, dkv, after, cos, sin, rot_k, val_k, attended, normed_one, from_chips(branch_grad)
    )
    input_gradient, gains, attention_half, layer_output, gate = close(
        ranks, shards, dqkv, qkv_full, layer_input, middle_grad, gain_one, gain_two_grad,
        attention_part, gate_own, from_chips(layer_rows),
    )
    attention_half, feed_own = lax.optimization_barrier((attention_half, feed_own))
    attention = whole_shard(reduce_fsdp(attention_half))
    feed = add_pieces(feed_own)
    layer_output, input_gradient = layer_output.astype(F32), input_gradient.astype(F32)
    ff_width = gate_weight.shape[1]
    gains = lax.dynamic_slice_in_dim(gains, me * gain_shard.shape[1], gain_shard.shape[1], 1)

    return (
        layer_output,
        input_gradient,
        gains[0],
        attention[:, :q_width],
        attention[:, q_width : q_width + kv_width],
        attention[:, q_width + kv_width : q_width + 2 * kv_width],
        attention[:, q_width + 2 * kv_width :].T,
        gains[1],
        gate,
        feed[:, :ff_width],
        feed[:, ff_width:].T,
    )


def solution(mesh):
    rows = P(("fsdp", "ctx"), None)
    into, out_of = P("fsdp", "tp"), P("tp", "fsdp")
    sizes = (mesh.shape["fsdp"], mesh.shape["ctx"], mesh.shape["tp"])
    return jax.shard_map(
        functools.partial(per_device, sizes),
        mesh=mesh,
        in_specs=(
            rows, P("fsdp", None), P("fsdp"), into, into, into, out_of, P("fsdp"), into, into,
            out_of, rows,
        ),
        out_specs=(
            rows, rows, P("fsdp"), into, into, into, out_of, P("fsdp"), into, into, out_of,
        ),
        check_vma=False,
    )
```

```python
import functools
import math

import jax
import jax.numpy as jnp
import ml_dtypes
import numpy as np
from jax import lax
from jax.experimental import pallas as pl
from jax.experimental.pallas import tpu as pltpu
from jax.sharding import PartitionSpec as P

HEAD_SIZE = 96
EPSILON = 1e-05
THETA = 100000.0
NEGATIVE = -1e30
LOG2E = 1.4426950408889634
LANES = 128
F32 = jnp.float32
BF16 = jnp.bfloat16
NN = (((1,), (0,)), ((), ()))
NT = (((1,), (1,)), ((), ()))
TN = (((0,), (0,)), ((), ()))


def dot(left, right, dims=NN):
    return lax.dot_general(left, right, dims, preferred_element_type=F32)


def select_rotary(heads, head_dim):
    col = np.arange(heads * head_dim)
    half = head_dim // 2
    within = col % head_dim
    lane = np.where(within < half, within, within - half + LANES // 2)
    return select_lanes(heads, (col // head_dim) * LANES + lane)


def select_value(heads, head_dim):
    col = np.arange(heads * head_dim)
    return select_lanes(heads, (col // head_dim) * LANES + col % head_dim)


def select_lanes(heads, want):
    return (np.arange(heads * LANES)[:, None] == want[None, :]).astype(ml_dtypes.bfloat16)


def rotary_lanes(positions, head_dim):
    half = head_dim // 2
    freqs = THETA ** (-(jnp.arange(half, dtype=F32) * 2.0 / head_dim))
    angles = positions.astype(F32)[:, None] * freqs[None, :]
    cos, sin = jnp.cos(angles), jnp.sin(angles)
    pad = jnp.zeros((positions.shape[0], LANES // 2 - half), F32)
    return (
        jnp.concatenate([cos, pad, cos, pad], axis=1),
        jnp.concatenate([-sin, pad, sin, pad], axis=1),
    )


def doc_positions(lengths, first, count):
    ends = jnp.cumsum(lengths)
    starts = ends - lengths
    index = first + jnp.arange(count, dtype=jnp.int32)
    document = jnp.sum((index[None, :] >= ends[:, None]).astype(jnp.int32), axis=0)
    chosen = document[None, :] == jnp.arange(lengths.shape[0], dtype=jnp.int32)[:, None]
    start_of = jnp.sum(jnp.where(chosen, starts[:, None], 0), axis=0)
    return index - start_of


def doc_start(ends_ref, base, rows):
    start = base if jnp.ndim(rows) == 0 else jnp.zeros_like(rows) + base
    for j in range(ends_ref.shape[0]):
        end = ends_ref[j]
        start = jnp.where(rows >= end, jnp.maximum(start, end), start)
    return start


def put_lanes(rows, column, lane):
    at = lax.broadcasted_iota(jnp.int32, rows.shape, 1)
    high = column.astype(BF16).astype(F32)
    rest = column - high
    mid = rest.astype(BF16).astype(F32)
    low = rest - mid
    wide = rows.astype(F32)
    wide = jnp.where(at == lane, high, wide)
    wide = jnp.where(at == lane + 1, mid, wide)
    return jnp.where(at == lane + 2, low, wide).astype(BF16)


def block_ranges(first_row, rows, block, low, last_low, key_base, key_count):
    begin = (jnp.maximum(low, key_base) - key_base) // block
    stop = jnp.minimum((first_row + rows - key_base + block - 1) // block, key_count // block)
    inner = jnp.minimum(jnp.maximum((last_low - key_base + block - 1) // block, begin), stop)
    diagonal = jnp.minimum(jnp.maximum((first_row - key_base) // block, inner), stop)
    return begin, inner, diagonal, stop


def stack_heads(ref, kv, group):
    parts = [ref[:, (kv * group + g) * LANES : (kv * group + g + 1) * LANES] for g in range(group)]
    return jnp.concatenate(parts, axis=0)


def row_marks(ends_ref, base, first_row, bq, group):
    rows = lax.broadcasted_iota(jnp.int32, (1, bq), 1) + first_row
    starts = doc_start(ends_ref, base, rows)
    return jnp.concatenate([rows] * group, axis=1), jnp.concatenate([starts] * group, axis=1)


def widen(dense_ref, spread_ref, mark_ref, wide_ref):
    @pl.when(pl.program_id(0) == 0)
    def _():
        wide = dot(dense_ref[...], spread_ref[...]) + mark_ref[...]
        wide_ref[...] = wide.astype(BF16)

    return wide_ref


def attention_forward_kernel(
    first, key_base, tokens, bq, bk, head_dim, group, ends_ref, base_ref, q_ref, kv_ref, *rest
):
    if first:
        max_ref, acc_ref = rest
    else:
        spread_ref, mark_ref, sel_ref, max_in, acc_in, o_ref, qa_ref, max_ref, acc_ref, wide = rest
        kv_ref = widen(kv_ref, spread_ref, mark_ref, wide)
    first_row = tokens + pl.program_id(0) * bq
    base = base_ref[0]
    low = doc_start(ends_ref, base, first_row)
    last_low = doc_start(ends_ref, base, first_row + bq - 1)
    rows, starts = row_marks(ends_ref, base, first_row, bq, group)
    kv_heads = kv_ref.shape[1] // LANES // 2
    unit = LOG2E / math.sqrt(head_dim)
    queries = [stack_heads(q_ref, h, group) for h in range(kv_heads)]
    if first:
        max_ref[...] = jnp.full(max_ref.shape, NEGATIVE, F32)
        acc_ref[...] = jnp.zeros(acc_ref.shape, F32)
    else:
        max_ref[...] = max_in[...]
        acc_ref[...] = acc_in[...]

    def body(masked, index, carry):
        at = pl.multiple_of(index * bk, bk)
        if masked:
            keys = lax.broadcasted_iota(jnp.int32, (bk, group * bq), 0) + (at + key_base)
            keep = (keys <= rows) & (keys >= starts)
        for h in range(kv_heads):
            key = kv_ref[pl.ds(at, bk), h * LANES : (h + 1) * LANES]
            value = kv_ref[pl.ds(at, bk), (kv_heads + h) * LANES : (kv_heads + h + 1) * LANES]
            scores = dot(key, queries[h], NT)
            if masked:
                scores = jnp.where(keep, scores, NEGATIVE)
            old = max_ref[0, h]
            new = jnp.maximum(old, jnp.max(scores, axis=0, keepdims=True))
            probs = jnp.exp2((scores - new) * unit)
            if masked:
                probs = jnp.where(keep, probs, 0.0)
            acc_ref[0, h] = acc_ref[0, h] * jnp.exp2((old - new) * unit) + dot(
                value, probs.astype(BF16), TN
            )
            max_ref[0, h] = new
        return carry

    begin, inner, diagonal, stop = block_ranges(
        first_row, bq, bk, low, last_low, key_base, kv_ref.shape[0]
    )
    lax.fori_loop(begin, inner, functools.partial(body, True), 0)
    lax.fori_loop(inner, diagonal, functools.partial(body, False), 0)
    lax.fori_loop(diagonal, stop, functools.partial(body, True), 0)
    if first:
        return
    outs = []
    for h in range(kv_heads):
        acc = acc_ref[0, h]
        total = acc[head_dim : head_dim + 1, :]
        out = jnp.transpose(acc * (1.0 / total)).astype(BF16)
        logsum = jnp.broadcast_to(max_ref[0, h] + jnp.log2(total) * (1.0 / unit), (8, group * bq))
        marked = put_lanes(queries[h], jnp.transpose(logsum)[:, :1], head_dim // 2)
        for g in range(group):
            head = h * group + g
            qa_ref[:, head * LANES : (head + 1) * LANES] = marked[g * bq : (g + 1) * bq]
            outs.append(out[g * bq : (g + 1) * bq])
    o_ref[...] = dot(jnp.concatenate(outs, axis=1), sel_ref[...]).astype(BF16)


def attention_forward(ends, base, q, kv, head_dim, key_base, state=None, extra=None):
    tokens, width = q.shape
    kv_heads = (kv if state is None else extra[0]).shape[1] // LANES // 2
    group = width // LANES // kv_heads
    bq = bk = math.gcd(tokens, 512)
    steps = tokens // bq
    whole = lambda a: pl.BlockSpec(a.shape, lambda i, *_: (0, 0))
    row = lambda w: pl.BlockSpec((bq, w), lambda i, *_: (i, 0))
    shapes = [(steps, kv_heads, 1, group * bq), (steps, kv_heads, LANES, group * bq)]
    kept = [pl.BlockSpec((1,) + a[1:], lambda i, *_: (i, 0, 0, 0)) for a in shapes]
    pairs = tokens * tokens * group * kv_heads // 2
    if state is None:
        in_specs, operands = [row(width), whole(kv)], (q, kv)
        out_specs, out_shape = kept, [jax.ShapeDtypeStruct(a, F32) for a in shapes]
        scratch = []
    else:
        select = extra[2]
        in_specs = [row(width), whole(kv)] + [whole(a) for a in extra] + kept
        operands = (q, kv) + tuple(extra) + tuple(state)
        out_specs = [row(select.shape[1]), row(width)]
        out_shape = [
            jax.ShapeDtypeStruct((tokens, select.shape[1]), BF16),
            jax.ShapeDtypeStruct(q.shape, BF16),
        ]
        scratch = [pltpu.VMEM((1,) + a[1:], F32) for a in shapes]
        scratch.append(pltpu.VMEM((tokens, extra[0].shape[1]), BF16))
    return pl.pallas_call(
        functools.partial(
            attention_forward_kernel, state is None, key_base, tokens, bq, bk, head_dim, group
        ),
        grid_spec=pltpu.PrefetchScalarGridSpec(
            num_scalar_prefetch=2, grid=(steps,), in_specs=in_specs, out_specs=out_specs,
            scratch_shapes=scratch,
        ),
        out_shape=out_shape,
        compiler_params=pltpu.CompilerParams(vmem_limit_bytes=40 << 20),
        cost_estimate=pl.CostEstimate(
            flops=pairs * 1024, bytes_accessed=8 << 20, transcendentals=pairs
        ),
        name="attention_forward",
    )(ends, base, *operands)


def attention_backward_kernel(
    first, key_base, tokens, bq, bk, head_dim, group,
    ends_ref, base_ref, qa_ref, do_ref, o_ref, kv_ref, spread_ref, *rest
):
    if first:
        widen_ref, mark_ref, dq_ref, dkv_ref, dk_acc, dv_acc, dq_acc, wide = rest
        kv_ref = widen(kv_ref, widen_ref, mark_ref, wide)
    else:
        part_ref, cos_ref, sin_ref, sel_ref, dq_ref, dkv_ref, dk_acc, dv_acc, dq_acc = rest
    step = pl.program_id(0)
    first_row = tokens + step * bq
    base = base_ref[0]
    low = doc_start(ends_ref, base, first_row)
    last_low = doc_start(ends_ref, base, first_row + bq - 1)
    kv_heads = kv_ref.shape[1] // LANES // 2
    scale = 1.0 / math.sqrt(head_dim)
    unit = LOG2E * scale
    begin, inner, diagonal, stop = block_ranges(
        first_row, bq, bk, low, last_low, key_base, kv_ref.shape[0]
    )

    @pl.when(step == 0)
    def _():
        dk_acc[...] = jnp.zeros(dk_acc.shape, F32)
        dv_acc[...] = jnp.zeros(dv_acc.shape, F32)

    if first:
        dq_acc[...] = jnp.zeros(dq_acc.shape, F32)
    else:
        for h in range(kv_heads):
            dq_acc[h] = stack_heads(part_ref, h, group)

    @pl.when(begin < stop)
    def _():
        rows, starts = row_marks(ends_ref, base, first_row, bq, group)
        grads_wide = dot(do_ref[...], spread_ref[...])
        outs_wide = dot(o_ref[...], spread_ref[...])
        queries, grads = [], []
        for h in range(kv_heads):
            queries.append(stack_heads(qa_ref, h, group))
            grad = stack_heads(grads_wide, h, group)
            inner_sum = jnp.sum(grad * stack_heads(outs_wide, h, group), axis=1, keepdims=True)
            grads.append(put_lanes(grad, -inner_sum, head_dim))

        def body(masked, index, carry):
            at = pl.multiple_of(index * bk, bk)
            if masked:
                keys = lax.broadcasted_iota(jnp.int32, (bk, group * bq), 0) + (at + key_base)
                keep = (keys <= rows) & (keys >= starts)
            for h in range(kv_heads):
                key = kv_ref[pl.ds(at, bk), h * LANES : (h + 1) * LANES]
                value = kv_ref[pl.ds(at, bk), (kv_heads + h) * LANES : (kv_heads + h + 1) * LANES]
                probs = jnp.exp2(dot(key, queries[h], NT) * unit)
                if masked:
                    probs = jnp.where(keep, probs, 0.0)
                slope = (probs * dot(value, grads[h], NT)).astype(BF16)
                dv_acc[h, pl.ds(at, bk), :] += dot(probs.astype(BF16), grads[h])
                dk_acc[h, pl.ds(at, bk), :] += dot(slope, queries[h])
                dq_acc[h] += dot(slope, key, TN)
            return carry

        lax.fori_loop(begin, inner, functools.partial(body, True), 0)
        lax.fori_loop(inner, diagonal, functools.partial(body, False), 0)
        lax.fori_loop(diagonal, stop, functools.partial(body, True), 0)

    outs = []
    for h in range(kv_heads):
        for g in range(group):
            grad = dq_acc[h, g * bq : (g + 1) * bq, :]
            if first:
                dq_ref[:, (h * group + g) * LANES : (h * group + g + 1) * LANES] = grad
            else:
                grad = grad * scale
                outs.append(
                    (grad * cos_ref[...] - pltpu.roll(grad, LANES // 2, 1) * sin_ref[...]).astype(BF16)
                )
    if not first:
        dq_ref[...] = dot(jnp.concatenate(outs, axis=1), sel_ref[...]).astype(BF16)

    @pl.when(step == pl.num_programs(0) - 1)
    def _():
        for h in range(kv_heads):
            dkv_ref[:, h * LANES : (h + 1) * LANES] = (dk_acc[h] * scale).astype(dkv_ref.dtype)
            dkv_ref[:, (kv_heads + h) * LANES : (kv_heads + h + 1) * LANES] = dv_acc[h].astype(dkv_ref.dtype)


def attention_backward(ends, base, qa, grad, out, kv, spread, head_dim, key_base, rest=None, extra=None):
    tokens, width = qa.shape
    keys = kv.shape[0]
    kv_lanes = (kv if rest is not None else extra[0]).shape[1]
    kv_heads = kv_lanes // LANES // 2
    group = width // LANES // kv_heads
    bq = bk = math.gcd(tokens, 512)
    whole = lambda a: pl.BlockSpec(a.shape, lambda i, *_: (0, 0))
    row = lambda w: pl.BlockSpec((bq, w), lambda i, *_: (i, 0))
    pairs = tokens * tokens * group * kv_heads // 2
    in_specs = [row(width), row(grad.shape[1]), row(out.shape[1]), whole(kv), whole(spread)]
    operands = (qa, grad, out, kv, spread)
    scratch = []
    if rest is None:
        in_specs += [whole(a) for a in extra]
        operands += tuple(extra)
        scratch = [pltpu.VMEM((keys, kv_lanes), BF16)]
        dq_width, dq_type, dkv_type = width, F32, BF16
    else:
        part, cos, sin, select = rest
        in_specs += [row(width), row(LANES), row(LANES), whole(select)]
        operands += (part, cos, sin, select)
        dq_width, dq_type, dkv_type = select.shape[1], BF16, F32
    return pl.pallas_call(
        functools.partial(
            attention_backward_kernel, rest is None, key_base, tokens, bq, bk, head_dim, group
        ),
        grid_spec=pltpu.PrefetchScalarGridSpec(
            num_scalar_prefetch=2,
            grid=(tokens // bq,),
            in_specs=in_specs,
            out_specs=[row(dq_width), pl.BlockSpec((keys, kv_lanes), lambda i, *_: (0, 0))],
            scratch_shapes=[
                pltpu.VMEM((kv_heads, keys, LANES), F32),
                pltpu.VMEM((kv_heads, keys, LANES), F32),
                pltpu.VMEM((kv_heads, group * bq, LANES), F32),
            ]
            + scratch,
        ),
        out_shape=[
            jax.ShapeDtypeStruct((tokens, dq_width), dq_type),
            jax.ShapeDtypeStruct((keys, kv_lanes), dkv_type),
        ],
        compiler_params=pltpu.CompilerParams(vmem_limit_bytes=48 << 20),
        cost_estimate=pl.CostEstimate(
            flops=pairs * 2560, bytes_accessed=12 << 20, transcendentals=pairs
        ),
        name="attention_backward",
    )(ends, base, qa, grad, out, kv, spread, *operands[5:])


MESH = pl.DeviceIdType.MESH


class Ranks:
    def __init__(self, count):
        self.count, self.chips = count, count // 2
        self.me = lax.axis_index("tp")
        self.chip, self.core = self.me // 2, self.me % 2

    def peer(self, k, j):
        return lax.rem(self.chip + k + self.chips, self.chips) * 2 + lax.rem(self.core + j, 2)

    def others(self):
        return [(k, j) for k in range(self.chips) for j in range(2) if k or j]

    def barrier(self):
        sem = pltpu.get_barrier_semaphore()
        for k, j in self.others():
            pl.semaphore_signal(sem, inc=1, device_id={"tp": self.peer(k, j)}, device_id_type=MESH)
        pl.semaphore_wait(sem, self.count - 1)


def remote(src, dst, send, recv, rank):
    return pltpu.make_async_remote_copy(
        src_ref=src, dst_ref=dst, send_sem=send, recv_sem=recv, device_id={"tp": rank},
        device_id_type=MESH,
    )


def row_mean(x):
    return jnp.sum(x, axis=-1, keepdims=True) * (1.0 / x.shape[-1])


class GatherRows:
    def __init__(self, ranks, rows_ref, out_ref, send, recv, local):
        own = rows_ref.shape[0]
        self.ranks, self.send, self.recv = ranks, send, recv
        self.at = lambda rank: out_ref.at[pl.ds(pl.multiple_of(rank * own, own), own)]
        self.keep = pltpu.make_async_copy(rows_ref, self.at(ranks.me), local)
        self.copies = []
        for k in list(range(1, ranks.chips)) + [0]:
            peer = ranks.peer(k, 0) if k else ranks.peer(0, 1)
            self.copies.append(remote(rows_ref, self.at(ranks.me), send.at[0, k], recv.at[0, k], peer))

    def start(self):
        for copy in self.copies:
            copy.start()
        self.keep.start()

    def finish(self):
        ranks, passed = self.ranks, []
        for k, copy in zip(range(1, ranks.chips), self.copies):
            copy.wait_recv()
            held = self.at(ranks.peer(-k, 0))
            passed.append(
                remote(held, held, self.send.at[1, k], self.recv.at[1, k], ranks.peer(0, 1))
            )
            passed[-1].start()
        self.copies[-1].wait_recv()
        for copy in self.copies:
            copy.wait_send()
        for copy in passed:
            copy.wait()
        self.keep.wait()


def both_cores(ranks, blocks, out_ref, send, recv, local):
    own = blocks[0].shape[0]
    copies = []
    for k, block in enumerate(blocks):
        there = out_ref.at[pl.ds(pl.multiple_of(ranks.peer(-k, 0) * own, own), own)]
        copies.append(remote(block, there, send.at[k], recv.at[k], ranks.peer(0, 1)))
        copies.append(pltpu.make_async_copy(block, there, local.at[k]))
    return copies


def mix_kernel(count, att_ref, x_ref, gain_ref, *rest):
    chips = count // 2
    blocks, rest = rest[:chips], rest[chips:]
    (
        n2_ref, mid_ref, other_ref, heads, rows_in, rows_out, others, a_send, a_recv, b_send, b_recv,
        g_send, g_recv, local,
    ) = rest
    ranks = Ranks(count)
    own = rows_in.shape[0]
    mine_at = pl.ds(pl.multiple_of(ranks.me * own, own), own)
    fetch = pltpu.make_async_copy(x_ref.at[mine_at], rows_in, local.at[0])
    fetch.start()
    mine = pltpu.make_async_copy(att_ref.at[mine_at], heads.at[0], local.at[1])
    mine.start()
    ranks.barrier()
    copies = {}
    for k, j in ranks.others()[::-1]:
        peer, slot = ranks.peer(k, j), 2 * k + j
        copies[slot] = remote(
            att_ref.at[pl.ds(pl.multiple_of(peer * own, own), own)], heads.at[slot],
            a_send.at[slot], a_recv.at[slot], peer,
        )
        copies[slot].start()
    swaps = [
        remote(blocks[k], others.at[k], b_send.at[k], b_recv.at[k], ranks.peer(0, 1))
        for k in range(chips)
    ]
    for copy in swaps:
        copy.start()
    fetch.wait()
    mine.wait()
    mid_ref[...] = rows_in[...] + dot(heads[0], blocks[0][...], NT)
    keeps = []
    for slot in range(1, count):
        k = slot // 2
        if slot % 2:
            swaps[k].wait_recv()
            keeps.append(pltpu.make_async_copy(others.at[k], other_ref.at[k], local.at[2 + k]))
            keeps[-1].start()
        copies[slot].wait_recv()
        mid_ref[...] += dot(heads[slot], others[k] if slot % 2 else blocks[k][...], NT)
    mid = mid_ref[...]
    factor = lax.rsqrt(row_mean(mid * mid) + EPSILON)
    rows_out[...] = (mid * factor * gain_ref[...]).astype(BF16)
    gather = GatherRows(ranks, rows_out, n2_ref, g_send, g_recv, local.at[0])
    gather.start()
    for slot in range(1, count):
        copies[slot].wait_send()
    for copy in swaps:
        copy.wait_send()
    for copy in keeps:
        copy.wait()
    gather.finish()


def mix(count, attended, layer_input, gain, blocks):
    tokens, model = layer_input.shape
    own = tokens // count
    chips = count // 2
    width = attended.shape[1]
    vmem, hbm = pl.BlockSpec(memory_space=pltpu.VMEM), pl.BlockSpec(memory_space=pl.ANY)
    sem = pltpu.SemaphoreType.DMA
    return pl.pallas_call(
        functools.partial(mix_kernel, count),
        in_specs=[hbm, hbm, vmem] + [vmem] * chips,
        out_specs=[hbm, vmem, hbm],
        out_shape=[
            jax.ShapeDtypeStruct((tokens, model), BF16),
            jax.ShapeDtypeStruct((own, model), F32),
            jax.ShapeDtypeStruct((chips, model, width), BF16),
        ],
        scratch_shapes=[
            pltpu.VMEM((count, own, width), BF16),
            pltpu.VMEM((own, model), F32),
            pltpu.VMEM((own, model), BF16),
            pltpu.VMEM((chips, model, width), BF16),
            sem((count,)), sem((count,)), sem((chips,)), sem((chips,)), sem((2, chips)),
            sem((2, chips)), sem((2 + chips,)),
        ],
        compiler_params=pltpu.CompilerParams(
            vmem_limit_bytes=40 << 20, collective_id=1, has_side_effects=True
        ),
        cost_estimate=pl.CostEstimate(
            flops=2 * tokens * model * model, bytes_accessed=150 << 20, transcendentals=0
        ),
        name="mix_heads",
    )(attended, layer_input, gain, *blocks)


def scatter_order(ranks, halves, own, i):
    k = lax.rem(i // halves + 1, ranks.chips)
    half = lax.rem(i, halves)
    rows = own // halves
    at = lambda j: pl.multiple_of(ranks.peer(k, j) * own + half * rows, rows)
    return k, half, at(0), at(1)


def half_rows(shard, which, half):
    return pl.ds(pl.multiple_of((shard * 2 + which) * half, half), half)


def swap_halves(src, dst, send, recv, shards):
    piece = lax.axis_index("ctx")
    half = src.shape[0] // (2 * shards)
    return [
        pltpu.make_async_remote_copy(
            src_ref=src.at[half_rows(s, 1 - piece, half)], dst_ref=dst.at[pl.ds(s * half, half)],
            send_sem=send.at[s], recv_sem=recv.at[s], device_id={"ctx": 1 - piece},
            device_id_type=MESH,
        )
        for s in range(shards)
    ]


def signal_piece(count):
    ranks = Ranks(count)
    sem = pltpu.get_barrier_semaphore()
    for k, j in ranks.others():
        pl.semaphore_signal(sem, inc=1, device_id={"tp": ranks.peer(k, j)}, device_id_type=MESH)
    pl.semaphore_signal(sem, inc=1, device_id={"ctx": 1 - lax.axis_index("ctx")}, device_id_type=MESH)
    pl.semaphore_wait(sem, count)


def feedforward_kernel(count, n2_ref, cot_ref, mid_ref, gain_ref, other_in, weight_ref, ff_ref, *rest):
    blocks_in, rest = rest[: count // 2], rest[count // 2 :]
    (
        ffb_ref, mg_ref, bg_ref, gain_grad_ref, da_ref, grad_ref, grads_ref,
        both_w, down_w, n2, fg, hid, gu, rows_in, ffb_out,
        c_send, c_recv, y_send, y_recv, f_send, f_recv, heads, other_ref, blocks,
        w_sem, in_sem, out_sem, cs, cr, ys, yr, fs, fr, hs, hr, local,
    ) = rest
    ranks = Ranks(count)
    own = mg_ref.shape[0]
    halves = 2
    rows = own // halves
    steps = ranks.chips * halves
    width = down_w.shape[1]
    model = n2.shape[1]
    cut = width - ff_ref.shape[1]
    loads = [
        pltpu.make_async_copy(n2_ref, n2, w_sem.at[0]),
        pltpu.make_async_copy(weight_ref.at[:, pl.ds(0, 2 * width)], both_w, w_sem.at[1]),
        pltpu.make_async_copy(
            weight_ref.at[:, pl.ds(2 * width, cut)], down_w.at[:, pl.ds(0, cut)], w_sem.at[3]
        ),
        pltpu.make_async_copy(ff_ref, down_w.at[:, pl.ds(cut, width - cut)], w_sem.at[4]),
    ]
    late = [pltpu.make_async_copy(other_in, other_ref, w_sem.at[5])] + [
        pltpu.make_async_copy(block, blocks.at[k], w_sem.at[6 + k])
        for k, block in enumerate(blocks_in)
    ]
    for load in loads + late:
        load.start()

    def read(at, slot):
        return pltpu.make_async_copy(cot_ref.at[pl.ds(at, rows)], rows_in.at[slot], in_sem.at[slot])

    def tile(at, slot, begin):
        here = pl.ds(at, rows)

        def ready(n):
            if begin is not None:
                @pl.when(begin)
                def _():
                    loads[n].wait()

        ready(0)
        ready(1)
        n = n2[here, :]
        grad = rows_in[slot].astype(BF16)
        fg[here, :] = grad
        gate = dot(n, both_w[:, :width])
        up = dot(n, both_w[:, width:])
        ready(2)
        ready(3)
        back = dot(grad, down_w[...])
        sig = 1.0 / (1.0 + jnp.exp(-gate))
        act = gate * sig
        hidden = (act * up).astype(BF16)
        hid[here, :] = hidden
        gg = (back * up * (sig * (1.0 + gate * (1.0 - sig)))).astype(BF16)
        gu[here, :width] = gg
        ug = (back * act).astype(BF16)
        gu[here, width:] = ug
        grad = dot(gg, both_w[:, :width], NT) + dot(ug, both_w[:, width:], NT)
        return grad, dot(hidden, down_w[...], NT)

    read(scatter_order(ranks, halves, own, 0)[3], 0).start()
    ranks.barrier()
    neighbour = ranks.peer(0, 1)

    def to_core(i):
        slot = lax.rem(i, 2)
        return [
            remote(c_send.at[slot], c_recv.at[slot], cs.at[slot], cr.at[slot], neighbour),
            remote(f_send.at[slot], f_recv.at[slot], fs.at[slot], fr.at[slot], neighbour),
        ]

    def to_chip(i, k):
        return remote(y_send.at[i], y_recv.at[i], ys.at[i], yr.at[i], ranks.peer(k, 0))

    def ffb_write(i):
        return pltpu.make_async_copy(ffb_out, ffb_ref.at[i], out_sem.at[0])

    def step(i, carry):
        k, u, at_mine, at_other = scatter_order(ranks, halves, own, i)
        slot = lax.rem(i, 2)
        read(at_mine, 1).start()
        read(at_other, 0).wait()
        grad, forward = tile(at_other, 0, i == 0)

        @pl.when(i + 1 < steps)
        def _():
            read(scatter_order(ranks, halves, own, i + 1)[3], 0).start()

        @pl.when(i > 1)
        def _():
            for copy in to_core(i):
                copy.wait_send()

        c_send[slot] = grad.astype(BF16)
        f_send[slot] = forward.astype(BF16)
        for copy in to_core(i):
            copy.start()
        read(at_mine, 1).wait()
        grad, forward = tile(at_mine, 1, None)

        @pl.when(i > 0)
        def _():
            ffb_write(i).wait()

        for copy in to_core(i):
            copy.wait_recv()
        grad = grad + c_recv[slot].astype(F32)
        ffb_out[...] = (forward + f_recv[slot].astype(F32)).astype(BF16)
        ffb_write(i).start()

        @pl.when(k != 0)
        def _():
            y_send[i] = grad.astype(BF16)
            to_chip(i, k).start()

        @pl.when(k == 0)
        def _():
            mg_ref[pl.ds(pl.multiple_of(u * rows, rows), rows), :] = grad

        return carry

    lax.fori_loop(0, steps, step, 0)
    mine_at = pl.multiple_of(ranks.me * own, own)
    fetch = lambda u: [
        pltpu.make_async_copy(mid_ref.at[pl.ds(u * rows, rows)], rows_in.at[0], in_sem.at[0]),
        read(mine_at + u * rows, 1),
    ]
    for copy in fetch(0):
        copy.start()
    cols = math.gcd(model, 256)
    writes = []

    def product(left, right, full):
        for d in range(model // cols):
            full[d * cols : (d + 1) * cols, :] = dot(
                left[:, d * cols : (d + 1) * cols], right, TN
            ).astype(BF16)

    def write(src, dst):
        writes.append(pltpu.make_async_copy(src, dst, out_sem.at[1 + len(writes)]))
        writes[-1].start()

    product(fg, hid[...], down_w)
    write(down_w, grads_ref.at[:, pl.ds(width, width)])
    gain = gain_ref[...]
    gain_total = None
    for u in range(halves):
        here = slice(u * rows, (u + 1) * rows)
        total = mg_ref[here, :]
        for k in range(1, ranks.chips):
            i = (k - 1) * halves + u
            to_chip(i, k).wait_recv()
            total = total + y_recv[i].astype(F32)
        for copy in fetch(u):
            copy.wait()
        mid = rows_in[0]
        factor = lax.rsqrt(row_mean(mid * mid) + EPSILON)
        hat = mid * factor
        term = jnp.sum(total * hat, axis=0, keepdims=True)
        gain_total = term if gain_total is None else gain_total + term
        inner = total * gain
        grad = rows_in[1] + factor * (inner - hat * row_mean(inner * hat))
        mg_ref[here, :] = grad
        bg_ref[here, :] = grad.astype(BF16)
        if u + 1 < halves:
            for copy in fetch(u + 1):
                copy.start()
    gain_grad_ref[...] = gain_total
    for load in late:
        load.wait()
    back = []
    for k, j in ranks.others()[::-1]:
        slot, peer = 2 * k + j, ranks.peer(-k, j)
        heads[slot] = dot(bg_ref[...], other_ref[k] if j else blocks[k]).astype(BF16)
        back.append(
            remote(heads.at[slot], da_ref.at[pl.ds(mine_at, own)], hs.at[slot], hr.at[slot], peer)
        )
        back[-1].start()
    heads[0] = dot(bg_ref[...], blocks[0]).astype(BF16)
    keep = pltpu.make_async_copy(heads.at[0], da_ref.at[pl.ds(mine_at, own)], local.at[0])
    keep.start()
    product(n2, gu[...], both_w)
    write(both_w.at[:, pl.ds(0, width)], grad_ref)
    write(both_w.at[:, pl.ds(width, width)], grads_ref.at[:, pl.ds(0, width)])
    for i in (steps - 2, steps - 1):
        for copy in to_core(i):
            copy.wait_send()
    for i in range(steps - halves):
        to_chip(i, i // halves + 1).wait_send()
    ffb_write(steps - 1).wait()
    for copy in back:
        copy.wait()
    keep.wait()
    for copy in writes:
        copy.wait()


def feedforward(count, n2, cotangent, middle, gain, weights, first, blocks, others):
    tokens, model = n2.shape
    own = tokens // count
    hidden = (weights.shape[1] + first.shape[1]) // 3
    width = blocks[0].shape[1]
    rows, steps = own // 2, count
    vmem, hbm = pl.BlockSpec(memory_space=pltpu.VMEM), pl.BlockSpec(memory_space=pl.ANY)
    sem = pltpu.SemaphoreType.DMA
    return pl.pallas_call(
        functools.partial(feedforward_kernel, count),
        in_specs=[hbm, hbm, hbm, vmem, hbm, hbm, hbm] + [hbm] * (count // 2),
        out_specs=[hbm, vmem, vmem, vmem, hbm, hbm, hbm],
        out_shape=[
            jax.ShapeDtypeStruct((steps, rows, model), BF16),
            jax.ShapeDtypeStruct((own, model), F32),
            jax.ShapeDtypeStruct((own, model), BF16),
            jax.ShapeDtypeStruct((1, model), F32),
            jax.ShapeDtypeStruct((tokens, width), BF16),
            jax.ShapeDtypeStruct((model, hidden), BF16),
            jax.ShapeDtypeStruct((model, 2 * hidden), BF16),
        ],
        scratch_shapes=[pltpu.VMEM((model, 2 * hidden), BF16), pltpu.VMEM((model, hidden), BF16)]
        + [
            pltpu.VMEM((tokens, model), BF16),
            pltpu.VMEM((tokens, model), BF16),
            pltpu.VMEM((tokens, hidden), BF16),
            pltpu.VMEM((tokens, 2 * hidden), BF16),
            pltpu.VMEM((2, rows, model), F32),
            pltpu.VMEM((rows, model), BF16),
        ]
        + [pltpu.VMEM((2, rows, model), BF16)] * 2
        + [pltpu.VMEM((steps - 2, rows, model), BF16)] * 2
        + [pltpu.VMEM((2, rows, model), BF16)] * 2
        + [
            pltpu.VMEM((count, own, width), BF16),
            pltpu.VMEM(others.shape, BF16),
            pltpu.VMEM(others.shape, BF16),
            sem((6 + count // 2,)), sem((2,)), sem((4,)),
            sem((2,)), sem((2,)), sem((steps - 2,)), sem((steps - 2,)),
            sem((2,)), sem((2,)), sem((count,)), sem((count,)), sem((1,)),
        ],
        compiler_params=pltpu.CompilerParams(
            vmem_limit_bytes=63 << 20, collective_id=2, has_side_effects=True
        ),
        cost_estimate=pl.CostEstimate(
            flops=2 * tokens * model * hidden * 9, bytes_accessed=280 << 20,
            transcendentals=tokens * hidden,
        ),
        name="feed_forward",
    )(n2, cotangent, middle, gain, others, weights, first, *blocks)


def shard_copy(src, dst, send, recv, axis, index):
    return pltpu.make_async_remote_copy(
        src_ref=src, dst_ref=dst, send_sem=send, recv_sem=recv, device_id={axis: index},
        device_id_type=MESH,
    )


def begin_kernel(
    shards, x_ref, qkv_ref, wo_ref, ff_ref, gains_ref, order_ref, n_ref, qkv_full_ref, wo_full_ref,
    ff_full_ref, gain_out_ref, qkv_full, wo_full, ff_full, normed, rows_in, gain_buf, zs, zr, xs, xr, gs, gr, own_sem, in_sem, out_sem,
):
    del order_ref
    me, piece = lax.axis_index("fsdp"), lax.axis_index("ctx")
    fulls, sources = (qkv_full, wo_full, ff_full), (qkv_ref, wo_ref, ff_ref)
    arrays = range(len(fulls))
    shard = qkv_ref.shape[0]
    half = shard // 2
    tokens = normed.shape[0]
    rows = rows_in.shape[1]
    steps = tokens // rows

    def read(i):
        return pltpu.make_async_copy(
            x_ref.at[pl.ds(i * rows, rows)], rows_in.at[i % 2], in_sem.at[i % 2]
        )

    read(0).start()
    keeps = [
        pltpu.make_async_copy(src, full.at[pl.ds(pl.multiple_of(me * shard, shard), shard)], own_sem.at[a])
        for a, (src, full) in enumerate(zip(sources, fulls))
    ]
    for copy in keeps:
        copy.start()
    keep_gain = pltpu.make_async_copy(gains_ref, gain_buf.at[me], own_sem.at[3])
    keep_gain.start()
    barrier = pltpu.get_barrier_semaphore()
    for k in range(1, shards):
        pl.semaphore_signal(
            barrier, inc=1, device_id={"fsdp": lax.rem(me + k, shards)}, device_id_type=MESH
        )
    pl.semaphore_signal(barrier, inc=1, device_id={"ctx": 1 - piece}, device_id_type=MESH)
    pl.semaphore_wait(barrier, shards)

    def place(a, s, which):
        return fulls[a].at[half_rows(s, which, half)]

    def own_half(a):
        return sources[a].at[pl.ds(pl.multiple_of(piece * half, half), half)]

    def along(a, s, step, mine):
        way = 0 if step > 0 else 1
        src = own_half(a) if mine else place(a, s, piece)
        return shard_copy(
            src, place(a, s, piece), zs.at[a, way, s], zr.at[a, s], "fsdp",
            lax.rem(me + step + shards, shards),
        )

    def across(a, s):
        return shard_copy(
            place(a, s, piece), place(a, s, piece), xs.at[a, s], xr.at[a, s], "ctx", 1 - piece
        )

    gain_copies = [
        shard_copy(
            gains_ref, gain_buf.at[me], gs.at[k], gr.at[k], "fsdp", lax.rem(me + k, shards)
        )
        for k in range(1, shards)
    ]
    for copy in gain_copies:
        copy.start()
    for a in arrays:
        for step, there in ((1, me < shards - 1), (-1, me > 0)):
            @pl.when(there)
            def _():
                along(a, me, step, True).start()

    for copy in gain_copies:
        copy.wait()
    keep_gain.wait()
    gain_out_ref[...] = jnp.concatenate([gain_buf[s] for s in range(shards)], axis=1)
    for i in range(steps):
        if i + 1 < steps:
            read(i + 1).start()
        read(i).wait()
        x = rows_in[i % 2]
        factor = lax.rsqrt(row_mean(x * x) + EPSILON)
        normed[i * rows : (i + 1) * rows, :] = (x * factor * gain_out_ref[0:1, :]).astype(BF16)
    write_normed = pltpu.make_async_copy(normed, n_ref, out_sem.at[0])
    write_normed.start()

    def arrival(d, step):
        s = me - step * d
        there = (s >= 0) & (s <= shards - 1)
        s = jnp.minimum(jnp.maximum(s, 0), shards - 1)
        onward = (me < shards - 1) if step > 0 else (me > 0)

        @pl.when(there)
        def _():
            for a in arrays:
                along(a, s, step, False).wait_recv()
                across(a, s).start()

        @pl.when(there & onward)
        def _():
            for a in arrays:
                along(a, s, step, False).start()

    for d in range(1, shards):
        arrival(d, 1)
        arrival(d, -1)
    for copy in keeps:
        copy.wait()
    for k in range(1, shards):
        s = lax.rem(me + k, shards)
        for a in arrays:
            across(a, s).wait_recv()
    writes = [
        pltpu.make_async_copy(qkv_full, qkv_full_ref, out_sem.at[1]),
        pltpu.make_async_copy(wo_full, wo_full_ref, out_sem.at[2]),
        pltpu.make_async_copy(ff_full, ff_full_ref, out_sem.at[3]),
    ]
    for copy in writes:
        copy.start()
    for a in arrays:
        for s in range(shards):
            @pl.when((me >= s) & (me < shards - 1))
            def _():
                along(a, s, 1, False).wait_send()

            @pl.when((me <= s) & (me > 0))
            def _():
                along(a, s, -1, False).wait_send()

        for k in range(1, shards):
            across(a, lax.rem(me + k, shards)).wait_send()
    write_normed.wait()
    for copy in writes:
        copy.wait()


def begin(shards, x, qkv, wo, ff, gains, order):
    tokens, model = x.shape
    rows = math.gcd(tokens, 256)
    vmem, hbm = pl.BlockSpec(memory_space=pltpu.VMEM), pl.BlockSpec(memory_space=pl.ANY)
    sem = pltpu.SemaphoreType.DMA
    return pl.pallas_call(
        functools.partial(begin_kernel, shards),
        in_specs=[hbm, vmem, vmem, vmem, vmem, hbm],
        out_specs=[hbm, hbm, hbm, hbm, vmem],
        out_shape=[
            jax.ShapeDtypeStruct((tokens, model), BF16),
            jax.ShapeDtypeStruct((model, qkv.shape[1]), BF16),
            jax.ShapeDtypeStruct((model, wo.shape[1]), BF16),
            jax.ShapeDtypeStruct((model, ff.shape[1]), BF16),
            jax.ShapeDtypeStruct((gains.shape[0], model), F32),
        ],
        scratch_shapes=[
            pltpu.VMEM((model, qkv.shape[1]), BF16),
            pltpu.VMEM((model, wo.shape[1]), BF16),
            pltpu.VMEM((model, ff.shape[1]), BF16),
            pltpu.VMEM((tokens, model), BF16),
            pltpu.VMEM((2, rows, model), F32),
            pltpu.VMEM((shards,) + gains.shape, F32),
            sem((3, 2, shards)), sem((3, shards)), sem((3, shards)), sem((3, shards)),
            sem((shards,)), sem((shards,)), sem((4,)), sem((2,)), sem((4,)),
        ],
        compiler_params=pltpu.CompilerParams(
            vmem_limit_bytes=48 << 20, collective_id=4, has_side_effects=True
        ),
        cost_estimate=pl.CostEstimate(flops=0, bytes_accessed=120 << 20, transcendentals=0),
        name="norm_and_gather",
    )(x, qkv, wo, ff, gains, order)


def project_kernel(
    q_heads, n_ref, qkv_ref, spread_ref, cos_ref, sin_ref, krow_ref, vrow_ref, pick_ref, q_ref, kv_ref,
    dense_ref, wide
):
    @pl.when(pl.program_id(0) == 0)
    def _():
        model = qkv_ref.shape[0]
        block = math.gcd(model, 512)
        for r in range(0, model, block):
            wide[r : r + block, :] = dot(qkv_ref[r : r + block, :], spread_ref[...]).astype(BF16)

    kv_heads = kv_ref.shape[1] // LANES // 2
    cos, sin = cos_ref[...], sin_ref[...]
    out = dot(n_ref[...], wide[...])
    plain = []
    for h in range(q_heads + 2 * kv_heads):
        part = out[:, h * LANES : (h + 1) * LANES]
        if h < q_heads + kv_heads:
            part = part * cos + pltpu.roll(part, LANES // 2, 1) * sin
        if h < q_heads:
            q_ref[:, h * LANES : (h + 1) * LANES] = part.astype(BF16)
        else:
            plain.append(part.astype(BF16))
            part = part + (krow_ref[...] if h < q_heads + kv_heads else vrow_ref[...])
            kv_ref[:, (h - q_heads) * LANES : (h - q_heads + 1) * LANES] = part.astype(BF16)
    dense_ref[...] = dot(jnp.concatenate(plain, axis=1), pick_ref[...]).astype(BF16)


def project(normed, qkv, spread, cos, sin, krow, vrow, pick, q_heads, kv_heads):
    tokens, model = normed.shape
    wide = spread.shape[1]
    bm = math.gcd(tokens, 256)
    whole = lambda a: pl.BlockSpec(a.shape, lambda i: (0, 0))
    row = lambda w: pl.BlockSpec((bm, w), lambda i: (i, 0))
    return pl.pallas_call(
        functools.partial(project_kernel, q_heads),
        grid=(tokens // bm,),
        in_specs=[row(model), whole(qkv), whole(spread), row(LANES), row(LANES), whole(krow), whole(vrow),
            whole(pick)],
        out_specs=[row(q_heads * LANES), row(2 * kv_heads * LANES), row(pick.shape[1])],
        out_shape=[
            jax.ShapeDtypeStruct((tokens, q_heads * LANES), BF16),
            jax.ShapeDtypeStruct((tokens, 2 * kv_heads * LANES), BF16),
            jax.ShapeDtypeStruct((tokens, pick.shape[1]), BF16),
        ],
        scratch_shapes=[pltpu.VMEM((model, wide), BF16)],
        compiler_params=pltpu.CompilerParams(vmem_limit_bytes=40 << 20),
        cost_estimate=pl.CostEstimate(
            flops=2 * tokens * model * wide, bytes_accessed=16 << 20, transcendentals=0
        ),
        name="project_qkv",
    )(normed, qkv, spread, cos, sin, krow, vrow, pick)


def dense_kernel(
    chips, dq_ref, dkv_ref, after_ref, cos_ref, sin_ref, rotk_ref, valk_ref, att_ref, n_ref, *rest
):
    blocks, rest = rest[:chips], rest[chips:]
    dense_ref, grad_ref, normed, branch, send, recv, local = rest
    ranks = Ranks(2 * chips)
    fetch = pltpu.make_async_copy(n_ref, normed, local.at[chips])
    fetch.start()
    sem = pltpu.get_barrier_semaphore()
    pl.semaphore_signal(sem, inc=1, device_id={"tp": ranks.peer(0, 1)}, device_id_type=MESH)
    pl.semaphore_wait(sem, 1)
    copies = both_cores(ranks, blocks, branch, send, recv, local)
    for copy in copies:
        copy.start()
    width = dense_ref.shape[1]
    lanes = dkv_ref.shape[1] // 2
    cos, sin = cos_ref[...], sin_ref[...]
    turned = []
    for h in range(lanes // LANES):
        at = slice(h * LANES, (h + 1) * LANES)
        key = dkv_ref[:, at] + after_ref[:, at].astype(F32)
        turned.append((key * cos - pltpu.roll(key, LANES // 2, 1) * sin).astype(BF16))
    dk = dot(jnp.concatenate(turned, axis=1), rotk_ref[...]).astype(BF16)
    dv = (dkv_ref[:, lanes:] + after_ref[:, lanes:].astype(F32)).astype(BF16)
    dv = dot(dv, valk_ref[...]).astype(BF16)
    dense_ref[...] = jnp.concatenate([dq_ref[...], dk, dv], axis=1)
    fetch.wait()
    model = normed.shape[1]
    cols = math.gcd(model, 384)
    for d in range(0, model, cols):
        grad_ref[d : d + cols, :width] = dot(
            normed[:, d : d + cols], dense_ref[...], TN
        ).astype(BF16)
    for copy in copies:
        copy.wait()
    for d in range(0, model, cols):
        grad_ref[d : d + cols, width:] = dot(branch[:, d : d + cols], att_ref[...], TN).astype(BF16)


def dense_gradients(dq, dkv, after, cos, sin, rot_k, val_k, attended, normed, blocks):
    tokens, model = normed.shape
    chips = len(blocks)
    width = dq.shape[1] + 2 * rot_k.shape[1]
    total = width + attended.shape[1]
    vmem, hbm = pl.BlockSpec(memory_space=pltpu.VMEM), pl.BlockSpec(memory_space=pl.ANY)
    sem = pltpu.SemaphoreType.DMA
    return pl.pallas_call(
        functools.partial(dense_kernel, chips),
        in_specs=[vmem] * 8 + [hbm] * (1 + chips),
        out_specs=[vmem, vmem],
        out_shape=[
            jax.ShapeDtypeStruct((tokens, width), BF16),
            jax.ShapeDtypeStruct((model, total), BF16),
        ],
        scratch_shapes=[
            pltpu.VMEM((tokens, model), BF16),
            pltpu.VMEM((tokens, model), BF16),
            sem((chips,)), sem((chips,)), sem((chips + 1,)),
        ],
        compiler_params=pltpu.CompilerParams(
            vmem_limit_bytes=48 << 20, collective_id=5, has_side_effects=True
        ),
        cost_estimate=pl.CostEstimate(
            flops=2 * tokens * model * total, bytes_accessed=24 << 20, transcendentals=0
        ),
        name="dense_gradients",
    )(dq, dkv, after, cos, sin, rot_k, val_k, attended, normed, *blocks)


def close_kernel(
    count, shards, dense_ref, w_ref, x_ref, mg_ref, gain_ref, gain_two_ref, grad_ref, gate_ref, *rest
):
    layers, rest = rest[: count // 2], rest[count // 2 :]
    (
        out_ref, gain_grad_ref, half_ref, lay_ref, gate_out_ref, rows_in, rows_out, sums, c_send, c_recv, y_send,
        y_recv, x_mine, x_recv, gate_mine, gate_recv, t_send, t_recv, cs, cr, ys, yr, g_send, g_recv, xs, xr, x_sem,
        ls, lr, lay_sem, ts, tr, gate_sem, local,
    ) = rest
    ranks = Ranks(count)
    own = rows_in.shape[0]
    halves = 2
    rows = own // halves
    steps = ranks.chips * halves
    fetch = pltpu.make_async_copy(
        x_ref.at[pl.ds(pl.multiple_of(ranks.me * own, own), own)], rows_in, local.at[0]
    )
    fetch.start()
    def tile(at):
        return dot(dense_ref[pl.ds(at, rows), :], w_ref[...], NT)

    piece = lax.axis_index("ctx")
    half = grad_ref.shape[0] // (2 * shards)
    keeps = [
        pltpu.make_async_copy(
            grad_ref.at[half_rows(s, piece, half)], x_mine.at[pl.ds(s * half, half)], x_sem.at[s]
        )
        for s in range(shards)
    ]
    keeps.append(pltpu.make_async_copy(gate_ref, gate_mine, gate_sem.at[0]))
    for copy in keeps:
        copy.start()
    me = lax.axis_index("fsdp")
    barrier = pltpu.get_barrier_semaphore()
    for k, j in ranks.others():
        pl.semaphore_signal(barrier, inc=1, device_id={"tp": ranks.peer(k, j)}, device_id_type=MESH)
    for k in range(1, shards):
        pl.semaphore_signal(
            barrier, inc=1, device_id={"fsdp": lax.rem(me + k, shards)}, device_id_type=MESH
        )
    pl.semaphore_signal(barrier, inc=1, device_id={"ctx": 1 - piece}, device_id_type=MESH)
    pl.semaphore_wait(barrier, count + shards - 1)
    swaps = swap_halves(grad_ref, x_recv, xs, xr, shards)
    swaps.append(
        pltpu.make_async_remote_copy(
            src_ref=gate_ref, dst_ref=gate_recv, send_sem=gate_sem.at[1], recv_sem=gate_sem.at[2],
            device_id={"ctx": 1 - piece}, device_id_type=MESH,
        )
    )
    for copy in swaps:
        copy.start()
    forward = both_cores(ranks, layers, lay_ref, ls, lr, lay_sem)
    for copy in forward:
        copy.start()
    neighbour = ranks.peer(0, 1)

    def to_core(i):
        return remote(c_send.at[i], c_recv.at[i], cs.at[i], cr.at[i], neighbour)

    def to_chip(i, k):
        return remote(y_send.at[i], y_recv.at[i], ys.at[i], yr.at[i], ranks.peer(k, 0))

    def send_step(i, carry):
        k, u, at_mine, at_other = scatter_order(ranks, halves, own, i)
        c_send[i] = tile(at_other).astype(BF16)
        to_core(i).start()
        return carry

    def sum_step(i, carry):
        k, u, at_mine, at_other = scatter_order(ranks, halves, own, i)
        grad = tile(at_mine)
        to_core(i).wait_recv()
        grad = grad + c_recv[i].astype(F32)

        @pl.when(k != 0)
        def _():
            y_send[i] = grad.astype(BF16)
            to_chip(i, k).start()

        @pl.when(k == 0)
        def _():
            sums[u] = grad

        return carry

    lax.fori_loop(0, steps, send_step, 0)
    lax.fori_loop(0, steps, sum_step, 0)
    fetch.wait()
    gain = gain_ref[...]
    gain_total = None
    for u in range(halves):
        total = sums[u]
        for k in range(1, ranks.chips):
            i = (k - 1) * halves + u
            to_chip(i, k).wait_recv()
            total = total + y_recv[i].astype(F32)
        x = rows_in[u * rows : (u + 1) * rows]
        factor = lax.rsqrt(row_mean(x * x) + EPSILON)
        hat = x * factor
        term = jnp.sum(total * hat, axis=0, keepdims=True)
        gain_total = term if gain_total is None else gain_total + term
        inner = total * gain
        grad = mg_ref[u * rows : (u + 1) * rows] + factor * (inner - hat * row_mean(inner * hat))
        rows_out[u * rows : (u + 1) * rows] = grad.astype(BF16)
    gather = GatherRows(ranks, rows_out, out_ref, g_send, g_recv, local.at[0])
    gather.start()
    total = jnp.concatenate([gain_total, gain_two_ref[...], jnp.zeros((6, gain_total.shape[1]), F32)], axis=0)
    hops = [[{"tp": ranks.peer(0, 1)}], [{"tp": ranks.peer(k, 0)} for k in range(1, ranks.chips)]]
    hops += [[{"ctx": 1 - piece}], [{"fsdp": lax.rem(me + k, shards)} for k in range(1, shards)]]
    slot, sent = 0, []
    for n, peers in enumerate(hops):
        t_send[n] = total
        copies = []
        for peer in peers:
            copies.append(
                pltpu.make_async_remote_copy(
                    src_ref=t_send.at[n], dst_ref=t_recv.at[slot], send_sem=ts.at[slot],
                    recv_sem=tr.at[slot], device_id=peer, device_id_type=MESH,
                )
            )
            copies[-1].start()
            slot += 1
        for copy, at in zip(copies, range(slot - len(copies), slot)):
            copy.wait_recv()
            total = total + t_recv[at]
        sent += copies
    gain_grad_ref[...] = total
    for copy in sent:
        copy.wait_send()
    gather.finish()
    for copy in forward:
        copy.wait()
    for s in range(shards):
        keeps[s].wait()
        swaps[s].wait_recv()
        here = slice(s * half, (s + 1) * half)
        half_ref[here, :] = (x_mine[here, :].astype(F32) + x_recv[here, :].astype(F32)).astype(BF16)
    keeps[shards].wait()
    swaps[shards].wait_recv()
    gate_out_ref[...] = gate_mine[...].astype(F32) + gate_recv[...].astype(F32)
    for copy in swaps:
        copy.wait_send()
    for i in range(steps):
        to_core(i).wait_send()
    for i in range(steps - halves):
        to_chip(i, i // halves + 1).wait_send()


def close(count, shards, dense, weight, layer_input, middle_grad, gain, gain_two, grad, gate, layers):
    tokens, model = layer_input.shape
    own = tokens // count
    rows, steps, chips = own // 2, count, count // 2
    vmem, hbm = pl.BlockSpec(memory_space=pltpu.VMEM), pl.BlockSpec(memory_space=pl.ANY)
    sem = pltpu.SemaphoreType.DMA
    return pl.pallas_call(
        functools.partial(close_kernel, count, shards),
        in_specs=[vmem, vmem, hbm, vmem, vmem, vmem, hbm, hbm] + [hbm] * chips,
        out_specs=[hbm, vmem, vmem, hbm, vmem],
        out_shape=[
            jax.ShapeDtypeStruct((tokens, model), BF16),
            jax.ShapeDtypeStruct((8, model), F32),
            jax.ShapeDtypeStruct((model // 2, grad.shape[1]), BF16),
            jax.ShapeDtypeStruct((tokens, model), BF16),
            jax.ShapeDtypeStruct(gate.shape, F32),
        ],
        scratch_shapes=[
            pltpu.VMEM((own, model), F32),
            pltpu.VMEM((own, model), BF16),
            pltpu.VMEM((2, rows, model), F32),
        ]
        + [pltpu.VMEM((steps, rows, model), BF16)] * 2
        + [pltpu.VMEM((steps - 2, rows, model), BF16)] * 2
        + [pltpu.VMEM((model // 2, grad.shape[1]), BF16)] * 2
        + [
            pltpu.VMEM(gate.shape, BF16),
            pltpu.VMEM(gate.shape, BF16),
            pltpu.VMEM((4, 8, model), F32),
            pltpu.VMEM((chips + shards, 8, model), F32),
            sem((steps,)), sem((steps,)), sem((steps - 2,)), sem((steps - 2,)),
            sem((2, chips)), sem((2, chips)), sem((shards,)), sem((shards,)), sem((shards,)),
            sem((chips,)), sem((chips,)), sem((chips,)), sem((chips + shards,)),
            sem((chips + shards,)), sem((3,)), sem((2,)),
        ],
        compiler_params=pltpu.CompilerParams(
            vmem_limit_bytes=48 << 20, collective_id=3, has_side_effects=True
        ),
        cost_estimate=pl.CostEstimate(
            flops=2 * tokens * model * dense.shape[1], bytes_accessed=200 << 20, transcendentals=0
        ),
        name="close_layer",
    )(dense, weight, layer_input, middle_grad, gain, gain_two, grad, gate, *layers)


def per_device(
    sizes,
    layer_input,
    doc_lengths,
    attention_gain,
    query_weight,
    key_matrix,
    value_matrix,
    output_weight,
    feedforward_gain,
    gate_weight,
    up_weight,
    down_weight,
    output_cotangent,
):
    shards, pieces, ranks = sizes
    assert pieces == 2 and ranks % 2 == 0
    chips = ranks // 2
    tokens, model = layer_input.shape
    own = tokens // ranks
    head_dim = HEAD_SIZE
    q_heads = query_weight.shape[1] // head_dim
    kv_heads = key_matrix.shape[1] // head_dim
    q_width, kv_width = q_heads * head_dim, kv_heads * head_dim
    piece = lax.axis_index("ctx")
    rank = lax.axis_index("tp")
    chip, core = rank // 2, rank % 2
    me = lax.axis_index("fsdp")
    scale = 1.0 / math.sqrt(head_dim)

    swap_x = [(0, 1), (1, 0)]
    swap_core = [(i, i ^ 1) for i in range(ranks)]

    def chip_shift(k):
        return [(i, (i + 2 * k) % ranks) for i in range(ranks)]

    def shard_shift(k):
        return [(i, (i + k) % shards) for i in range(shards)]

    def pick(array, index, axis=0):
        return lax.dynamic_index_in_dim(array, index, axis, keepdims=False)

    def half_of(shard):
        rows = shard.shape[0] // 2
        return lax.dynamic_slice_in_dim(shard, piece * rows, rows, 0)

    both_axes = ("fsdp", "ctx")

    def reduce_fsdp(part):
        return lax.psum_scatter(part, "fsdp", scatter_dimension=0, tiled=True)

    def add_pieces(mine):
        return mine.astype(F32) + lax.ppermute(mine, "ctx", swap_x).astype(F32)

    def whole_shard(mine):
        other = lax.ppermute(mine, "ctx", swap_x)
        pair = jnp.where(
            piece == 0, jnp.concatenate([mine, other], 0), jnp.concatenate([other, mine], 0)
        )
        return pair.astype(F32)

    cut = down_weight.shape[0] // 2
    down_columns = down_weight.T
    ff_half = half_of(jnp.concatenate([gate_weight, up_weight, down_columns[:, :cut]], axis=1))
    gain_shard = jnp.stack([attention_gain, feedforward_gain]).astype(F32)
    gain_shard = jnp.pad(gain_shard, ((0, 6), (0, 0)))
    qkv_shard = jnp.concatenate([query_weight, key_matrix, value_matrix], axis=1)
    positions = doc_positions(doc_lengths[0], piece * tokens, tokens)
    cos, sin = rotary_lanes(positions, head_dim)
    lane = np.arange(LANES)[None, :]
    half_dim = head_dim // 2
    krow = np.where((lane >= half_dim) & (lane < half_dim + 3), -1.0, 0.0).astype(np.float32)
    vrow = np.where((lane >= head_dim) & (lane < head_dim + 3), 1.0, 0.0).astype(np.float32)
    rot_q, rot_k = select_rotary(q_heads, head_dim), select_rotary(kv_heads, head_dim)
    val_q, val_k = select_value(q_heads, head_dim), select_value(kv_heads, head_dim)
    val_q_wide = np.ascontiguousarray(val_q.T)
    spread = np.zeros((q_width + 2 * kv_width, (q_heads + 2 * kv_heads) * LANES), rot_q.dtype)
    at_key, at_value = q_heads * LANES, (q_heads + kv_heads) * LANES
    spread[:q_width, :at_key] = rot_q.T
    spread[q_width : q_width + kv_width, at_key:at_value] = rot_k.T
    spread[q_width + kv_width :, at_value:] = val_k.T
    normed_one, qkv_full, out_own, ff_first, gains_full = begin(
        shards, layer_input, qkv_shard, output_weight.T, down_columns[:, cut:], gain_shard, ff_half
    )
    widen_kv = np.ascontiguousarray(spread[q_width:, at_key:])
    marks = np.concatenate([krow] * kv_heads + [vrow] * kv_heads, axis=1)
    queries, keys_values, dense_kv = project(
        normed_one, qkv_full, spread, cos, sin, krow, vrow, np.ascontiguousarray(widen_kv.T), q_heads, kv_heads
    )
    ff_half, gains_full = lax.optimization_barrier((ff_half, gains_full))
    ff_full = lax.all_gather(ff_half, both_axes, axis=0, tiled=True)
    gain_one, gain_two = gains_full[0:1], gains_full[1:2]
    before = lax.ppermute(dense_kv, "ctx", [(0, 1)])
    base = -(piece - 1) * tokens
    ends = jnp.cumsum(doc_lengths[0]).astype(jnp.int32) + base
    base = base.astype(jnp.int32).reshape(1)
    state = attention_forward(ends, base, queries, keys_values, head_dim, tokens)
    attended, marked = attention_forward(
        ends, base, queries, before, head_dim, 0, state, (widen_kv, marks, val_q)
    )
    wo = [out_own] + [lax.ppermute(out_own, "tp", chip_shift(k)) for k in range(1, chips)]
    normed_two, middle, wo_others = mix(ranks, attended, layer_input, gain_two, wo)
    (
        feed_sums, middle_grad, branch_grad, gain_two_grad, attended_grad, gate_part, feed_part,
    ) = feedforward(
        ranks, normed_two, output_cotangent, middle, gain_two, ff_full, ff_first, wo, wo_others
    )
    gate_own, feed_own = reduce_fsdp(gate_part), reduce_fsdp(feed_part)
    cut = feed_sums.reshape(chips, own, model)
    feed_sums = [lax.ppermute(cut[k - 1], "tp", chip_shift(k)) for k in range(1, chips)]
    dq_part, dkv_before = attention_backward(
        ends, base, marked, attended_grad, attended, before, val_q_wide, head_dim, 0,
        extra=(widen_kv, marks),
    )
    after = lax.ppermute(dkv_before, "ctx", [(1, 0)])
    dq, dkv = attention_backward(
        ends, base, marked, attended_grad, attended, keys_values, val_q_wide, head_dim, tokens,
        (dq_part, cos, sin, rot_q),
    )

    feed_sums, dq = lax.optimization_barrier((feed_sums, dq))
    layer_rows = middle + cut[chips - 1].astype(F32)
    for block in feed_sums:
        layer_rows = layer_rows + block.astype(F32)
    layer_rows = layer_rows.astype(BF16)

    def from_chips(rows):
        return [rows] + [lax.ppermute(rows, "tp", chip_shift(k)) for k in range(1, chips)]

    dqkv, attention_part = dense_gradients(
        dq, dkv, after, cos, sin, rot_k, val_k, attended, normed_one, from_chips(branch_grad)
    )
    input_gradient, gains, attention_half, layer_output, gate = close(
        ranks, shards, dqkv, qkv_full, layer_input, middle_grad, gain_one, gain_two_grad,
        attention_part, gate_own, from_chips(layer_rows),
    )
    attention_half, feed_own = lax.optimization_barrier((attention_half, feed_own))
    attention = whole_shard(reduce_fsdp(attention_half))
    feed = add_pieces(feed_own)
    layer_output, input_gradient = layer_output.astype(F32), input_gradient.astype(F32)
    ff_width = gate_weight.shape[1]
    gains = lax.dynamic_slice_in_dim(gains, me * gain_shard.shape[1], gain_shard.shape[1], 1)

    return (
        layer_output,
        input_gradient,
        gains[0],
        attention[:, :q_width],
        attention[:, q_width : q_width + kv_width],
        attention[:, q_width + kv_width : q_width + 2 * kv_width],
        attention[:, q_width + 2 * kv_width :].T,
        gains[1],
        gate,
        feed[:, :ff_width],
        feed[:, ff_width:].T,
    )


def solution(mesh):
    rows = P(("fsdp", "ctx"), None)
    into, out_of = P("fsdp", "tp"), P("tp", "fsdp")
    sizes = (mesh.shape["fsdp"], mesh.shape["ctx"], mesh.shape["tp"])
    return jax.shard_map(
        functools.partial(per_device, sizes),
        mesh=mesh,
        in_specs=(
            rows, P("fsdp", None), P("fsdp"), into, into, into, out_of, P("fsdp"), into, into,
            out_of, rows,
        ),
        out_specs=(
            rows, rows, P("fsdp"), into, into, into, out_of, P("fsdp"), into, into, out_of,
        ),
        check_vma=False,
    )
```
